128 devices in a mesh: row: 16 (over y_hi, x, core), col: 8 (over z, y_lo).
Axes of the slice: x: 4, y: 4 (y_hi: 2, y_lo: 2; y = y_hi * 2 + y_lo), z: 4, core: 2. Of those that a mesh axis runs over, the one named last changes fastest.
Arguments:
- pair_in: bfloat16 [2, 512, 512, 128], P(None, 'row', 'col'), may hold values from -6 to 6
- lengths: int32 [2], replicated, may hold values from 256 to 512, as said below
- pair_cotangent: bfloat16 [2, 512, 512, 128], P(None, 'row', 'col'), may hold values from -6 to 6
- triangle_weights: float32 [2, 6, 128, 128], replicated, may hold values from -0.5 to 0.5
- expand_weights: float32 [2, 2, 128, 512], replicated, may hold values from -0.5 to 0.5
- shrink_weights: float32 [2, 512, 128], replicated, may hold values from -0.25 to 0.25
- norm_params: float32 [2, 6, 128], replicated, may hold values from -2 to 2, as said below
- triangle_first: float32 [2, 6, 128, 128], replicated, may hold values from -0.001953125 to 0.001953125
- triangle_second: float32 [2, 6, 128, 128], replicated, may hold values from 8.477105e-10 to 6.781684e-09
- expand_first: float32 [2, 2, 128, 512], replicated, may hold values from -0.001953125 to 0.001953125
- expand_second: float32 [2, 2, 128, 512], replicated, may hold values from 8.477105e-10 to 6.781684e-09
- shrink_first: float32 [2, 512, 128], replicated, may hold values from -0.001953125 to 0.001953125
- shrink_second: float32 [2, 512, 128], replicated, may hold values from 8.477105e-10 to 6.781684e-09
- norm_first: float32 [2, 6, 128], replicated, may hold values from -0.0078125 to 0.0078125
- norm_second: float32 [2, 6, 128], replicated, may hold values from 1.3563368e-08 to 1.08506946e-07
Outputs:
- pair_out: bfloat16 [2, 512, 512, 128], P(None, 'row', 'col')
- pair_grad: float32 [2, 512, 512, 128], P(None, 'row', 'col')
- triangle_moment: float32 [2, 6, 128, 128], replicated
- triangle_square: float32 [2, 6, 128, 128], replicated
- triangle_master: float32 [2, 6, 128, 128], replicated
- expand_moment: float32 [2, 2, 128, 512], replicated
- expand_square: float32 [2, 2, 128, 512], replicated
- expand_master: float32 [2, 2, 128, 512], replicated
- shrink_moment: float32 [2, 512, 128], replicated
- shrink_square: float32 [2, 512, 128], replicated
- shrink_master: float32 [2, 512, 128], replicated
- norm_moment: float32 [2, 6, 128], replicated
- norm_square: float32 [2, 6, 128], replicated
- norm_master: float32 [2, 6, 128], replicated
- triangle_copy: bfloat16 [2, 6, 128, 128], replicated
- expand_copy: bfloat16 [2, 2, 128, 512], replicated
- shrink_copy: bfloat16 [2, 512, 128], replicated
- grad_norm: float32 [], replicated
The draws below stay inside these ranges and needn't reach their ends.
Inputs may be any that keep to these rules, and one draw needn't show every extreme that they name: `lengths`: each length lies between 256 and 512, and one crop of every draw has all 512 tokens. `norm_params`: gains lie between 0.7 and 1.3.
All inputs are finite; a program needn't handle non-finite values.
Results may differ from the reference program's by a relative error of at most 0.018.
Values may be sent and summed in bfloat16 or wider, within the bound.
A program may use at most 256 MiB of HBM per device.

```python
import math
import jax
import jax.numpy as jnp
from jax import lax

C = 128
HID = 512
CROP = 512
MB = 2
LAYERS = 2
STEP = 10
PARAMS = 589824


def draw_lengths(key, part):
    key = jax.random.fold_in(key, 11)
    key_values, key_pick = jax.random.split(key)
    values = jax.random.randint(key_values, (MB,), CROP // 2, CROP + 1)
    chosen = jax.random.randint(key_pick, (), 0, MB)
    return jnp.where(jnp.arange(MB) == chosen, CROP, values).astype(jnp.int32)


def draw_norm_params(key, part):
    key = jax.random.fold_in(key, 7)
    key_gain, key_bias = jax.random.split(key)
    gains = jax.random.uniform(key_gain, (LAYERS, 3, C), jnp.float32, 0.7, 1.3)
    biases = 0.3 * jax.random.normal(key_bias, (LAYERS, 3, C), jnp.float32)
    return jnp.stack([gains, biases], axis=2).reshape(LAYERS, 6, C).astype(jnp.float32)


def block_scale(rng, shape, pieces, smallest, top_value):
    level = 1.0
    for position, parts in pieces:
        heights = jax.random.uniform(jax.random.fold_in(jax.random.fold_in(rng, 6), position), (parts,), jnp.float32, smallest / len(pieces), top_value / len(pieces))
        level = level * jnp.repeat(jnp.exp(heights), shape[position] // parts).reshape((-1,) + (1,) * (len(shape) - 1 - position))
    return level


def bell_draw(own_key, dims, deviation, bound, cuts=(), held_as=jnp.bfloat16):
    array = deviation * jax.random.normal(own_key, dims, jnp.float32)
    if cuts:
        array = array * block_scale(own_key, dims, cuts, -0.22, 0.18)
    return jnp.clip(array, -bound, bound).astype(held_as)


def setup_inputs(seed: int = 0) -> dict:
    splits = jax.random.split(jax.random.key(seed), 16)
    return {
        "pair_in": bell_draw(splits[0], (MB, CROP, CROP, C), 1.0, 6.0, ((1, 16), (2, 8))),
        "lengths": draw_lengths(jax.random.fold_in(splits[15], 71), 0),
        "pair_cotangent": bell_draw(splits[2], (MB, CROP, CROP, C), 1.0, 6.0, ((1, 16), (2, 8))),
        "triangle_weights": bell_draw(splits[3], (LAYERS, 6, C, C), C ** -0.5, 0.5, (), jnp.float32),
        "expand_weights": bell_draw(splits[4], (LAYERS, 2, C, HID), C ** -0.5, 0.5, (), jnp.float32),
        "shrink_weights": bell_draw(splits[5], (LAYERS, HID, C), HID ** -0.5, 0.25, (), jnp.float32),
        "norm_params": draw_norm_params(jax.random.fold_in(splits[15], 71), 0),
        "triangle_first": bell_draw(splits[7], (LAYERS, 6, C, C), (0.11 * PARAMS ** -0.5), 0.001953125, (), jnp.float32),
        "triangle_second": jnp.clip(jnp.exp(jax.random.uniform(splits[8], (LAYERS, 6, C, C), jnp.float32, math.log(8.477105128967821e-10), math.log(6.781684103174257e-09))), 8.477105128967821e-10, 6.781684103174257e-09),
        "expand_first": bell_draw(splits[9], (LAYERS, 2, C, HID), (0.11 * PARAMS ** -0.5), 0.001953125, (), jnp.float32),
        "expand_second": jnp.clip(jnp.exp(jax.random.uniform(splits[10], (LAYERS, 2, C, HID), jnp.float32, math.log(8.477105128967821e-10), math.log(6.781684103174257e-09))), 8.477105128967821e-10, 6.781684103174257e-09),
        "shrink_first": bell_draw(splits[11], (LAYERS, HID, C), (0.11 * PARAMS ** -0.5), 0.001953125, (), jnp.float32),
        "shrink_second": jnp.clip(jnp.exp(jax.random.uniform(splits[12], (LAYERS, HID, C), jnp.float32, math.log(8.477105128967821e-10), math.log(6.781684103174257e-09))), 8.477105128967821e-10, 6.781684103174257e-09),
        "norm_first": bell_draw(splits[13], (LAYERS, 6, C), (0.44 * PARAMS ** -0.5), 0.0078125, (), jnp.float32),
        "norm_second": jnp.clip(jnp.exp(jax.random.uniform(splits[14], (LAYERS, 6, C), jnp.float32, math.log(1.3563368206348514e-08), math.log(1.0850694565078811e-07))), 1.3563368206348514e-08, 1.0850694565078811e-07),
    }


EPS_NORM = 1e-05
BETA_ONE = 0.9
BETA_TWO = 0.999
ADAM_EPS = 1e-08
RATE = 0.1
NORM_RATE = 0.5
DECAY_RATE = 0.01
CLIP = 1.0

@jax.custom_vjp
def low(v):
    return lax.optimization_barrier(v.astype(jnp.bfloat16)).astype(jnp.float32)

@jax.custom_vjp
def low_back(v):
    return v

def low_keep(v):
    return (low(v), None)

def low_pass(kept, grad):
    return (grad,)

def back_keep(v):
    return (v, None)

def back_low(kept, grad):
    return (low(grad),)
low.defvjp(low_keep, low_pass)
low_back.defvjp(back_keep, back_low)

def layer_norm(values, gain, bias):
    average = lax.optimization_barrier(jnp.mean(values, axis=-1, keepdims=True))
    centered = values - average
    variance = lax.optimization_barrier(jnp.mean(centered * centered, axis=-1, keepdims=True))
    return centered * lax.rsqrt(variance + EPS_NORM) * gain + bias

def matmul(values, weight):
    return jnp.einsum('...c,ce->...e', values, weight, precision=lax.Precision.HIGHEST)

def transition(row_block, gain, bias, expand, shrink):
    normed = low(layer_norm(row_block, gain, bias))
    gate_part = low_back(matmul(normed, expand[0]))
    up_part = low_back(matmul(normed, expand[1]))
    hidden_low = low(jax.nn.silu(gate_part) * up_part)
    return low_back(matmul(hidden_low, shrink))

def pair_layer(state, pair_mask, triangle, expand, shrink, norms):
    normed = low(layer_norm(state, norms[0], norms[1]))
    projected = low_back(jnp.einsum('ijc,nce->nije', normed, triangle[:5], precision=lax.Precision.HIGHEST))
    left_side = low(pair_mask * jax.nn.sigmoid(projected[0]) * projected[1])
    right_side = low(pair_mask * jax.nn.sigmoid(projected[2]) * projected[3])
    update = low_back(jnp.einsum('ikc,jkc->ijc', left_side, right_side, precision=lax.Precision.HIGHEST))
    update_in = low(layer_norm(update, norms[2], norms[3]))
    branch = low_back(matmul(update_in, triangle[5]))
    middle = state + jax.nn.sigmoid(projected[4]) * branch
    crop_size = middle.shape[0]
    block_rows = math.gcd(crop_size, 64)
    blocks = middle.reshape(crop_size // block_rows, block_rows, crop_size, middle.shape[-1])
    block_step = jax.checkpoint(lambda row_block: transition(row_block, norms[4], norms[5], expand, shrink))
    branch_two = lax.map(block_step, blocks).reshape(middle.shape)
    return middle + branch_two

def forward(params, pair_value, length):
    triangle, expand, shrink, norms = params
    triangle = low(triangle)
    expand = low(expand)
    shrink = low(shrink)
    positions = jnp.arange(CROP)
    valid_rows = (positions < length).astype(jnp.float32)
    pair_mask = (valid_rows[:, None] * valid_rows[None, :])[:, :, None]
    state = pair_value
    for depth_index in range(LAYERS):
        state = jax.checkpoint(pair_layer)(state, pair_mask, triangle[depth_index], expand[depth_index], shrink[depth_index], norms[depth_index])
    return state

def adamw(weight, gradient, moment, second_moment, clip_factor, step_rate, decay_rate):
    clipped = gradient * clip_factor
    moment_new = BETA_ONE * moment + (1.0 - BETA_ONE) * clipped
    square_new = BETA_TWO * second_moment + (1.0 - BETA_TWO) * clipped * clipped
    correct_one = 1.0 - BETA_ONE ** STEP
    correct_two = 1.0 - BETA_TWO ** STEP
    update_step = moment_new / correct_one / (jnp.sqrt(square_new / correct_two) + ADAM_EPS)
    renewed = weight - step_rate * (update_step + decay_rate * weight)
    return (moment_new, square_new, renewed)

def reference(pair_in, lengths, pair_cotangent, triangle_weights, expand_weights, shrink_weights, norm_params, triangle_first, triangle_second, expand_first, expand_second, shrink_first, shrink_second, norm_first, norm_second):
    params = (triangle_weights, expand_weights, shrink_weights, norm_params)
    zero_grads = jax.tree.map(jnp.zeros_like, params)

    def crop_step(totals, crop_item):
        pair_value, cotangent, length = crop_item
        result, pullback = jax.vjp(lambda params_in, pair_arg: forward(params_in, pair_arg, length), params, pair_value.astype(jnp.float32))
        crop_grads, pair_grad = pullback(cotangent.astype(jnp.float32))
        totals = jax.tree.map(jnp.add, totals, crop_grads)
        return (totals, (result.astype(jnp.bfloat16), pair_grad))
    totals, (pair_out, pair_grad) = lax.scan(crop_step, zero_grads, (pair_in, pair_cotangent, lengths))
    squares = sum((jnp.sum(entry * entry) for entry in totals))
    grad_norm = jnp.sqrt(squares)
    clip_factor = jnp.minimum(1.0, CLIP / (grad_norm + 1e-06))
    tri_m, tri_v, tri_w = adamw(triangle_weights, totals[0], triangle_first, triangle_second, clip_factor, RATE, DECAY_RATE)
    exp_m, exp_v, exp_w = adamw(expand_weights, totals[1], expand_first, expand_second, clip_factor, RATE, DECAY_RATE)
    shr_m, shr_v, shr_w = adamw(shrink_weights, totals[2], shrink_first, shrink_second, clip_factor, RATE, DECAY_RATE)
    nrm_m, nrm_v, nrm_w = adamw(norm_params, totals[3], norm_first, norm_second, clip_factor, NORM_RATE, 0.0)
    return (pair_out, pair_grad, tri_m, tri_v, tri_w, exp_m, exp_v, exp_w, shr_m, shr_v, shr_w, nrm_m, nrm_v, nrm_w, tri_w.astype(jnp.bfloat16), exp_w.astype(jnp.bfloat16), shr_w.astype(jnp.bfloat16), grad_norm)
```

```python
import functools

import jax
import jax.numpy as jnp
from jax import lax
from jax.experimental import pallas as pl
from jax.experimental.pallas import tpu as pltpu
from jax.sharding import PartitionSpec as P

LAYERS = 2
STEP = 10
CROPS = 2

EPS_NORM = 1e-05
BETA_ONE = 0.9
BETA_TWO = 0.999
ADAM_EPS = 1e-08
RATE = 0.1
NORM_RATE = 0.5
DECAY_RATE = 0.01
CLIP = 1.0

MESH = pl.DeviceIdType.MESH
BF = jnp.bfloat16
F32 = jnp.float32

C = 128
HID = 512
TILES = 16
PAIRS = 2048
WIDE = 256
CHUNKS = PAIRS // WIDE
PER = WIDE // 128
VMEM_LIMIT = 60 << 20


def dot(left, right):
    return lax.dot_general(left, right, (((1,), (0,)), ((), ())), preferred_element_type=F32)


def dot_nt(left, right):
    return lax.dot_general(left, right, (((1,), (1,)), ((), ())), preferred_element_type=F32)


def dot_tn(left, right):
    return lax.dot_general(left, right, (((0,), (0,)), ((), ())), preferred_element_type=F32)


def sigmoid(v):
    return 0.5 * jnp.tanh(0.5 * v) + 0.5


def mean_rows(v):
    return jnp.sum(v, axis=0, keepdims=True) * (1.0 / C)


def normalize(v):
    centered = v - mean_rows(v)
    scale = lax.rsqrt(mean_rows(centered * centered) + EPS_NORM)
    return centered * scale, scale


def normalize_back(grad, gain, hat, scale):
    grad_hat = grad * gain
    return scale * (grad_hat - mean_rows(grad_hat) - hat * mean_rows(grad_hat * hat))


def lanes_of(step):
    return pl.ds(pl.multiple_of(step * WIDE, WIDE), WIDE)


def scatter_tiles(scratch, step, value):
    for part in range(PER):
        scratch[pl.ds(step * PER + part, C, stride=TILES), :] = value[:, part * 128 : part * 128 + 128]


def gather_tiles(scratch, step):
    return jnp.concatenate(
        [scratch[pl.ds(step * PER + part, C, stride=TILES), :] for part in range(PER)], axis=1
    )


def pack_tiles(scratch, send, offset):
    def body(step, carry):
        rows = scratch[pl.ds(pl.multiple_of(step * 256, 256), 256), :]
        send[pl.ds(step * 16, 16), pl.ds(offset, TILES), :] = rows.astype(BF).reshape(16, TILES, 128)
        return carry

    lax.fori_loop(0, C // 16, body, 0)


def unpack_tiles(recv, offset, scratch):
    def body(step, carry):
        block = recv[pl.ds(step * 16, 16), pl.ds(offset, TILES), :]
        scratch[pl.ds(pl.multiple_of(step * 256, 256), 256), :] = block.reshape(256, 128).astype(F32)
        return carry

    lax.fori_loop(0, C // 16, body, 0)


def swap_halves(first, second):
    low = jnp.concatenate([first[:, :64], second[:, :64]], axis=1)
    high = jnp.concatenate([first[:, 64:], second[:, 64:]], axis=1)
    return low, high


def assemble(recv, offset, whole):
    def body(row, carry):
        base = pl.multiple_of(row * 32, 32)
        for pair in range(4):
            low, high = swap_halves(
                recv[row * 8 + 2 * pair, pl.ds(offset, TILES), :],
                recv[row * 8 + 2 * pair + 1, pl.ds(offset, TILES), :],
            )
            whole[pl.ds(base, 16), pair * 128 : pair * 128 + 128] = low
            whole[pl.ds(base + 16, 16), pair * 128 : pair * 128 + 128] = high
        return carry

    lax.fori_loop(0, 16, body, 0)


def disassemble(whole, send, offset):
    def body(row, carry):
        base = pl.multiple_of(row * 32, 32)
        for pair in range(4):
            first, second = swap_halves(
                whole[pl.ds(base, 16), pair * 128 : pair * 128 + 128],
                whole[pl.ds(base + 16, 16), pair * 128 : pair * 128 + 128],
            )
            send[row * 8 + 2 * pair, pl.ds(offset, TILES), :] = first
            send[row * 8 + 2 * pair + 1, pl.ds(offset, TILES), :] = second
        return carry

    lax.fori_loop(0, 16, body, 0)


def load_pairs(pair_ref, out_ref):
    def body(tile, carry):
        rows = jnp.concatenate([pair_ref[tile], pair_ref[tile + TILES]], axis=0).astype(F32)
        out_ref[:, pl.ds(pl.multiple_of(tile * 128, 128), 128)] = rows.T
        return carry

    lax.fori_loop(0, TILES, body, 0)


def store_pairs(value, step, out_ref):
    for part in range(PER):
        rows = value[:, part * 128 : part * 128 + 128].T
        out_ref[step * PER + part] = rows[:64].astype(out_ref.dtype)
        out_ref[step * PER + part + TILES] = rows[64:].astype(out_ref.dtype)


def project_step(x, mask, five, norms, scratch_a, scratch_b, gate_ref, step):
    hat, _ = normalize(x)
    normed = (hat * norms[0] + norms[1]).astype(BF)
    projected = dot(five[...], normed)
    left = mask * sigmoid(projected[:C]) * projected[C : 2 * C]
    right = mask * sigmoid(projected[2 * C : 3 * C]) * projected[3 * C : 4 * C]
    scatter_tiles(scratch_a, step, left)
    scatter_tiles(scratch_b, step, right)
    gate_ref[:, lanes_of(step)] = sigmoid(projected[4 * C :])


def update_step(x, gate, z, out_t, expand_t, norms):
    z_hat, z_scale = normalize(z)
    updated = (z_hat * norms[2] + norms[3]).astype(BF)
    branch = dot(out_t[...], updated)
    middle = x + gate * branch
    mid_hat, mid_scale = normalize(middle)
    normed = (mid_hat * norms[4] + norms[5]).astype(BF)
    gate_up = dot(expand_t[...], normed)
    return (z_hat, z_scale, updated, branch, middle, mid_hat, mid_scale, normed, gate_up)


def swiglu(gate_up):
    gate_half = gate_up[:HID]
    sig = sigmoid(gate_half)
    silu = gate_half * sig
    return (sig, silu, (silu * gate_up[HID:]).astype(BF))


def back_step(upstream, parts, hidden_parts, gate, shrink, expand, out_n, norms, grads):
    z_hat, z_scale, updated, branch, middle, mid_hat, mid_scale, normed, gate_up = parts
    sig, silu, hidden = hidden_parts
    g_tri, g_exp, g_shr, g_norm = grads
    upstream_low = upstream.astype(BF)
    g_shr[...] += dot_nt(hidden, upstream_low)
    grad_hidden = dot(shrink[...], upstream_low)
    grad_gate = (grad_hidden * gate_up[HID:] * (sig + silu * (1.0 - sig))).astype(BF)
    grad_up = (grad_hidden * silu).astype(BF)
    grad_gate_up = jnp.concatenate([grad_gate, grad_up], axis=0)
    g_exp[...] += dot_nt(normed, grad_gate_up)
    grad_normed = dot(expand[...], grad_gate_up)
    add_norm(g_norm, 4, grad_normed * mid_hat, grad_normed)
    grad_middle = upstream + normalize_back(grad_normed, norms[4], mid_hat, mid_scale)
    scaled = grad_middle * gate
    grad_branch = scaled.astype(BF)
    grad_out_gate = (scaled * branch * (1.0 - gate)).astype(BF)
    g_tri[:, 5 * C :] += dot_nt(updated, grad_branch)
    grad_updated = dot(out_n[...], grad_branch)
    add_norm(g_norm, 2, grad_updated * z_hat, grad_updated)
    grad_z = normalize_back(grad_updated, norms[2], z_hat, z_scale)
    return (grad_middle, grad_out_gate, grad_z)


def add_norm(g_norm, index, gain_term, bias_term):
    for place, term in ((index, gain_term), (index + 1, bias_term)):
        total = term[:, :128]
        for part in range(1, PER):
            total = total + term[:, part * 128 : part * 128 + 128]
        g_norm[place] += total


def project_back_step(
    x, mask, grad_left, grad_right, grad_out_gate, grad_middle, five, five_n, norms, g_tri, g_norm
):
    hat, scale = normalize(x)
    normed = (hat * norms[0] + norms[1]).astype(BF)
    projected = dot(five[: 4 * C, :], normed)
    pieces = []
    for grad, base in ((grad_left, 0), (grad_right, 2 * C)):
        sig = sigmoid(projected[base : base + C])
        masked = grad * mask * sig
        pieces.append((masked * projected[base + C : base + 2 * C] * (1.0 - sig)).astype(BF))
        pieces.append(masked.astype(BF))
    pieces.append(grad_out_gate)
    grad_projected = jnp.concatenate(pieces, axis=0)
    g_tri[:, : 5 * C] += dot_nt(normed, grad_projected)
    grad_normed = dot(five_n[...], grad_projected)
    add_norm(g_norm, 0, grad_normed * hat, grad_normed)
    return grad_middle + normalize_back(grad_normed, norms[0], hat, scale)


class Norms:
    def __init__(self, ref, layer):
        self.ref, self.layer = ref, layer

    def __getitem__(self, index):
        value = self.ref[self.layer, index]
        return jnp.concatenate([value] * PER, axis=1)


def first_kernel(pair, mask, five, norms, send, x_out, gate_out, scratch_a, scratch_b):
    for crop in range(CROPS):
        load_pairs(pair.at[crop], x_out.at[crop])

        def body(step, carry):
            x = x_out[crop, :, lanes_of(step)]
            project_step(
                x, mask[crop, :, lanes_of(step)], five.at[0], Norms(norms, 0), scratch_a, scratch_b, gate_out.at[crop], step
            )
            return carry

        lax.fori_loop(0, CHUNKS, body, 0)
        pack_tiles(scratch_a, send.at[:, pl.ds(crop * 32, 32)], 0)
        pack_tiles(scratch_b, send.at[:, pl.ds(crop * 32, 32)], TILES)


def middle_kernel(recv, mask, x_in, gate_in, out_t, expand_t, shrink_t, five, norms, send, x_out, gate_out, scratch_a, scratch_b, scratch_z):
    for crop in range(CROPS):
        unpack_tiles(recv, crop * TILES, scratch_z)

        def body(step, carry):
            x = x_in[crop, :, lanes_of(step)]
            gate = gate_in[crop, :, lanes_of(step)]
            parts = update_step(x, gate, gather_tiles(scratch_z, step), out_t.at[0], expand_t.at[0], Norms(norms, 0))
            _, _, hidden = swiglu(parts[-1])
            x_new = parts[4] + dot(shrink_t[0], hidden)
            x_out[crop, :, lanes_of(step)] = x_new
            project_step(
                x_new, mask[crop, :, lanes_of(step)], five.at[1], Norms(norms, 1), scratch_a, scratch_b, gate_out.at[crop], step
            )
            return carry

        lax.fori_loop(0, CHUNKS, body, 0)
        pack_tiles(scratch_a, send.at[:, pl.ds(crop * 32, 32)], 0)
        pack_tiles(scratch_b, send.at[:, pl.ds(crop * 32, 32)], TILES)


def zero(*refs):
    for ref in refs:
        ref[...] = jnp.zeros_like(ref)


def turn_kernel(
    recv, x_in, gate_in, cotangent, out_t, expand_t, shrink_t, shrink, expand, out_n, norms,
    pair_out, send, grad_mid, grad_gate, g_tri, g_exp, g_shr, g_norm, scratch_z, scratch_d, cot,
):
    zero(g_tri, g_exp, g_shr, g_norm)
    for crop in range(CROPS):
        unpack_tiles(recv, crop * TILES, scratch_z)
        load_pairs(cotangent.at[crop], cot)

        def body(step, carry):
            lanes = lanes_of(step)
            gate = gate_in[crop, :, lanes]
            gains = Norms(norms, 1)
            parts = update_step(x_in[crop, :, lanes], gate, gather_tiles(scratch_z, step), out_t.at[1], expand_t.at[1], gains)
            hidden_parts = swiglu(parts[-1])
            store_pairs(parts[4] + dot(shrink_t[1], hidden_parts[2]), step, pair_out.at[crop])
            middle, out_gate, grad_z = back_step(
                cot[:, lanes], parts, hidden_parts, gate, shrink.at[1], expand.at[1], out_n.at[1], gains, (g_tri, g_exp, g_shr, g_norm)
            )
            grad_mid[crop, :, lanes] = middle
            grad_gate[crop, :, lanes] = out_gate
            scatter_tiles(scratch_d, step, grad_z)
            return carry

        lax.fori_loop(0, CHUNKS, body, 0)
        pack_tiles(scratch_d, send, crop * TILES)


def deep_kernel(
    recv_ab, recv_z, mask, x_one, x_zero, gate_in, mid_in, out_gate_in, five, five_n, out_t, expand_t, shrink, expand, out_n, norms,
    send, grad_mid, grad_gate, g_five, g_norm_one, g_tri, g_exp, g_shr, g_norm, scratch_z, scratch_a, scratch_b, scratch_d,
):
    zero(g_five, g_norm_one, g_tri, g_exp, g_shr, g_norm)
    for crop in range(CROPS):
        unpack_tiles(recv_ab, crop * 32, scratch_a)
        unpack_tiles(recv_ab, crop * 32 + TILES, scratch_b)
        unpack_tiles(recv_z, crop * TILES, scratch_z)

        def body(step, carry):
            lanes = lanes_of(step)
            upstream = project_back_step(
                x_one[crop, :, lanes], mask[crop, :, lanes], gather_tiles(scratch_a, step), gather_tiles(scratch_b, step),
                out_gate_in[crop, :, lanes], mid_in[crop, :, lanes], five.at[1], five_n.at[1], Norms(norms, 1), g_five, g_norm_one,
            )
            gate = gate_in[crop, :, lanes]
            gains = Norms(norms, 0)
            parts = update_step(x_zero[crop, :, lanes], gate, gather_tiles(scratch_z, step), out_t.at[0], expand_t.at[0], gains)
            middle, out_gate, grad_z = back_step(
                upstream, parts, swiglu(parts[-1]), gate, shrink.at[0], expand.at[0], out_n.at[0], gains, (g_tri, g_exp, g_shr, g_norm)
            )
            grad_mid[crop, :, lanes] = middle
            grad_gate[crop, :, lanes] = out_gate
            scatter_tiles(scratch_d, step, grad_z)
            return carry

        lax.fori_loop(0, CHUNKS, body, 0)
        pack_tiles(scratch_d, send, crop * TILES)


def last_kernel(
    recv_ab, mask, x_zero, mid_in, out_gate_in, five, five_n, norms, pair_grad, g_five, g_norm, scratch_a, scratch_b
):
    zero(g_five, g_norm)
    for crop in range(CROPS):
        unpack_tiles(recv_ab, crop * 32, scratch_a)
        unpack_tiles(recv_ab, crop * 32 + TILES, scratch_b)

        def body(step, carry):
            lanes = lanes_of(step)
            upstream = project_back_step(
                x_zero[crop, :, lanes], mask[crop, :, lanes], gather_tiles(scratch_a, step), gather_tiles(scratch_b, step),
                out_gate_in[crop, :, lanes], mid_in[crop, :, lanes], five.at[0], five_n.at[0], Norms(norms, 0), g_five, g_norm,
            )
            store_pairs(upstream, step, pair_grad.at[crop])
            return carry

        lax.fori_loop(0, CHUNKS, body, 0)


def join_kernel(recv, send, left_out, right_out, whole):
    for crop in range(CROPS):
        assemble(recv, crop * 32, left_out.at[crop])
        assemble(recv, crop * 32 + TILES, right_out.at[crop])
        whole[...] = dot_nt(left_out[crop], right_out[crop]).astype(BF)
        disassemble(whole, send, crop * TILES)


def join_back_kernel(recv, left, right, send, whole, result):
    for crop in range(CROPS):
        assemble(recv, crop * TILES, whole)
        result[...] = dot(whole[...], right[crop]).astype(BF)
        disassemble(result, send, crop * 32)
        result[...] = dot_tn(whole[...], left[crop]).astype(BF)
        disassemble(result, send, crop * 32 + TILES)


def exchange_kernel(rows, cols, x_ref, o_ref, send_sem, recv_sem, local_sem):
    row = lax.axis_index("row")
    col = lax.axis_index("col")
    me = row * cols + col
    count = rows * cols

    def target(offset):
        return lax.rem(row + offset // cols, rows), lax.rem(col + lax.rem(offset, cols), cols)

    barrier = pltpu.get_barrier_semaphore()

    def greet(offset, carry):
        pl.semaphore_signal(barrier, inc=1, device_id=target(offset), device_id_type=MESH)
        return carry

    lax.fori_loop(1, count, greet, 0)
    pl.semaphore_wait(barrier, count - 1)
    own = pltpu.make_async_copy(x_ref.at[me], o_ref.at[me], local_sem)
    own.start()

    def push(offset, carry):
        to_row, to_col = target(offset)
        pltpu.make_async_remote_copy(
            x_ref.at[to_row * cols + to_col], o_ref.at[me], send_sem, recv_sem, device_id=(to_row, to_col), device_id_type=MESH
        ).start()
        return carry

    lax.fori_loop(1, count, push, 0)
    own.wait()
    others = pl.ds(0, count - 1)
    pltpu.make_async_copy(x_ref.at[others], o_ref.at[others], send_sem).wait()
    pltpu.make_async_copy(x_ref.at[others], o_ref.at[others], recv_sem).wait()


def exchange(x, rows, cols):
    return pl.pallas_call(
        functools.partial(exchange_kernel, rows, cols),
        out_shape=jax.ShapeDtypeStruct(x.shape, x.dtype),
        in_specs=[pl.BlockSpec(memory_space=pltpu.VMEM)],
        out_specs=pl.BlockSpec(memory_space=pltpu.VMEM),
        scratch_shapes=[pltpu.SemaphoreType.DMA] * 3,
        compiler_params=pltpu.CompilerParams(
            collective_id=x.shape[1] // 32, has_side_effects=True, vmem_limit_bytes=VMEM_LIMIT
        ),
        name=f"exchange_{x.shape[1]}",
    )(x)


def call(kernel, outs, scratch, *args):
    return pl.pallas_call(
        kernel,
        out_shape=[jax.ShapeDtypeStruct(shape, dtype) for shape, dtype in outs],
        in_specs=[pl.BlockSpec(memory_space=pltpu.VMEM)] * len(args),
        out_specs=[pl.BlockSpec(memory_space=pltpu.VMEM)] * len(outs),
        scratch_shapes=[pltpu.VMEM(shape, dtype) for shape, dtype in scratch],
        compiler_params=pltpu.CompilerParams(vmem_limit_bytes=VMEM_LIMIT),
        name=kernel.__name__,
    )(*args)


def adamw(weight, gradient, moment, second_moment, clip_factor, step_rate, decay_rate):
    clipped = gradient * clip_factor
    moment_new = BETA_ONE * moment + (1.0 - BETA_ONE) * clipped
    square_new = BETA_TWO * second_moment + (1.0 - BETA_TWO) * clipped * clipped
    correct_one = 1.0 - BETA_ONE**STEP
    correct_two = 1.0 - BETA_TWO**STEP
    update = moment_new / correct_one / (jnp.sqrt(square_new / correct_two) + ADAM_EPS)
    renewed = weight - step_rate * (update + decay_rate * weight)
    return (moment_new, square_new, renewed)


def local(
    rows, cols,
    pair_in, lengths, pair_cotangent, triangle_weights, expand_weights, shrink_weights, norm_params, triangle_first,
    triangle_second, expand_first, expand_second, shrink_first, shrink_second, norm_first, norm_second,
):
    rows_dev, cols_dev = pair_in.shape[1], pair_in.shape[2]
    row_ids = lax.axis_index("row") * rows_dev + jnp.arange(rows_dev)
    col_ids = lax.axis_index("col") * cols_dev + jnp.arange(cols_dev)
    valid_rows = row_ids[None, :] < lengths[:, None]
    valid_cols = col_ids[None, :] < lengths[:, None]
    mask = (valid_rows[:, :, None] & valid_cols[:, None, :]).astype(F32)
    mask = mask.reshape(CROPS, 2, TILES, cols_dev).transpose(0, 2, 1, 3).reshape(CROPS, 1, PAIRS)

    triangle_low = triangle_weights.astype(BF)
    expand_low = expand_weights.astype(BF)
    shrink = shrink_weights.astype(BF)
    turned = jnp.swapaxes(triangle_low, 2, 3)
    five = turned[:, :5].reshape(LAYERS, 5 * C, C)
    out_t = turned[:, 5]
    five_n = jnp.moveaxis(triangle_low[:, :5], 1, 2).reshape(LAYERS, C, 5 * C)
    out_n = triangle_low[:, 5]
    expand_t = jnp.swapaxes(expand_low, 2, 3).reshape(LAYERS, 2 * HID, C)
    expand = jnp.moveaxis(expand_low, 1, 2).reshape(LAYERS, C, 2 * HID)
    shrink_t = jnp.swapaxes(shrink, 1, 2)
    norms = jnp.broadcast_to(norm_params[..., None], norm_params.shape + (128,))

    big = (CROPS, C, PAIRS)
    tiles = ((PAIRS, 128), F32)
    wide_send = ((C, CROPS * 2 * TILES, 128), BF)
    slim_send = ((C, CROPS * TILES, 128), BF)
    square = ((CROPS, 512, 512), BF)
    grads = [((C, 6 * C), F32), ((C, 2 * HID), F32), ((HID, C), F32), ((6, C, 128), F32)]
    five_grads = [((C, 5 * C), F32), ((6, C, 128), F32)]

    send, x_zero, gate_zero = call(first_kernel, [wide_send, (big, F32), (big, F32)], [tiles, tiles], pair_in, mask, five, norms)
    recv = exchange(send, rows, cols)
    send, left_zero, right_zero = call(join_kernel, [slim_send, square, square], [((512, 512), BF)], recv)
    z_zero = exchange(send, rows, cols)
    send, x_one, gate_one = call(
        middle_kernel, [wide_send, (big, F32), (big, F32)], [tiles, tiles, tiles],
        z_zero, mask, x_zero, gate_zero, out_t, expand_t, shrink_t, five, norms,
    )
    recv = exchange(send, rows, cols)
    send, left_one, right_one = call(join_kernel, [slim_send, square, square], [((512, 512), BF)], recv)
    z_one = exchange(send, rows, cols)
    pair_out, send, mid_one, out_gate_one, *grads_one = call(
        turn_kernel, [(pair_in.shape, BF), slim_send, (big, F32), (big, BF)] + grads, [tiles, tiles, ((C, PAIRS), F32)],
        z_one, x_one, gate_one, pair_cotangent, out_t, expand_t, shrink_t, shrink, expand, out_n, norms,
    )
    recv = exchange(send, rows, cols)
    (send,) = call(join_back_kernel, [wide_send], [((512, 512), BF)] * 2, recv, left_one, right_one)
    recv = exchange(send, rows, cols)
    send, mid_zero, out_gate_zero, five_one, norm_one, *grads_zero = call(
        deep_kernel, [slim_send, (big, F32), (big, BF)] + five_grads + grads, [tiles] * 4,
        recv, z_zero, mask, x_one, x_zero, gate_zero, mid_one, out_gate_one, five, five_n, out_t, expand_t, shrink, expand, out_n, norms,
    )
    recv = exchange(send, rows, cols)
    (send,) = call(join_back_kernel, [wide_send], [((512, 512), BF)] * 2, recv, left_zero, right_zero)
    recv = exchange(send, rows, cols)
    pair_grad, five_zero, norm_zero = call(
        last_kernel, [(pair_in.shape, F32)] + five_grads, [tiles, tiles],
        recv, mask, x_zero, mid_zero, out_gate_zero, five, five_n, norms,
    )

    grad_triangle, grad_expand, grad_shrink, grad_norms = [], [], [], []
    for (g_tri, g_exp, g_shr, g_norm), g_five, g_norm_first in (
        (grads_zero, five_zero, norm_zero),
        (grads_one, five_one, norm_one),
    ):
        g_tri = jnp.concatenate([g_five, g_tri[:, 5 * C :]], axis=1)
        grad_triangle.append(jnp.moveaxis(g_tri.reshape(C, 6, C), 1, 0))
        grad_expand.append(jnp.moveaxis(g_exp.reshape(C, 2, HID), 1, 0))
        grad_shrink.append(g_shr)
        grad_norms.append(jnp.sum(g_norm + g_norm_first, axis=-1))
    totals = lax.psum(
        (jnp.stack(grad_triangle), jnp.stack(grad_expand), jnp.stack(grad_shrink), jnp.stack(grad_norms)), ("row", "col")
    )
    squares = sum(jnp.sum(entry * entry) for entry in totals)
    grad_norm = jnp.sqrt(squares)
    clip_factor = jnp.minimum(1.0, CLIP / (grad_norm + 1e-06))
    tri = adamw(triangle_weights, totals[0], triangle_first, triangle_second, clip_factor, RATE, DECAY_RATE)
    exp = adamw(expand_weights, totals[1], expand_first, expand_second, clip_factor, RATE, DECAY_RATE)
    shr = adamw(shrink_weights, totals[2], shrink_first, shrink_second, clip_factor, RATE, DECAY_RATE)
    nrm = adamw(norm_params, totals[3], norm_first, norm_second, clip_factor, NORM_RATE, 0.0)
    copies = (tri[2].astype(BF), exp[2].astype(BF), shr[2].astype(BF))
    return (pair_out, pair_grad) + tri + exp + shr + nrm + copies + (grad_norm,)


def solution(mesh):
    pair = P(None, "row", "col", None)
    return jax.shard_map(
        functools.partial(local, mesh.shape["row"], mesh.shape["col"]),
        mesh=mesh,
        in_specs=(pair, P(), pair) + (P(),) * 12,
        out_specs=(pair, pair) + (P(),) * 16,
        check_vma=False,
    )
```

```python
import functools

import jax
import jax.numpy as jnp
from jax import lax
from jax.experimental import pallas as pl
from jax.experimental.pallas import tpu as pltpu
from jax.sharding import PartitionSpec as P

LAYERS = 2
STEP = 10
CROPS = 2

EPS_NORM = 1e-05
BETA_ONE = 0.9
BETA_TWO = 0.999
ADAM_EPS = 1e-08
RATE = 0.1
NORM_RATE = 0.5
DECAY_RATE = 0.01
CLIP = 1.0

MESH = pl.DeviceIdType.MESH
BF = jnp.bfloat16
F32 = jnp.float32

C = 128
HID = 512
TILES = 16
PAIRS = 2048
WIDE = 256
CHUNKS = PAIRS // WIDE
PER = WIDE // 128
VMEM_LIMIT = 60 << 20

EXPAND_ROW = LAYERS * 6 * C
SHRINK_ROW = EXPAND_ROW + LAYERS * 2 * HID
NORM_ROW = SHRINK_ROW + LAYERS * HID
PIECE = 48
PIECES = 49
HALF = PIECE * PIECES


def triangle_rows(layer, matrix):
    return pl.ds((layer * 6 + matrix) * C, C)


def expand_rows(layer, matrix, block):
    return pl.ds(EXPAND_ROW + ((layer * 2 + matrix) * 4 + block) * C, C)


def shrink_rows(layer):
    return pl.ds(SHRINK_ROW + layer * HID, HID)


def dot(left, right):
    return lax.dot_general(left, right, (((1,), (0,)), ((), ())), preferred_element_type=F32)


def dot_nt(left, right):
    return lax.dot_general(left, right, (((1,), (1,)), ((), ())), preferred_element_type=F32)


def dot_tn(left, right):
    return lax.dot_general(left, right, (((0,), (0,)), ((), ())), preferred_element_type=F32)


def sigmoid(v):
    return 0.5 * jnp.tanh(0.5 * v) + 0.5


def mean_rows(v):
    return jnp.sum(v, axis=0, keepdims=True) * (1.0 / C)


def normalize(v):
    centered = v - mean_rows(v)
    scale = lax.rsqrt(mean_rows(centered * centered) + EPS_NORM)
    return centered * scale, scale


def normalize_back(grad, gain, hat, scale):
    grad_hat = grad * gain
    return scale * (grad_hat - mean_rows(grad_hat) - hat * mean_rows(grad_hat * hat))


def lanes_of(step):
    return pl.ds(pl.multiple_of(step * WIDE, WIDE), WIDE)


def scatter_tiles(scratch, step, value):
    for part in range(PER):
        scratch[pl.ds(step * PER + part, C, stride=TILES), :] = value[:, part * 128 : part * 128 + 128]


def gather_tiles(scratch, step):
    return jnp.concatenate(
        [scratch[pl.ds(step * PER + part, C, stride=TILES), :] for part in range(PER)], axis=1
    )


def pack_tiles(scratch, send, offset):
    def body(step, carry):
        rows = scratch[pl.ds(pl.multiple_of(step * 256, 256), 256), :]
        send[pl.ds(step * 16, 16), pl.ds(offset, TILES), :] = rows.astype(BF).reshape(16, TILES, 128)
        return carry

    lax.fori_loop(0, C // 16, body, 0)


def unpack_tiles(recv, offset, scratch):
    def body(step, carry):
        block = recv[pl.ds(step * 16, 16), pl.ds(offset, TILES), :]
        scratch[pl.ds(pl.multiple_of(step * 256, 256), 256), :] = block.reshape(256, 128).astype(F32)
        return carry

    lax.fori_loop(0, C // 16, body, 0)


def swap_halves(first, second):
    low = jnp.concatenate([first[:, :64], second[:, :64]], axis=1)
    high = jnp.concatenate([first[:, 64:], second[:, 64:]], axis=1)
    return low, high


def assemble(recv, offset, whole):
    def body(row, carry):
        base = pl.multiple_of(row * 32, 32)
        for pair in range(4):
            low, high = swap_halves(
                recv[row * 8 + 2 * pair, pl.ds(offset, TILES), :],
                recv[row * 8 + 2 * pair + 1, pl.ds(offset, TILES), :],
            )
            whole[pl.ds(base, 16), pair * 128 : pair * 128 + 128] = low
            whole[pl.ds(base + 16, 16), pair * 128 : pair * 128 + 128] = high
        return carry

    lax.fori_loop(0, 16, body, 0)


def disassemble(whole, send, offset):
    def body(row, carry):
        base = pl.multiple_of(row * 32, 32)
        for pair in range(4):
            first, second = swap_halves(
                whole[pl.ds(base, 16), pair * 128 : pair * 128 + 128],
                whole[pl.ds(base + 16, 16), pair * 128 : pair * 128 + 128],
            )
            send[row * 8 + 2 * pair, pl.ds(offset, TILES), :] = first
            send[row * 8 + 2 * pair + 1, pl.ds(offset, TILES), :] = second
        return carry

    lax.fori_loop(0, 16, body, 0)


def load_pairs(pair_ref, out_ref):
    def body(tile, carry):
        rows = jnp.concatenate([pair_ref[tile], pair_ref[tile + TILES]], axis=0).astype(F32)
        out_ref[:, pl.ds(pl.multiple_of(tile * 128, 128), 128)] = rows.T
        return carry

    lax.fori_loop(0, TILES, body, 0)


def store_pairs(value, step, out_ref):
    for part in range(PER):
        rows = value[:, part * 128 : part * 128 + 128].T
        out_ref[step * PER + part] = rows[:64].astype(out_ref.dtype)
        out_ref[step * PER + part + TILES] = rows[64:].astype(out_ref.dtype)


def project_step(x, mask, five, norms, scratch_a, scratch_b, gate_ref, step):
    hat, _ = normalize(x)
    normed = (hat * norms[0] + norms[1]).astype(BF)
    projected = dot(five[...], normed)
    left = mask * sigmoid(projected[:C]) * projected[C : 2 * C]
    right = mask * sigmoid(projected[2 * C : 3 * C]) * projected[3 * C : 4 * C]
    scatter_tiles(scratch_a, step, left)
    scatter_tiles(scratch_b, step, right)
    gate_ref[:, lanes_of(step)] = sigmoid(projected[4 * C :])


def update_step(x, gate, z, out_t, expand_t, norms):
    z_hat, z_scale = normalize(z)
    updated = (z_hat * norms[2] + norms[3]).astype(BF)
    branch = dot(out_t[...], updated)
    middle = x + gate * branch
    mid_hat, mid_scale = normalize(middle)
    normed = (mid_hat * norms[4] + norms[5]).astype(BF)
    gate_up = dot(expand_t[...], normed)
    return (z_hat, z_scale, updated, branch, middle, mid_hat, mid_scale, normed, gate_up)


def swiglu(gate_up):
    gate_half = gate_up[:HID]
    sig = sigmoid(gate_half)
    silu = gate_half * sig
    return (sig, silu, (silu * gate_up[HID:]).astype(BF))


def back_step(upstream, parts, hidden_parts, gate, shrink, expand, out_n, norms, grads):
    z_hat, z_scale, updated, branch, middle, mid_hat, mid_scale, normed, gate_up = parts
    sig, silu, hidden = hidden_parts
    layer, grad_rows, g_norm = grads
    upstream_low = upstream.astype(BF)
    grad_rows[shrink_rows(layer), :] += dot_nt(hidden, upstream_low)
    grad_hidden = dot(shrink[...], upstream_low)
    grad_gate = (grad_hidden * gate_up[HID:] * (sig + silu * (1.0 - sig))).astype(BF)
    grad_up = (grad_hidden * silu).astype(BF)
    grad_gate_up = jnp.concatenate([grad_gate, grad_up], axis=0)
    term = dot_nt(normed, grad_gate_up)
    for block in range(8):
        grad_rows[expand_rows(layer, block // 4, block % 4), :] += term[:, block * C : block * C + C]
    grad_normed = dot(expand[...], grad_gate_up)
    add_norm(g_norm, 4, grad_normed * mid_hat, grad_normed)
    grad_middle = upstream + normalize_back(grad_normed, norms[4], mid_hat, mid_scale)
    scaled = grad_middle * gate
    grad_branch = scaled.astype(BF)
    grad_out_gate = (scaled * branch * (1.0 - gate)).astype(BF)
    grad_rows[triangle_rows(layer, 5), :] += dot_nt(updated, grad_branch)
    grad_updated = dot(out_n[...], grad_branch)
    add_norm(g_norm, 2, grad_updated * z_hat, grad_updated)
    grad_z = normalize_back(grad_updated, norms[2], z_hat, z_scale)
    return (grad_middle, grad_out_gate, grad_z)


def add_norm(g_norm, index, gain_term, bias_term):
    for place, term in ((index, gain_term), (index + 1, bias_term)):
        total = term[:, :128]
        for part in range(1, PER):
            total = total + term[:, part * 128 : part * 128 + 128]
        g_norm[place] += total


def project_back_step(
    x, mask, grad_left, grad_right, grad_out_gate, grad_middle, five, five_n, norms, grads
):
    layer, grad_rows, g_norm = grads
    hat, scale = normalize(x)
    normed = (hat * norms[0] + norms[1]).astype(BF)
    projected = dot(five[: 4 * C, :], normed)
    pieces = []
    for grad, base in ((grad_left, 0), (grad_right, 2 * C)):
        sig = sigmoid(projected[base : base + C])
        masked = grad * mask * sig
        pieces.append((masked * projected[base + C : base + 2 * C] * (1.0 - sig)).astype(BF))
        pieces.append(masked.astype(BF))
    pieces.append(grad_out_gate)
    grad_projected = jnp.concatenate(pieces, axis=0)
    term = dot_nt(normed, grad_projected)
    for matrix in range(5):
        grad_rows[triangle_rows(layer, matrix), :] += term[:, matrix * C : matrix * C + C]
    grad_normed = dot(five_n[...], grad_projected)
    add_norm(g_norm, 0, grad_normed * hat, grad_normed)
    return grad_middle + normalize_back(grad_normed, norms[0], hat, scale)


class Norms:
    def __init__(self, ref, layer):
        self.ref, self.layer = ref, layer

    def __getitem__(self, index):
        value = self.ref[self.layer, index]
        return jnp.concatenate([value] * PER, axis=1)


def zero(*refs):
    for ref in refs:
        ref[...] = jnp.zeros_like(ref)


def exchange_start(rows, cols, send, recv, send_sem, recv_sem):
    row = lax.axis_index("row")
    col = lax.axis_index("col")
    me = row * cols + col
    recv[me] = send[me]

    def push(offset, carry):
        to_row = lax.rem(row + offset // cols, rows)
        to_col = lax.rem(col + lax.rem(offset, cols), cols)
        pltpu.make_async_remote_copy(
            send.at[to_row * cols + to_col], recv.at[me], send_sem, recv_sem, device_id=(to_row, to_col), device_id_type=MESH
        ).start()
        return carry

    lax.fori_loop(1, rows * cols, push, 0)


def exchange_wait(count, ref, sem):
    others = pl.ds(0, count - 1)
    pltpu.make_async_copy(ref.at[others], ref.at[others], sem).wait()


def join(recv, left, right, whole, send):
    assemble(recv, 0, left)
    assemble(recv, TILES, right)
    whole[...] = dot_nt(left[...], right[...]).astype(BF)
    disassemble(whole, send, 0)


def join_back(recv, left, right, whole, result, send):
    assemble(recv, 0, whole)
    result[...] = dot(whole[...], right[...]).astype(BF)
    disassemble(result, send, 0)
    result[...] = dot_tn(whole[...], left[...]).astype(BF)
    disassemble(result, send, TILES)


INPUTS = (
    "pair", "cotangent", "mask", "five", "five_n", "out_t", "out_n", "expand_t", "expand", "shrink_t", "shrink", "norms",
)
OUTPUTS = ("pair_out", "pair_grad", "total")
SCRATCH = {
    "x": ((LAYERS, CROPS, C, PAIRS), F32),
    "gate": ((LAYERS, CROPS, C, PAIRS), F32),
    "recv_ab": ((LAYERS, CROPS, C, 2 * TILES, 128), BF),
    "recv_z": ((LAYERS, CROPS, C, TILES, 128), BF),
    "recv_dz": ((LAYERS, CROPS, C, TILES, 128), BF),
    "recv_dab": ((LAYERS, CROPS, C, 2 * TILES, 128), BF),
    "send_wide": ((CROPS, C, 2 * TILES, 128), BF),
    "send_slim": ((CROPS, C, TILES, 128), BF),
    "left": ((LAYERS, CROPS, 512, 512), BF),
    "right": ((LAYERS, CROPS, 512, 512), BF),
    "mid": ((CROPS, C, PAIRS), F32),
    "out_gate": ((CROPS, C, PAIRS), BF),
    "cot": ((C, PAIRS), F32),
    "tiles_a": ((PAIRS, 128), F32),
    "tiles_b": ((PAIRS, 128), F32),
    "tiles_z": ((PAIRS, 128), F32),
    "tiles_d": ((PAIRS, 128), F32),
    "whole": ((512, 512), BF),
    "result": ((512, 512), BF),
    "grad_rows": ((2 * HALF, 128), F32),
    "g_norm": ((LAYERS, 6, C, 128), F32),
    "share": ((HALF, 128), BF),
    "sibling": ((HALF, 128), BF),
    "pieces": ((PIECES, PIECE, 128), BF),
    "landed": ((64, PIECE, 128), BF),
    "summed": ((PIECES, PIECE, 128), BF),
}


def window_kernel(rows, cols, *refs):
    names = INPUTS + OUTPUTS + tuple(SCRATCH)
    r = dict(zip(names, refs))
    send_sem, recv_sem, sum_sem = refs[len(names) :]
    count = rows * cols
    row = lax.axis_index("row")
    col = lax.axis_index("col")

    barrier = pltpu.get_barrier_semaphore()

    def greet(offset, carry):
        to = (lax.rem(row + offset // cols, rows), lax.rem(col + lax.rem(offset, cols), cols))
        pl.semaphore_signal(barrier, inc=1, device_id=to, device_id_type=MESH)
        return carry

    lax.fori_loop(1, count, greet, 0)

    in_flight = {}

    def free(kind, crop):
        if (kind, crop) in in_flight:
            exchange_wait(count, r[kind].at[crop], send_sem.at[in_flight.pop((kind, crop))])

    def begin(kind, crop, recv, index):
        in_flight[kind, crop] = index
        exchange_start(rows, cols, r[kind].at[crop], recv, send_sem.at[index], recv_sem.at[index])

    def project(layer, crop, step, x):
        project_step(
            x, r["mask"][crop, :, lanes_of(step)], r["five"].at[layer], Norms(r["norms"], layer), r["tiles_a"], r["tiles_b"],
            r["gate"].at[layer, crop], step,
        )

    def send_sides(layer, crop):
        free("send_wide", crop)
        pack_tiles(r["tiles_a"], r["send_wide"].at[crop], 0)
        pack_tiles(r["tiles_b"], r["send_wide"].at[crop], TILES)
        begin("send_wide", crop, r["recv_ab"].at[layer, crop], layer * 8 + crop)

    def update(layer, crop, step):
        lanes = lanes_of(step)
        gate = r["gate"][layer, crop, :, lanes]
        gains = Norms(r["norms"], layer)
        parts = update_step(
            r["x"][layer, crop, :, lanes], gate, gather_tiles(r["tiles_z"], step), r["out_t"].at[layer], r["expand_t"].at[layer], gains
        )
        return gate, gains, parts

    def back(layer, crop, step, upstream, gate, gains, parts, hidden_parts):
        lanes = lanes_of(step)
        grads = (layer, r["grad_rows"], r["g_norm"].at[layer])
        middle, out_gate, grad_z = back_step(
            upstream, parts, hidden_parts, gate, r["shrink"].at[layer], r["expand"].at[layer], r["out_n"].at[layer], gains, grads
        )
        r["mid"][crop, :, lanes] = middle
        r["out_gate"][crop, :, lanes] = out_gate
        scatter_tiles(r["tiles_d"], step, grad_z)

    def project_back(layer, crop, step):
        lanes = lanes_of(step)
        return project_back_step(
            r["x"][layer, crop, :, lanes], r["mask"][crop, :, lanes], gather_tiles(r["tiles_a"], step), gather_tiles(r["tiles_b"], step),
            r["out_gate"][crop, :, lanes], r["mid"][crop, :, lanes], r["five"].at[layer], r["five_n"].at[layer],
            Norms(r["norms"], layer), (layer, r["grad_rows"], r["g_norm"].at[layer]),
        )

    def send_grad_z(layer, crop):
        free("send_slim", crop)
        pack_tiles(r["tiles_d"], r["send_slim"].at[crop], 0)
        begin("send_slim", crop, r["recv_dz"].at[layer, crop], layer * 8 + 4 + crop)

    def each_step(body):
        def run(step, carry):
            body(step)
            return carry

        lax.fori_loop(0, CHUNKS, run, 0)

    zero(r["grad_rows"], r["g_norm"])
    for crop in range(CROPS):
        load_pairs(r["pair"].at[crop], r["x"].at[0, crop])
        each_step(lambda step: project(0, crop, step, r["x"][0, crop, :, lanes_of(step)]))
        if crop == 0:
            pl.semaphore_wait(barrier, count - 1)
        send_sides(0, crop)

    for layer in range(LAYERS):
        for crop in range(CROPS):
            recv = r["recv_ab"].at[layer, crop]
            exchange_wait(count, recv, recv_sem.at[layer * 8 + crop])
            free("send_slim", crop)
            join(recv, r["left"].at[layer, crop], r["right"].at[layer, crop], r["whole"], r["send_slim"].at[crop])
            begin("send_slim", crop, r["recv_z"].at[layer, crop], layer * 8 + 2 + crop)
        for crop in range(CROPS):
            recv = r["recv_z"].at[layer, crop]
            exchange_wait(count, recv, recv_sem.at[layer * 8 + 2 + crop])
            unpack_tiles(recv, 0, r["tiles_z"])
            if layer + 1 < LAYERS:

                def forward(step):
                    gate, gains, parts = update(layer, crop, step)
                    x_new = parts[4] + dot(r["shrink_t"][layer], swiglu(parts[-1])[2])
                    r["x"][layer + 1, crop, :, lanes_of(step)] = x_new
                    project(layer + 1, crop, step, x_new)

                each_step(forward)
                send_sides(layer + 1, crop)
            else:
                load_pairs(r["cotangent"].at[crop], r["cot"])

                def turn(step):
                    gate, gains, parts = update(layer, crop, step)
                    hidden_parts = swiglu(parts[-1])
                    store_pairs(parts[4] + dot(r["shrink_t"][layer], hidden_parts[2]), step, r["pair_out"].at[crop])
                    back(layer, crop, step, r["cot"][:, lanes_of(step)], gate, gains, parts, hidden_parts)

                each_step(turn)
                send_grad_z(layer, crop)

    for layer in reversed(range(LAYERS)):
        for crop in range(CROPS):
            recv = r["recv_dz"].at[layer, crop]
            exchange_wait(count, recv, recv_sem.at[layer * 8 + 4 + crop])
            free("send_wide", crop)
            join_back(
                recv, r["left"].at[layer, crop], r["right"].at[layer, crop], r["whole"], r["result"], r["send_wide"].at[crop]
            )
            begin("send_wide", crop, r["recv_dab"].at[layer, crop], layer * 8 + 6 + crop)
        for crop in range(CROPS):
            recv = r["recv_dab"].at[layer, crop]
            exchange_wait(count, recv, recv_sem.at[layer * 8 + 6 + crop])
            unpack_tiles(recv, 0, r["tiles_a"])
            unpack_tiles(recv, TILES, r["tiles_b"])
            if layer > 0:
                unpack_tiles(r["recv_z"].at[layer - 1, crop], 0, r["tiles_z"])

                def deep(step):
                    upstream = project_back(layer, crop, step)
                    gate, gains, parts = update(layer - 1, crop, step)
                    back(layer - 1, crop, step, upstream, gate, gains, parts, swiglu(parts[-1]))

                each_step(deep)
                send_grad_z(layer - 1, crop)
            else:
                each_step(lambda step: store_pairs(project_back(layer, crop, step), step, r["pair_grad"].at[crop]))
    for kind in ("send_wide", "send_slim"):
        for crop in range(CROPS):
            free(kind, crop)
    for layer in range(LAYERS):
        for index in range(6):
            place = NORM_ROW + layer * 6 + index
            r["grad_rows"][place : place + 1, :] = jnp.sum(r["g_norm"][layer, index].T, axis=0, keepdims=True)
    reduce_rows(rows, cols, r, sum_sem)


def reduce_rows(rows, cols, r, sem):
    row = lax.axis_index("row")
    col = lax.axis_index("col")
    core = lax.rem(row, 2)
    chip = (row // 2) * cols + col
    chips = rows * cols // 2
    other = (row + 1 - 2 * core, col)
    owner = chip < PIECES

    def device(index):
        return (index // cols) * 2 + core, lax.rem(index, cols)

    def swap(source, target, place):
        return pltpu.make_async_remote_copy(
            source, target, sem.at[place], sem.at[place + 1], device_id=other, device_id_type=MESH
        )

    def half(start):
        return pl.ds(pl.multiple_of(start, HALF), HALF)

    r["share"][...] = r["grad_rows"][half((1 - core) * HALF), :].astype(BF)
    first = swap(r["share"], r["sibling"], 0)
    first.start()
    first.wait()
    both = r["grad_rows"][half(core * HALF), :] + r["sibling"][...].astype(F32)
    r["pieces"][...] = both.astype(BF).reshape(PIECES, PIECE, 128)

    def push(step, carry):
        piece = lax.rem(chip + step, PIECES)

        @pl.when(piece != chip)
        def _():
            pltpu.make_async_remote_copy(
                r["pieces"].at[piece], r["landed"].at[chip], sem.at[2], sem.at[3], device_id=device(piece), device_id_type=MESH
            ).start()

        return carry

    lax.fori_loop(0, PIECES, push, 0)

    def wait(ref, count, place):
        some = ref.at[pl.ds(0, count)]
        pltpu.make_async_copy(some, some, sem.at[place]).wait()

    @pl.when(owner)
    def _():
        r["landed"][chip] = r["pieces"][chip]
        wait(r["pieces"], PIECES - 1, 2)
        wait(r["landed"], chips - 1, 3)

        def add(index, carry):
            return carry + r["landed"][index].astype(F32)

        r["summed"][chip] = lax.fori_loop(1, chips, add, r["landed"][0].astype(F32)).astype(BF)

        def spread(step, carry):
            pltpu.make_async_remote_copy(
                r["summed"].at[chip], r["summed"].at[chip], sem.at[4], sem.at[5], device_id=device(lax.rem(chip + step, chips)),
                device_id_type=MESH,
            ).start()
            return carry

        lax.fori_loop(1, chips, spread, 0)
        wait(r["landed"], chips - 1, 4)
        wait(r["summed"], PIECES - 1, 5)

    @pl.when(jnp.logical_not(owner))
    def _():
        wait(r["pieces"], PIECES, 2)
        wait(r["summed"], PIECES, 5)

    r["total"][core] = r["summed"][...].reshape(HALF, 128)
    last = swap(r["total"].at[core], r["total"].at[core], 6)
    last.start()
    last.wait()


def window(rows, cols, outs, *args):
    return pl.pallas_call(
        functools.partial(window_kernel, rows, cols),
        out_shape=[jax.ShapeDtypeStruct(shape, dtype) for shape, dtype in outs],
        in_specs=[pl.BlockSpec(memory_space=pltpu.VMEM)] * len(args),
        out_specs=[pl.BlockSpec(memory_space=pltpu.VMEM)] * len(outs),
        scratch_shapes=[pltpu.VMEM(shape, dtype) for shape, dtype in SCRATCH.values()]
        + [pltpu.SemaphoreType.DMA((8 * LAYERS,))] * 2
        + [pltpu.SemaphoreType.DMA((8,))],
        compiler_params=pltpu.CompilerParams(collective_id=1, has_side_effects=True, vmem_limit_bytes=VMEM_LIMIT),
        name="window",
    )(*args)


def adamw(gradient, weight, first, second, clip_factor, step_rate, decay_rate, outs):
    clipped = gradient * clip_factor
    moment = BETA_ONE * first + (1.0 - BETA_ONE) * clipped
    square = BETA_TWO * second + (1.0 - BETA_TWO) * clipped * clipped
    correct_one = 1.0 - BETA_ONE**STEP
    correct_two = 1.0 - BETA_TWO**STEP
    update = moment / correct_one / (jnp.sqrt(square / correct_two) + ADAM_EPS)
    renewed = weight - step_rate * (update + decay_rate * weight)
    for (ref, place), value in zip(outs, (moment, square, renewed, renewed)):
        ref[place] = value.astype(ref.dtype)


def settle_kernel(*refs):
    total = refs[0]
    ins = [refs[1 + 3 * kind : 4 + 3 * kind] for kind in range(4)]
    outs = [refs[13 + 4 * kind : 17 + 4 * kind] for kind in range(3)] + [refs[25:28]]
    norm_ref = refs[28]

    def square(step, carry):
        rows = total[step // (HALF // 336), pl.ds(pl.multiple_of(lax.rem(step, HALF // 336) * 336, 16), 336), :].astype(F32)
        return carry + jnp.sum((rows * rows).reshape(42, 8, 128), axis=0)

    squares = lax.fori_loop(0, 2 * HALF // 336, square, jnp.zeros((8, 128), F32))
    squares = jnp.sum(jnp.sum(squares, axis=1, keepdims=True), axis=0, keepdims=True)
    grad_norm = jnp.sqrt(squares)
    norm_ref[...] = grad_norm
    factor = jnp.minimum(1.0, CLIP / (grad_norm + 1e-06))

    def gradient(start, size):
        parts = []
        if start < HALF:
            parts.append(total[0, start : min(start + size, HALF), :])
        if start + size > HALF:
            parts.append(total[1, max(start - HALF, 0) : start + size - HALF, :])
        return (parts[0] if len(parts) == 1 else jnp.concatenate(parts, axis=0)).astype(F32)

    def run(kind, start, size, place, rate=RATE, decay=DECAY_RATE):
        values = [ref[place] for ref in ins[kind]]
        adamw(gradient(start, size), *values, factor, rate, decay, [(ref, place) for ref in outs[kind]])

    for layer in range(LAYERS):
        for matrix in range(6):
            run(0, (layer * 6 + matrix) * C, C, (layer, matrix))
        for matrix in range(2):
            for block in range(4):
                place = (layer, matrix, slice(None), slice(block * C, block * C + C))
                run(1, EXPAND_ROW + ((layer * 2 + matrix) * 4 + block) * C, C, place)
        for block in range(4):
            run(2, SHRINK_ROW + layer * HID + block * C, C, (layer, slice(block * C, block * C + C)))
    normed = gradient(NORM_ROW, 16)
    for layer in range(LAYERS):
        values = [ref[layer] for ref in ins[3]]
        rows = normed[layer * 6 : layer * 6 + 6]
        adamw(rows, *values, factor, NORM_RATE, 0.0, [(ref, layer) for ref in outs[3]])


def settle(total, kinds):
    shapes = [jax.ShapeDtypeStruct(kind[0].shape, dtype) for kind in kinds[:3] for dtype in (F32, F32, F32, BF)]
    shapes += [jax.ShapeDtypeStruct(kinds[3][0].shape, F32)] * 3 + [jax.ShapeDtypeStruct((1, 1), F32)]
    args = [total] + [array for kind in kinds for array in kind]
    return pl.pallas_call(
        settle_kernel,
        out_shape=shapes,
        in_specs=[pl.BlockSpec(memory_space=pltpu.VMEM)] * len(args),
        out_specs=[pl.BlockSpec(memory_space=pltpu.VMEM)] * len(shapes),
        compiler_params=pltpu.CompilerParams(vmem_limit_bytes=VMEM_LIMIT),
        name="settle",
    )(*args)


def local(
    rows, cols,
    pair_in, lengths, pair_cotangent, triangle_weights, expand_weights, shrink_weights, norm_params, triangle_first,
    triangle_second, expand_first, expand_second, shrink_first, shrink_second, norm_first, norm_second,
):
    rows_dev, cols_dev = pair_in.shape[1], pair_in.shape[2]
    row_ids = lax.axis_index("row") * rows_dev + jnp.arange(rows_dev)
    col_ids = lax.axis_index("col") * cols_dev + jnp.arange(cols_dev)
    valid_rows = row_ids[None, :] < lengths[:, None]
    valid_cols = col_ids[None, :] < lengths[:, None]
    mask = (valid_rows[:, :, None] & valid_cols[:, None, :]).astype(F32)
    mask = mask.reshape(CROPS, 2, TILES, cols_dev).transpose(0, 2, 1, 3).reshape(CROPS, 1, PAIRS)

    triangle_low = triangle_weights.astype(BF)
    expand_low = expand_weights.astype(BF)
    shrink = shrink_weights.astype(BF)
    turned = jnp.swapaxes(triangle_low, 2, 3)
    five = turned[:, :5].reshape(LAYERS, 5 * C, C)
    out_t = turned[:, 5]
    five_n = jnp.moveaxis(triangle_low[:, :5], 1, 2).reshape(LAYERS, C, 5 * C)
    out_n = triangle_low[:, 5]
    expand_t = jnp.swapaxes(expand_low, 2, 3).reshape(LAYERS, 2 * HID, C)
    expand = jnp.moveaxis(expand_low, 1, 2).reshape(LAYERS, C, 2 * HID)
    shrink_t = jnp.swapaxes(shrink, 1, 2)
    norms = jnp.broadcast_to(norm_params[..., None], norm_params.shape + (128,))

    outs = [(pair_in.shape, BF), (pair_in.shape, F32), ((2, HALF, 128), BF)]
    pair_out, pair_grad, total = window(
        rows, cols, outs, pair_in, pair_cotangent, mask, five, five_n, out_t, out_n, expand_t, expand, shrink_t, shrink, norms
    )
    kinds = (
        (triangle_weights, triangle_first, triangle_second),
        (expand_weights, expand_first, expand_second),
        (shrink_weights, shrink_first, shrink_second),
        (norm_params, norm_first, norm_second),
    )
    new = settle(total, kinds)
    moments = [new[4 * kind + place] for kind in range(3) for place in range(3)]
    copies = [new[4 * kind + 3] for kind in range(3)]
    return (pair_out, pair_grad, *moments, *new[12:15], *copies, new[15].reshape(()))


def solution(mesh):
    pair = P(None, "row", "col", None)
    return jax.shard_map(
        functools.partial(local, mesh.shape["row"], mesh.shape["col"]),
        mesh=mesh,
        in_specs=(pair, P(), pair) + (P(),) * 12,
        out_specs=(pair, pair) + (P(),) * 16,
        check_vma=False,
    )
```

```python
import jax
import jax.numpy as jnp
from jax import lax
from jax.experimental import pallas as pl
from jax.experimental.pallas import tpu as pltpu
from jax.sharding import PartitionSpec as P

LAYERS = 2
STEP = 10
CROPS = 2
COLS = 8
DEVICES = 128

EPS_NORM = 1e-05
BETA_ONE = 0.9
BETA_TWO = 0.999
ADAM_EPS = 1e-08
RATE = 0.1
NORM_RATE = 0.5
DECAY_RATE = 0.01
CLIP = 1.0

MESH = pl.DeviceIdType.MESH
BF = jnp.bfloat16
F32 = jnp.float32

C = 128
HID = 512
TILES = 16
PAIRS = 2048
WIDE = 1024
CHUNKS = PAIRS // WIDE
PER = WIDE // 128
VMEM_LIMIT = 60 << 20

EXPAND_ROW = LAYERS * 6 * C
SHRINK_ROW = EXPAND_ROW + LAYERS * 2 * HID
NORM_ROW = SHRINK_ROW + LAYERS * HID
PIECE = 48
PIECES = 49
HALF = PIECE * PIECES


def triangle_rows(layer, matrix):
    return pl.ds((layer * 6 + matrix) * C, C)


def expand_rows(layer, matrix, block):
    return pl.ds(EXPAND_ROW + ((layer * 2 + matrix) * 4 + block) * C, C)


def shrink_rows(layer):
    return pl.ds(SHRINK_ROW + layer * HID, HID)


def dot(left, right):
    return lax.dot_general(left, right, (((1,), (0,)), ((), ())), preferred_element_type=F32)


def dot_nt(left, right):
    return lax.dot_general(left, right, (((1,), (1,)), ((), ())), preferred_element_type=F32)


def dot_tn(left, right):
    return lax.dot_general(left, right, (((0,), (0,)), ((), ())), preferred_element_type=F32)


def sigmoid(v):
    return 0.5 * jnp.tanh(0.5 * v) + 0.5


def mean_rows(v):
    return jnp.sum(v, axis=0, keepdims=True) * (1.0 / C)


def normalize(v):
    centered = v - mean_rows(v)
    scale = lax.rsqrt(mean_rows(centered * centered) + EPS_NORM)
    return centered * scale, scale


def normalize_back(grad, gain, hat, scale):
    grad_hat = grad * gain
    return scale * (grad_hat - mean_rows(grad_hat) - hat * mean_rows(grad_hat * hat))


def lanes_of(step):
    return pl.ds(pl.multiple_of(step * WIDE, WIDE), WIDE)


def scatter_tiles(scratch, step, value):
    for part in range(PER):
        scratch[pl.ds(step * PER + part, C, stride=TILES), :] = value[:, part * 128 : part * 128 + 128]


def gather_tiles(scratch, step):
    return jnp.concatenate(
        [scratch[pl.ds(step * PER + part, C, stride=TILES), :] for part in range(PER)], axis=1
    )


def pack_tiles(scratch, send, offset):
    send[:, offset : offset + TILES, :] = scratch[...].astype(BF).reshape(C, TILES, 128)


def unpack_tiles(recv, offset, scratch):
    scratch[...] = recv[:, offset : offset + TILES, :].reshape(PAIRS, 128).astype(F32)


def swap_halves(first, second):
    low = jnp.concatenate([first[:, :64], second[:, :64]], axis=1)
    high = jnp.concatenate([first[:, 64:], second[:, 64:]], axis=1)
    return low, high


def assemble(recv, offset, whole):
    for row in range(16):
        base = row * 32
        for pair in range(4):
            low, high = swap_halves(
                recv[row * 8 + 2 * pair, offset : offset + TILES, :],
                recv[row * 8 + 2 * pair + 1, offset : offset + TILES, :],
            )
            whole[base : base + 16, pair * 128 : pair * 128 + 128] = low
            whole[base + 16 : base + 32, pair * 128 : pair * 128 + 128] = high


def disassemble(whole, send, offset):
    for row in range(16):
        base = row * 32
        for pair in range(4):
            first, second = swap_halves(
                whole[base : base + 16, pair * 128 : pair * 128 + 128],
                whole[base + 16 : base + 32, pair * 128 : pair * 128 + 128],
            )
            send[row * 8 + 2 * pair, offset : offset + TILES, :] = first
            send[row * 8 + 2 * pair + 1, offset : offset + TILES, :] = second


def load_pairs(pair_ref, step):
    parts = []
    for part in range(PER):
        tile = step * PER + part
        parts.append(jnp.concatenate([pair_ref[tile], pair_ref[tile + TILES]], axis=0).astype(F32).T)
    return jnp.concatenate(parts, axis=1)


def store_pairs(value, step, out_ref):
    for part in range(PER):
        rows = value[:, part * 128 : part * 128 + 128].T
        out_ref[step * PER + part] = rows[:64].astype(out_ref.dtype)
        out_ref[step * PER + part + TILES] = rows[64:].astype(out_ref.dtype)


def project_step(x, mask, five, norms, scratch_a, scratch_b, gate_ref, step):
    hat, _ = normalize(x)
    normed = (hat * norms[0] + norms[1]).astype(BF)
    projected = dot(five[...], normed)
    left = mask * sigmoid(projected[:C]) * projected[C : 2 * C]
    right = mask * sigmoid(projected[2 * C : 3 * C]) * projected[3 * C : 4 * C]
    scatter_tiles(scratch_a, step, left)
    scatter_tiles(scratch_b, step, right)
    gate_ref[:, lanes_of(step)] = sigmoid(projected[4 * C :])


def update_step(x, gate, z, out_t, expand_t, norms):
    z_hat, z_scale = normalize(z)
    updated = (z_hat * norms[2] + norms[3]).astype(BF)
    branch = dot(out_t[...], updated)
    middle = x + gate * branch
    mid_hat, mid_scale = normalize(middle)
    normed = (mid_hat * norms[4] + norms[5]).astype(BF)
    gate_up = dot(expand_t[...], normed)
    return (z_hat, z_scale, updated, branch, middle, mid_hat, mid_scale, normed, gate_up)


def swiglu(gate_up):
    gate_half = gate_up[:HID]
    sig = sigmoid(gate_half)
    silu = gate_half * sig
    return (sig, silu, (silu * gate_up[HID:]).astype(BF))


def back_step(upstream, parts, hidden_parts, gate, shrink, expand, out_n, norms, grads):
    z_hat, z_scale, updated, branch, middle, mid_hat, mid_scale, normed, gate_up = parts
    sig, silu, hidden = hidden_parts
    layer, grad_rows, g_norm = grads
    upstream_low = upstream.astype(BF)
    grad_rows[shrink_rows(layer), :] += dot_nt(hidden, upstream_low)
    grad_hidden = dot(shrink[...], upstream_low)
    grad_gate = (grad_hidden * gate_up[HID:] * (sig + silu * (1.0 - sig))).astype(BF)
    grad_up = (grad_hidden * silu).astype(BF)
    grad_gate_up = jnp.concatenate([grad_gate, grad_up], axis=0)
    term = dot_nt(normed, grad_gate_up)
    for block in range(8):
        grad_rows[expand_rows(layer, block // 4, block % 4), :] += term[:, block * C : block * C + C]
    grad_normed = dot(expand[...], grad_gate_up)
    add_norm(g_norm, 4, grad_normed * mid_hat, grad_normed)
    grad_middle = upstream + normalize_back(grad_normed, norms[4], mid_hat, mid_scale)
    scaled = grad_middle * gate
    grad_branch = scaled.astype(BF)
    grad_out_gate = (scaled * branch * (1.0 - gate)).astype(BF)
    grad_rows[triangle_rows(layer, 5), :] += dot_nt(updated, grad_branch)
    grad_updated = dot(out_n[...], grad_branch)
    add_norm(g_norm, 2, grad_updated * z_hat, grad_updated)
    grad_z = normalize_back(grad_updated, norms[2], z_hat, z_scale)
    return (grad_middle, grad_out_gate, grad_z)


def add_norm(g_norm, index, gain_term, bias_term):
    for place, term in ((index, gain_term), (index + 1, bias_term)):
        total = term[:, :128]
        for part in range(1, PER):
            total = total + term[:, part * 128 : part * 128 + 128]
        g_norm[place] += total


def project_back_step(
    x, mask, grad_left, grad_right, grad_out_gate, grad_middle, five, five_n, norms, grads
):
    layer, grad_rows, g_norm = grads
    hat, scale = normalize(x)
    normed = (hat * norms[0] + norms[1]).astype(BF)
    projected = dot(five[: 4 * C, :], normed)
    pieces = []
    for grad, base in ((grad_left, 0), (grad_right, 2 * C)):
        sig = sigmoid(projected[base : base + C])
        masked = grad * mask * sig
        pieces.append((masked * projected[base + C : base + 2 * C] * (1.0 - sig)).astype(BF))
        pieces.append(masked.astype(BF))
    pieces.append(grad_out_gate)
    grad_projected = jnp.concatenate(pieces, axis=0)
    term = dot_nt(normed, grad_projected)
    for matrix in range(5):
        grad_rows[triangle_rows(layer, matrix), :] += term[:, matrix * C : matrix * C + C]
    grad_normed = dot(five_n[...], grad_projected)
    add_norm(g_norm, 0, grad_normed * hat, grad_normed)
    return grad_middle + normalize_back(grad_normed, norms[0], hat, scale)


class Norms:
    def __init__(self, ref, layer):
        self.ref, self.layer = ref, layer

    def __getitem__(self, index):
        value = self.ref[self.layer, index]
        return jnp.concatenate([value] * PER, axis=1)


def zero(*refs):
    for ref in refs:
        ref[...] = jnp.zeros_like(ref)


def distance(offset):
    return sum(min(step, 4 - step) for step in offset[:3])


OFFSETS = [(i % 4, i // 4 % 4, i // 16 % 4, i // 64) for i in range(1, 128)]
OFFSETS = [o for _, _, o in sorted((-distance(o), (i * 53 + 17) % 127, o) for i, o in enumerate(OFFSETS))]


class Place:
    def __init__(self):
        self.row, self.col = lax.axis_index("row"), lax.axis_index("col")
        self.me = self.row * COLS + self.col
        self.core = lax.rem(self.row, 2)
        x, y, z = lax.rem(self.row // 2, 4), self.row // 8 * 2 + lax.rem(self.col, 2), self.col // 2
        self.chip = self.row // 2 * COLS + self.col
        xs = [lax.rem(x + step, 4) * 2 for step in range(4)]
        ys = [lax.rem(y + step, 4) for step in range(4)]
        zs = [lax.rem(z + step, 4) * 2 for step in range(4)]
        cores = [self.core, 1 - self.core]
        highs, lows = [v // 2 * 8 for v in ys], [lax.rem(v, 2) for v in ys]
        self.rows = {(a, b, d): highs[b] + xs[a] + cores[d] for a in range(4) for b in range(4) for d in range(2)}
        self.cols = {(b, c): zs[c] + lows[b] for b in range(4) for c in range(4)}

    def at(self, offset):
        a, b, c, d = offset
        return self.rows[a, b, d], self.cols[b, c]


def exchange_start(place, send, recv, send_sem, recv_sem):
    for offset in OFFSETS:
        row, col = place.at(offset)
        pltpu.make_async_remote_copy(
            send.at[row * COLS + col], recv.at[place.me], send_sem, recv_sem, device_id=(row, col), device_id_type=MESH
        ).start()
    recv[place.me] = send[place.me]


def exchange_wait(ref, sem):
    others = pl.ds(0, DEVICES - 1)
    pltpu.make_async_copy(ref.at[others], ref.at[others], sem).wait()


def join(recv, left, right, whole, send):
    assemble(recv, 0, left)
    assemble(recv, TILES, right)
    whole[...] = dot_nt(left[...], right[...]).astype(BF)
    disassemble(whole, send, 0)


def join_back(recv, left, right, whole, result, send):
    assemble(recv, 0, whole)
    result[...] = dot(whole[...], right[...]).astype(BF)
    disassemble(result, send, 0)
    result[...] = dot_tn(whole[...], left[...]).astype(BF)
    disassemble(result, send, TILES)


INPUTS = ("lengths", "pair", "cotangent", "triangle", "expand_in", "shrink_in", "norms_in")
OUTPUTS = ("pair_out", "pair_grad", "total")
SCRATCH = {
    "mask": ((CROPS, 1, PAIRS), F32),
    "norms": ((LAYERS, 6, C, 128), F32),
    "five": ((LAYERS, 5 * C, C), BF),
    "five_n": ((LAYERS, C, 5 * C), BF),
    "out_t": ((LAYERS, C, C), BF),
    "out_n": ((LAYERS, C, C), BF),
    "expand_t": ((LAYERS, 2 * HID, C), BF),
    "expand": ((LAYERS, C, 2 * HID), BF),
    "shrink_t": ((LAYERS, C, HID), BF),
    "shrink": ((LAYERS, HID, C), BF),
    "x": ((LAYERS, CROPS, C, PAIRS), F32),
    "gate": ((LAYERS, CROPS, C, PAIRS), F32),
    "recv_ab": ((LAYERS, CROPS, C, 2 * TILES, 128), BF),
    "recv_z": ((LAYERS, CROPS, C, TILES, 128), BF),
    "recv_dz": ((LAYERS, CROPS, C, TILES, 128), BF),
    "send_wide": ((CROPS, C, 2 * TILES, 128), BF),
    "send_slim": ((CROPS, C, TILES, 128), BF),
    "left": ((LAYERS, CROPS, 512, 512), BF),
    "right": ((LAYERS, CROPS, 512, 512), BF),
    "mid": ((CROPS, C, PAIRS), F32),
    "out_gate": ((CROPS, C, PAIRS), BF),
    "tiles_a": ((PAIRS, 128), F32),
    "tiles_b": ((PAIRS, 128), F32),
    "tiles_z": ((PAIRS, 128), F32),
    "whole": ((512, 512), BF),
    "result": ((512, 512), BF),
    "grad_rows": ((2 * HALF, 128), F32),
    "g_norm": ((LAYERS, 6, C, 128), F32),
    "share": ((HALF, 128), BF),
    "sibling": ((HALF, 128), BF),
    "pieces": ((PIECES, PIECE, 128), BF),
    "landed": ((64, PIECE, 128), BF),
    "summed": ((PIECES, PIECE, 128), BF),
}


def prepare_triangle(r, layer):
    for index in range(6):
        row = r["norms_in"][index, layer : layer + 1, :]
        r["norms"][layer, index] = jnp.broadcast_to(row, (C, C)).T
    for matrix in range(5):
        weight = r["triangle"][layer, matrix]
        r["five"][layer, matrix * C : matrix * C + C, :] = weight.T.astype(BF)
        r["five_n"][layer, :, matrix * C : matrix * C + C] = weight.astype(BF)
    r["out_t"][layer] = r["triangle"][layer, 5].T.astype(BF)
    r["out_n"][layer] = r["triangle"][layer, 5].astype(BF)


def prepare_transition(r, layer):
    for matrix in range(2):
        for block in range(4):
            lanes = slice(block * C, block * C + C)
            rows = slice(matrix * HID + block * C, matrix * HID + block * C + C)
            weight = r["expand_in"][layer, matrix, :, lanes]
            r["expand_t"][layer, rows, :] = weight.T.astype(BF)
            r["expand"][layer, :, rows] = weight.astype(BF)
    for block in range(4):
        rows = slice(block * C, block * C + C)
        weight = r["shrink_in"][layer, rows, :]
        r["shrink_t"][layer, :, rows] = weight.T.astype(BF)
        r["shrink"][layer, rows, :] = weight.astype(BF)


def prepare_mask(r, place):
    pair = lax.broadcasted_iota(jnp.int32, (1, PAIRS), 1)
    tile, lane = pair // 128, lax.rem(pair, 128)
    first = place.row * 32 + lane // 64 * TILES + tile
    second = place.col * 64 + lax.rem(lane, 64)
    last = jnp.maximum(first, second)
    for crop in range(CROPS):
        r["mask"][crop] = jnp.clip(r["lengths"][crop] - last, 0, 1).astype(F32)


def for_crops(visit):
    def run(crop, carry):
        visit(crop)
        return carry

    lax.fori_loop(0, CROPS, run, 0)


def for_steps(visit):
    def run(step, carry):
        visit(step)
        return carry

    lax.fori_loop(0, CHUNKS, run, 0)


def window_kernel(*refs):
    names = INPUTS + OUTPUTS + tuple(SCRATCH)
    r = dict(zip(names, refs))
    send_sem, recv_sem, sum_sem = refs[len(names) :]
    place = Place()

    barrier = pltpu.get_barrier_semaphore()
    for offset in OFFSETS:
        pl.semaphore_signal(barrier, inc=1, device_id=place.at(offset), device_id_type=MESH)

    in_flight = {}

    def free(kind, crop):
        if kind in in_flight:
            exchange_wait(r[kind].at[crop], send_sem.at[in_flight[kind] + crop])

    def begin(kind, crop, recv, index):
        exchange_start(place, r[kind].at[crop], recv, send_sem.at[index + crop], recv_sem.at[index + crop])

    def project(layer, crop, step, x):
        project_step(
            x, r["mask"][crop, :, lanes_of(step)], r["five"].at[layer], Norms(r["norms"], layer), r["tiles_a"], r["tiles_b"],
            r["gate"].at[layer, crop], step,
        )

    def send_sides(layer, crop):
        free("send_wide", crop)
        pack_tiles(r["tiles_a"], r["send_wide"].at[crop], 0)
        pack_tiles(r["tiles_b"], r["send_wide"].at[crop], TILES)
        begin("send_wide", crop, r["recv_ab"].at[layer, crop], layer * 8)

    def update(layer, crop, step):
        lanes = lanes_of(step)
        gate = r["gate"][layer, crop, :, lanes]
        gains = Norms(r["norms"], layer)
        parts = update_step(
            r["x"][layer, crop, :, lanes], gate, gather_tiles(r["tiles_z"], step), r["out_t"].at[layer], r["expand_t"].at[layer], gains
        )
        return gate, gains, parts

    def back(layer, crop, step, upstream, gate, gains, parts, hidden_parts):
        lanes = lanes_of(step)
        grads = (layer, r["grad_rows"], r["g_norm"].at[layer])
        middle, out_gate, grad_z = back_step(
            upstream, parts, hidden_parts, gate, r["shrink"].at[layer], r["expand"].at[layer], r["out_n"].at[layer], gains, grads
        )
        r["mid"][crop, :, lanes] = middle
        r["out_gate"][crop, :, lanes] = out_gate
        scatter_tiles(r["tiles_z"], step, grad_z)

    def project_back(layer, crop, step):
        lanes = lanes_of(step)
        return project_back_step(
            r["x"][layer, crop, :, lanes], r["mask"][crop, :, lanes], gather_tiles(r["tiles_a"], step), gather_tiles(r["tiles_b"], step),
            r["out_gate"][crop, :, lanes], r["mid"][crop, :, lanes], r["five"].at[layer], r["five_n"].at[layer],
            Norms(r["norms"], layer), (layer, r["grad_rows"], r["g_norm"].at[layer]),
        )

    def send_grad_z(layer, crop):
        free("send_slim", crop)
        pack_tiles(r["tiles_z"], r["send_slim"].at[crop], 0)
        begin("send_slim", crop, r["recv_dz"].at[layer, crop], layer * 8 + 4)

    prepare_mask(r, place)
    prepare_triangle(r, 0)

    def first(crop):
        def steps(step):
            x = load_pairs(r["pair"].at[crop], step)
            r["x"][0, crop, :, lanes_of(step)] = x
            project(0, crop, step, x)

        for_steps(steps)

        @pl.when(crop == 0)
        def _():
            pl.semaphore_wait(barrier, DEVICES - 1)

        send_sides(0, crop)

    for_crops(first)
    in_flight["send_wide"] = 0
    prepare_transition(r, 0)
    for layer in range(1, LAYERS):
        prepare_triangle(r, layer)
        prepare_transition(r, layer)
    zero(r["grad_rows"], r["g_norm"])

    for layer in range(LAYERS):

        def products(crop):
            recv = r["recv_ab"].at[layer, crop]
            exchange_wait(recv, recv_sem.at[layer * 8 + crop])
            free("send_slim", crop)
            join(recv, r["left"].at[layer, crop], r["right"].at[layer, crop], r["whole"], r["send_slim"].at[crop])
            begin("send_slim", crop, r["recv_z"].at[layer, crop], layer * 8 + 2)

        for_crops(products)
        in_flight["send_slim"] = layer * 8 + 2

        def onward(crop):
            recv = r["recv_z"].at[layer, crop]
            exchange_wait(recv, recv_sem.at[layer * 8 + 2 + crop])
            unpack_tiles(recv, 0, r["tiles_z"])

            def forward(step):
                gate, gains, parts = update(layer, crop, step)
                x_new = parts[4] + dot(r["shrink_t"][layer], swiglu(parts[-1])[2])
                r["x"][layer + 1, crop, :, lanes_of(step)] = x_new
                project(layer + 1, crop, step, x_new)

            def turn(step):
                gate, gains, parts = update(layer, crop, step)
                hidden_parts = swiglu(parts[-1])
                store_pairs(parts[4] + dot(r["shrink_t"][layer], hidden_parts[2]), step, r["pair_out"].at[crop])
                back(layer, crop, step, load_pairs(r["cotangent"].at[crop], step), gate, gains, parts, hidden_parts)

            if layer + 1 < LAYERS:
                for_steps(forward)
                send_sides(layer + 1, crop)
            else:
                for_steps(turn)
                send_grad_z(layer, crop)

        for_crops(onward)
        in_flight.update({"send_wide": layer * 8 + 8} if layer + 1 < LAYERS else {"send_slim": layer * 8 + 4})

    for layer in reversed(range(LAYERS)):

        def products_back(crop):
            recv = r["recv_dz"].at[layer, crop]
            exchange_wait(recv, recv_sem.at[layer * 8 + 4 + crop])
            free("send_wide", crop)
            join_back(
                recv, r["left"].at[layer, crop], r["right"].at[layer, crop], r["whole"], r["result"], r["send_wide"].at[crop]
            )
            begin("send_wide", crop, r["recv_ab"].at[layer, crop], layer * 8 + 6)

        for_crops(products_back)
        in_flight["send_wide"] = layer * 8 + 6

        def backward(crop):
            recv = r["recv_ab"].at[layer, crop]
            exchange_wait(recv, recv_sem.at[layer * 8 + 6 + crop])
            unpack_tiles(recv, 0, r["tiles_a"])
            unpack_tiles(recv, TILES, r["tiles_b"])

            def deep(step):
                upstream = project_back(layer, crop, step)
                gate, gains, parts = update(layer - 1, crop, step)
                back(layer - 1, crop, step, upstream, gate, gains, parts, swiglu(parts[-1]))

            if layer > 0:
                unpack_tiles(r["recv_z"].at[layer - 1, crop], 0, r["tiles_z"])
                for_steps(deep)
                send_grad_z(layer - 1, crop)
            else:
                for_steps(lambda step: store_pairs(project_back(layer, crop, step), step, r["pair_grad"].at[crop]))

        for_crops(backward)
        if layer > 0:
            in_flight["send_slim"] = layer * 8 - 4
    for_crops(lambda crop: free("send_wide", crop))
    for_crops(lambda crop: free("send_slim", crop))
    for layer in range(LAYERS):
        for index in range(6):
            row = NORM_ROW + index * LAYERS + layer
            r["grad_rows"][row : row + 1, :] = jnp.sum(r["g_norm"][layer, index].T, axis=0, keepdims=True)
    reduce_rows(place, r, sum_sem)


def reduce_rows(place, r, sem):
    core, chip, chips = place.core, place.chip, DEVICES // 2
    owner = chip < PIECES
    offsets = [offset for offset in OFFSETS if offset[3] == 0]

    def chip_at(offset):
        row, col = place.at(offset)
        return row // 2 * COLS + col

    def swap(source, target, index):
        return pltpu.make_async_remote_copy(
            source, target, sem.at[index], sem.at[index + 1], device_id=place.at((0, 0, 0, 1)), device_id_type=MESH
        )

    def half(start):
        return pl.ds(pl.multiple_of(start, HALF), HALF)

    r["share"][...] = r["grad_rows"][half((1 - core) * HALF), :].astype(BF)
    first = swap(r["share"], r["sibling"], 0)
    first.start()
    first.wait()
    both = r["grad_rows"][half(core * HALF), :] + r["sibling"][...].astype(F32)
    r["pieces"][...] = both.astype(BF).reshape(PIECES, PIECE, 128)

    for offset in offsets:
        piece = chip_at(offset)

        @pl.when(piece < PIECES)
        def _():
            pltpu.make_async_remote_copy(
                r["pieces"].at[piece], r["landed"].at[chip], sem.at[2], sem.at[3], device_id=place.at(offset), device_id_type=MESH
            ).start()

    def wait(ref, count, index):
        some = ref.at[pl.ds(0, count)]
        pltpu.make_async_copy(some, some, sem.at[index]).wait()

    @pl.when(owner)
    def _():
        r["landed"][chip] = r["pieces"][chip]
        wait(r["pieces"], PIECES - 1, 2)
        wait(r["landed"], chips - 1, 3)

        def add(index, carry):
            return carry + r["landed"][index].astype(F32)

        r["summed"][chip] = lax.fori_loop(1, chips, add, r["landed"][0].astype(F32)).astype(BF)

        for offset in offsets:
            pltpu.make_async_remote_copy(
                r["summed"].at[chip], r["summed"].at[chip], sem.at[4], sem.at[5], device_id=place.at(offset), device_id_type=MESH
            ).start()
        wait(r["landed"], chips - 1, 4)
        wait(r["summed"], PIECES - 1, 5)

    @pl.when(jnp.logical_not(owner))
    def _():
        wait(r["pieces"], PIECES, 2)
        wait(r["summed"], PIECES, 5)

    own = half(core * HALF)
    r["total"][own, :] = r["summed"][...].reshape(HALF, 128)
    last = swap(r["total"].at[own], r["total"].at[own], 6)
    last.start()
    last.wait()


def window(outs, lengths, *args):
    return pl.pallas_call(
        window_kernel,
        out_shape=[jax.ShapeDtypeStruct(shape, dtype) for shape, dtype in outs],
        in_specs=[pl.BlockSpec(memory_space=pltpu.SMEM)] + [pl.BlockSpec(memory_space=pltpu.VMEM)] * len(args),
        out_specs=[pl.BlockSpec(memory_space=pltpu.VMEM)] * len(outs),
        scratch_shapes=[pltpu.VMEM(shape, dtype) for shape, dtype in SCRATCH.values()]
        + [pltpu.SemaphoreType.DMA((8 * LAYERS,))] * 2
        + [pltpu.SemaphoreType.DMA((8,))],
        compiler_params=pltpu.CompilerParams(collective_id=1, has_side_effects=True, vmem_limit_bytes=VMEM_LIMIT),
        name="window",
    )(lengths, *args)


def adamw(gradient, weight, first, second, clip_factor, step_rate, decay_rate, outs):
    clipped = gradient * clip_factor
    moment = BETA_ONE * first + (1.0 - BETA_ONE) * clipped
    square = BETA_TWO * second + (1.0 - BETA_TWO) * clipped * clipped
    correct_one = 1.0 - BETA_ONE**STEP
    correct_two = 1.0 - BETA_TWO**STEP
    update = moment / correct_one / (jnp.sqrt(square / correct_two) + ADAM_EPS)
    renewed = weight - step_rate * (update + decay_rate * weight)
    for (ref, place), value in zip(outs, (moment, square, renewed, renewed)):
        ref[place] = value.astype(ref.dtype)


def settle_kernel(*refs):
    total = refs[0]
    ins = [refs[1 + 3 * kind : 4 + 3 * kind] for kind in range(4)]
    outs = [refs[13 + 4 * kind : 17 + 4 * kind] for kind in range(3)] + [refs[25:28]]
    norm_ref, factor_ref = refs[28:]
    layer, part = pl.program_id(0), pl.program_id(1)

    def gradient(start, size):
        return total[pl.ds(pl.multiple_of(start, 64), size), :].astype(F32)

    @pl.when(layer + part == 0)
    def _():
        def square(step, carry):
            rows = total[pl.ds(pl.multiple_of(step * 672, 16), 672), :].astype(F32)
            return carry + jnp.sum((rows * rows).reshape(84, 8, 128), axis=0)

        squares = lax.fori_loop(0, 2 * HALF // 672, square, jnp.zeros((8, 128), F32))
        grad_norm = jnp.sqrt(jnp.sum(jnp.sum(squares, axis=1, keepdims=True), axis=0, keepdims=True))
        norm_ref[...] = grad_norm
        factor_ref[...] = jnp.minimum(1.0, CLIP / (grad_norm + 1e-06))
        rows = total[NORM_ROW : NORM_ROW + 16, :].astype(F32)
        for index in range(6):
            values = [ref[index] for ref in ins[3]]
            outputs = [(ref, index) for ref in outs[3]]
            adamw(rows[index * LAYERS : index * LAYERS + LAYERS], *values, factor_ref[...], NORM_RATE, 0.0, outputs)

    factor = factor_ref[...]

    def run(kind, start, size, place):
        values = [ref[place] for ref in ins[kind]]
        adamw(gradient(start, size), *values, factor, RATE, DECAY_RATE, [(ref, place) for ref in outs[kind]])

    for matrix in range(3):
        run(0, (layer * 6 + part * 3 + matrix) * C, C, (0, matrix))
    for block in range(4):
        place = (0, 0, slice(None), slice(block * C, block * C + C))
        run(1, EXPAND_ROW + ((layer * 2 + part) * 4 + block) * C, C, place)
        run(2, SHRINK_ROW + layer * HID + part * 256 + block * 64, 64, (0, slice(block * 64, block * 64 + 64)))


def settle(total, kinds):
    blocks = [
        pl.BlockSpec((1, 3, C, C), lambda layer, part: (layer, part, 0, 0)),
        pl.BlockSpec((1, 1, C, HID), lambda layer, part: (layer, part, 0, 0)),
        pl.BlockSpec((1, HID // 2, C), lambda layer, part: (layer, part, 0)),
        pl.BlockSpec((6, LAYERS, C), lambda layer, part: (0, 0, 0)),
    ]
    shapes, out_specs = [], []
    for kind, block in zip(kinds, blocks):
        for dtype in (F32, F32, F32, BF)[: 3 if block is blocks[3] else 4]:
            shapes.append(jax.ShapeDtypeStruct(kind[0].shape, dtype))
            out_specs.append(block)
    shapes.append(jax.ShapeDtypeStruct((1, 1), F32))
    out_specs.append(pl.BlockSpec((1, 1), lambda layer, part: (0, 0)))
    return pl.pallas_call(
        settle_kernel,
        grid=(LAYERS, 2),
        out_shape=shapes,
        in_specs=[pl.BlockSpec(total.shape, lambda layer, part: (0, 0))] + [block for block in blocks for _ in range(3)],
        out_specs=out_specs,
        scratch_shapes=[pltpu.VMEM((1, 1), F32)],
        compiler_params=pltpu.CompilerParams(vmem_limit_bytes=VMEM_LIMIT),
        name="settle",
    )(total, *[array for kind in kinds for array in kind])


def local(
    pair_in, lengths, pair_cotangent, triangle_weights, expand_weights, shrink_weights, norm_params, triangle_first,
    triangle_second, expand_first, expand_second, shrink_first, shrink_second, norm_first, norm_second,
):
    norms = [jnp.swapaxes(array, 0, 1) for array in (norm_params, norm_first, norm_second)]
    outs = [(pair_in.shape, BF), (pair_in.shape, F32), ((2 * HALF, 128), BF)]
    pair_out, pair_grad, total = window(
        outs, lengths, pair_in, pair_cotangent, triangle_weights, expand_weights, shrink_weights, norms[0]
    )
    kinds = (
        (triangle_weights, triangle_first, triangle_second),
        (expand_weights, expand_first, expand_second),
        (shrink_weights, shrink_first, shrink_second),
        norms,
    )
    new = settle(total, kinds)
    moments = [new[4 * kind + place] for kind in range(3) for place in range(3)]
    norms_new = [jnp.swapaxes(array, 0, 1) for array in new[12:15]]
    copies = [new[4 * kind + 3] for kind in range(3)]
    return (pair_out, pair_grad, *moments, *norms_new, *copies, new[15].reshape(()))


def solution(mesh):
    pair = P(None, "row", "col", None)
    return jax.shard_map(
        local,
        mesh=mesh,
        in_specs=(pair, P(), pair) + (P(),) * 12,
        out_specs=(pair, pair) + (P(),) * 16,
        check_vma=False,
    )
```

```python
import jax
import jax.numpy as jnp
from jax import lax
from jax.experimental import pallas as pl
from jax.experimental.pallas import tpu as pltpu
from jax.sharding import PartitionSpec as P

LAYERS = 2
STEP = 10
CROPS = 2
COLS = 8
DEVICES = 128

EPS_NORM = 1e-05
BETA_ONE = 0.9
BETA_TWO = 0.999
ADAM_EPS = 1e-08
RATE = 0.1
NORM_RATE = 0.5
DECAY_RATE = 0.01
CLIP = 1.0

MESH = pl.DeviceIdType.MESH
BF = jnp.bfloat16
F32 = jnp.float32

C = 128
HID = 512
TILES = 16
PAIRS = 2048
WIDE = 1024
CHUNKS = PAIRS // WIDE
PER = WIDE // 128
VMEM_LIMIT = 61 << 20

EXPAND_ROW = 7 * C
SHRINK_ROW = EXPAND_ROW + LAYERS * 2 * HID
LATE_ROW = SHRINK_ROW + LAYERS * HID
NORM_ROW = LATE_ROW + 5 * C
EARLY = (0, 62, 32)
LATE = (LATE_ROW, 21, 16)
ROWS = LATE_ROW + 2 * 21 * 16


def triangle_start(layer, matrix):
    if layer == 1:
        return matrix * C
    return 6 * C if matrix == 5 else LATE_ROW + matrix * C


def triangle_rows(layer, matrix):
    return pl.ds(triangle_start(layer, matrix), C)


def expand_rows(layer, matrix, block):
    return pl.ds(EXPAND_ROW + ((layer * 2 + matrix) * 4 + block) * C, C)


def shrink_rows(layer):
    return pl.ds(SHRINK_ROW + layer * HID, HID)


def dot(left, right):
    return lax.dot_general(left, right, (((1,), (0,)), ((), ())), preferred_element_type=F32)


def dot_nt(left, right):
    return lax.dot_general(left, right, (((1,), (1,)), ((), ())), preferred_element_type=F32)


def dot_tn(left, right):
    return lax.dot_general(left, right, (((0,), (0,)), ((), ())), preferred_element_type=F32)


def sigmoid(v):
    return 0.5 * jnp.tanh(0.5 * v) + 0.5


KEPT = ("hidden", "grad_gate_up", "normed", "upstream", "updated", "grad_branch")


def mean_rows(v):
    return jnp.sum(v, axis=0, keepdims=True) * (1.0 / C)


def normalize(v):
    centered = v - mean_rows(v)
    scale = lax.rsqrt(mean_rows(centered * centered) + EPS_NORM)
    return centered * scale, scale


def normalize_back(grad, gain, hat, scale):
    grad_hat = grad * gain
    return scale * (grad_hat - mean_rows(grad_hat) - hat * mean_rows(grad_hat * hat))


def lanes_of(step):
    return pl.ds(pl.multiple_of(step * WIDE, WIDE), WIDE)


def scatter_tiles(scratch, step, value):
    for part in range(PER):
        scratch[pl.ds(step * PER + part, C, stride=TILES), :] = value[:, part * 128 : part * 128 + 128]


def gather_tiles(scratch, step):
    return jnp.concatenate(
        [scratch[pl.ds(step * PER + part, C, stride=TILES), :] for part in range(PER)], axis=1
    )


def pack_tiles(scratch, send, offset):
    send[:, offset : offset + TILES, :] = scratch[...].astype(BF).reshape(C, TILES, 128)


def unpack_tiles(recv, offset, scratch):
    scratch[...] = recv[:, offset : offset + TILES, :].reshape(PAIRS, 128).astype(F32)


def swap_halves(first, second):
    low = jnp.concatenate([first[:, :64], second[:, :64]], axis=1)
    high = jnp.concatenate([first[:, 64:], second[:, 64:]], axis=1)
    return low, high


def assemble(recv, offset, whole):
    for row in range(16):
        base = row * 32
        for pair in range(4):
            low, high = swap_halves(
                recv[row * 8 + 2 * pair, offset : offset + TILES, :],
                recv[row * 8 + 2 * pair + 1, offset : offset + TILES, :],
            )
            whole[base : base + 16, pair * 128 : pair * 128 + 128] = low
            whole[base + 16 : base + 32, pair * 128 : pair * 128 + 128] = high


def disassemble(whole, send, offset):
    for row in range(16):
        base = row * 32
        for pair in range(4):
            first, second = swap_halves(
                whole[base : base + 16, pair * 128 : pair * 128 + 128],
                whole[base + 16 : base + 32, pair * 128 : pair * 128 + 128],
            )
            send[row * 8 + 2 * pair, offset : offset + TILES, :] = first
            send[row * 8 + 2 * pair + 1, offset : offset + TILES, :] = second


def load_pairs(pair_ref, step):
    parts = []
    for part in range(PER):
        tile = step * PER + part
        parts.append(jnp.concatenate([pair_ref[tile], pair_ref[tile + TILES]], axis=0).astype(F32).T)
    return jnp.concatenate(parts, axis=1)


def store_pairs(value, step, out_ref):
    for part in range(PER):
        rows = value[:, part * 128 : part * 128 + 128].T
        out_ref[step * PER + part] = rows[:64].astype(out_ref.dtype)
        out_ref[step * PER + part + TILES] = rows[64:].astype(out_ref.dtype)


def project_step(x, mask, five, norms, scratch_a, scratch_b, gate_ref, step):
    hat, _ = normalize(x)
    normed = (hat * norms[0] + norms[1]).astype(BF)
    projected = dot(five[...], normed)
    left = mask * sigmoid(projected[:C]) * projected[C : 2 * C]
    right = mask * sigmoid(projected[2 * C : 3 * C]) * projected[3 * C : 4 * C]
    scatter_tiles(scratch_a, step, left)
    scatter_tiles(scratch_b, step, right)
    gate_ref[:, lanes_of(step)] = sigmoid(projected[4 * C :]).astype(BF)


def update_step(x, gate, z, out_t, expand_t, norms):
    z_hat, z_scale = normalize(z)
    updated = (z_hat * norms[2] + norms[3]).astype(BF)
    branch = dot(out_t[...], updated)
    middle = x + gate * branch
    mid_hat, mid_scale = normalize(middle)
    normed = (mid_hat * norms[4] + norms[5]).astype(BF)
    gate_up = dot(expand_t[...], normed)
    return (z_hat, z_scale, updated, branch, middle, mid_hat, mid_scale, normed, gate_up)


def swiglu(gate_up):
    gate_half = gate_up[:HID]
    sig = sigmoid(gate_half)
    silu = gate_half * sig
    return (sig, silu, (silu * gate_up[HID:]).astype(BF))


def back_step(upstream, parts, hidden_parts, gate, weights, norms, kept, lanes, g_norm):
    z_hat, z_scale, updated, branch, middle, mid_hat, mid_scale, normed, gate_up = parts
    sig, silu, hidden = hidden_parts
    shrink, expand, out_n = weights
    upstream_low = upstream.astype(BF)
    grad_hidden = dot(shrink[...], upstream_low)
    grad_gate = (grad_hidden * gate_up[HID:] * (sig + silu * (1.0 - sig))).astype(BF)
    grad_up = (grad_hidden * silu).astype(BF)
    grad_gate_up = jnp.concatenate([grad_gate, grad_up], axis=0)
    grad_normed = dot(expand[...], grad_gate_up)
    add_norm(g_norm, 4, grad_normed * mid_hat, grad_normed)
    grad_middle = upstream + normalize_back(grad_normed, norms[4], mid_hat, mid_scale)
    scaled = grad_middle * gate
    grad_branch = scaled.astype(BF)
    grad_out_gate = (scaled * branch * (1.0 - gate)).astype(BF)
    grad_updated = dot(out_n[...], grad_branch)
    add_norm(g_norm, 2, grad_updated * z_hat, grad_updated)
    grad_z = normalize_back(grad_updated, norms[2], z_hat, z_scale)
    for name, value in zip(KEPT, (hidden, grad_gate_up, normed, upstream_low, updated, grad_branch)):
        kept[name][:, lanes] = value
    return (grad_middle, grad_out_gate, grad_z)


def weight_grads(layer, kept, grad_rows):
    def steps(step):
        hidden, grad_gate_up, normed, upstream, updated, grad_branch = (kept[name][:, lanes_of(step)] for name in KEPT)
        grad_rows[shrink_rows(layer), :] += dot_nt(hidden, upstream)
        term = dot_nt(normed, grad_gate_up)
        for block in range(8):
            grad_rows[expand_rows(layer, block // 4, block % 4), :] += term[:, block * C : block * C + C]
        grad_rows[triangle_rows(layer, 5), :] += dot_nt(updated, grad_branch)

    for_steps(steps)


def add_norm(g_norm, index, gain_term, bias_term):
    for place, term in ((index, gain_term), (index + 1, bias_term)):
        total = term[:, :128]
        for part in range(1, PER):
            total = total + term[:, part * 128 : part * 128 + 128]
        g_norm[place] += total


def project_back_step(
    x, mask, grad_left, grad_right, grad_out_gate, grad_middle, five, five_n, norms, grads
):
    layer, grad_rows, g_norm = grads
    hat, scale = normalize(x)
    normed = (hat * norms[0] + norms[1]).astype(BF)
    projected = dot(five[: 4 * C, :], normed)
    pieces = []
    for grad, base in ((grad_left, 0), (grad_right, 2 * C)):
        sig = sigmoid(projected[base : base + C])
        masked = grad * mask * sig
        pieces.append((masked * projected[base + C : base + 2 * C] * (1.0 - sig)).astype(BF))
        pieces.append(masked.astype(BF))
    pieces.append(grad_out_gate)
    grad_projected = jnp.concatenate(pieces, axis=0)
    term = dot_nt(normed, grad_projected)
    for matrix in range(5):
        grad_rows[triangle_rows(layer, matrix), :] += term[:, matrix * C : matrix * C + C]
    grad_normed = dot(five_n[...], grad_projected)
    add_norm(g_norm, 0, grad_normed * hat, grad_normed)
    return grad_middle + normalize_back(grad_normed, norms[0], hat, scale)


class Norms:
    def __init__(self, ref, layer):
        self.ref, self.layer = ref, layer

    def __getitem__(self, index):
        value = self.ref[self.layer, index]
        return jnp.concatenate([value] * PER, axis=1)


def zero(*refs):
    for ref in refs:
        ref[...] = jnp.zeros_like(ref)


def distance(offset):
    return sum(min(step, 4 - step) for step in offset[:3])


OFFSETS = [(i % 4, i // 4 % 4, i // 16 % 4, i // 64) for i in range(1, 128)]
OFFSETS = [o for _, _, o in sorted((-distance(o), (i * 53 + 17) % 127, o) for i, o in enumerate(OFFSETS))]


class Place:
    def __init__(self):
        self.row, self.col = lax.axis_index("row"), lax.axis_index("col")
        self.me = self.row * COLS + self.col
        self.core = lax.rem(self.row, 2)
        x, y, z = lax.rem(self.row // 2, 4), self.row // 8 * 2 + lax.rem(self.col, 2), self.col // 2
        self.chip = self.row // 2 * COLS + self.col
        xs = [lax.rem(x + step, 4) * 2 for step in range(4)]
        ys = [lax.rem(y + step, 4) for step in range(4)]
        zs = [lax.rem(z + step, 4) * 2 for step in range(4)]
        cores = [self.core, 1 - self.core]
        highs, lows = [v // 2 * 8 for v in ys], [lax.rem(v, 2) for v in ys]
        self.rows = {(a, b, d): highs[b] + xs[a] + cores[d] for a in range(4) for b in range(4) for d in range(2)}
        self.cols = {(b, c): zs[c] + lows[b] for b in range(4) for c in range(4)}

    def at(self, offset):
        a, b, c, d = offset
        return self.rows[a, b, d], self.cols[b, c]


def exchange_start(place, send, recv, send_sem, recv_sem):
    for offset in OFFSETS:
        row, col = place.at(offset)
        pltpu.make_async_remote_copy(
            send.at[row * COLS + col], recv.at[place.me], send_sem, recv_sem, device_id=(row, col), device_id_type=MESH
        ).start()
    recv[place.me] = send[place.me]


def exchange_wait(ref, sem):
    others = pl.ds(0, DEVICES - 1)
    pltpu.make_async_copy(ref.at[others], ref.at[others], sem).wait()


def join(recv, left, right, whole, send):
    assemble(recv, 0, left)
    assemble(recv, TILES, right)
    whole[...] = dot_nt(left[...], right[...]).astype(BF)
    disassemble(whole, send, 0)


def join_back(recv, left, right, whole, result, send):
    assemble(recv, 0, whole)
    result[...] = dot(whole[...], right[...]).astype(BF)
    disassemble(result, send, 0)
    result[...] = dot_tn(whole[...], left[...]).astype(BF)
    disassemble(result, send, TILES)


INPUTS = ("lengths", "pair", "triangle", "norms_in", "cotangent_far", "expand_far", "shrink_far")
FAR = 3
OUTPUTS = ("pair_out_far", "pair_grad_far", "total")
SCRATCH = {
    "pair_out": ((CROPS, 32, 64, C), BF),
    "pair_grad": ((CROPS, 32, 64, C), F32),
    "cotangent": ((CROPS, 32, 64, C), BF),
    "expand_in": ((LAYERS, 2, C, HID), F32),
    "shrink_in": ((LAYERS, HID, C), F32),
    "mask": ((CROPS, 1, PAIRS), F32),
    "norms": ((LAYERS, 6, C, 128), F32),
    "five": ((LAYERS, 5 * C, C), BF),
    "five_n": ((LAYERS, C, 5 * C), BF),
    "out_t": ((LAYERS, C, C), BF),
    "out_n": ((LAYERS, C, C), BF),
    "expand_t": ((LAYERS, 2 * HID, C), BF),
    "expand": ((LAYERS, C, 2 * HID), BF),
    "shrink_t": ((LAYERS, C, HID), BF),
    "shrink": ((LAYERS, HID, C), BF),
    "x": ((LAYERS, CROPS, C, PAIRS), F32),
    "gate": ((LAYERS, CROPS, C, PAIRS), BF),
    "recv_ab": ((CROPS, C, 2 * TILES, 128), BF),
    "recv_z": ((LAYERS, CROPS, C, TILES, 128), BF),
    "recv_dz": ((CROPS, C, TILES, 128), BF),
    "send_wide": ((CROPS, C, 2 * TILES, 128), BF),
    "send_slim": ((CROPS, C, TILES, 128), BF),
    "left": ((LAYERS, CROPS, 512, 512), BF),
    "right": ((LAYERS, CROPS, 512, 512), BF),
    "mid": ((CROPS, C, PAIRS), F32),
    "out_gate": ((CROPS, C, PAIRS), BF),
    "tiles_a": ((PAIRS, 128), F32),
    "tiles_b": ((PAIRS, 128), F32),
    "tiles_z": ((PAIRS, 128), F32),
    "whole": ((512, 512), BF),
    "result": ((512, 512), BF),
    "hidden": ((HID, PAIRS), BF),
    "grad_gate_up": ((2 * HID, PAIRS), BF),
    "normed": ((C, PAIRS), BF),
    "upstream": ((C, PAIRS), BF),
    "updated": ((C, PAIRS), BF),
    "grad_branch": ((C, PAIRS), BF),
    "level": ((C, PAIRS), F32),
    "grad_rows": ((ROWS, 128), F32),
    "g_norm": ((LAYERS, 6, C, 128), F32),
}
for group, (_, pieces, piece) in (("early", EARLY), ("late", LATE)):
    SCRATCH.update({
        group + "_share": ((pieces * piece, 128), BF),
        group + "_sibling": ((pieces * piece, 128), BF),
        group + "_pieces": ((pieces, piece, 128), BF),
        group + "_landed": ((DEVICES // 2, piece, 128), BF),
        group + "_summed": ((pieces, piece, 128), BF),
    })


def prepare_triangle(r, layer):
    for index in range(6):
        row = r["norms_in"][index, layer : layer + 1, :]
        r["norms"][layer, index] = jnp.broadcast_to(row, (C, C)).T
    for matrix in range(5):
        weight = r["triangle"][layer, matrix]
        r["five"][layer, matrix * C : matrix * C + C, :] = weight.T.astype(BF)
        r["five_n"][layer, :, matrix * C : matrix * C + C] = weight.astype(BF)
    r["out_t"][layer] = r["triangle"][layer, 5].T.astype(BF)
    r["out_n"][layer] = r["triangle"][layer, 5].astype(BF)


def prepare_transition(r, layer):
    for matrix in range(2):
        for block in range(4):
            lanes = slice(block * C, block * C + C)
            rows = slice(matrix * HID + block * C, matrix * HID + block * C + C)
            weight = r["expand_in"][layer, matrix, :, lanes]
            r["expand_t"][layer, rows, :] = weight.T.astype(BF)
            r["expand"][layer, :, rows] = weight.astype(BF)
    for block in range(4):
        rows = slice(block * C, block * C + C)
        weight = r["shrink_in"][layer, rows, :]
        r["shrink_t"][layer, :, rows] = weight.T.astype(BF)
        r["shrink"][layer, rows, :] = weight.astype(BF)


def prepare_mask(r, place):
    pair = lax.broadcasted_iota(jnp.int32, (1, PAIRS), 1)
    tile, lane = pair // 128, lax.rem(pair, 128)
    first = place.row * 32 + lane // 64 * TILES + tile
    second = place.col * 64 + lax.rem(lane, 64)
    last = jnp.maximum(first, second)
    for crop in range(CROPS):
        r["mask"][crop] = jnp.clip(r["lengths"][crop] - last, 0, 1).astype(F32)


def for_crops(visit):
    def run(crop, carry):
        visit(crop)
        return carry

    lax.fori_loop(0, CROPS, run, 0)


def for_steps(visit):
    def run(step, carry):
        visit(step)
        return carry

    lax.fori_loop(0, CHUNKS, run, 0)


def window_kernel(*refs):
    names = INPUTS + OUTPUTS + tuple(SCRATCH)
    r = dict(zip(names, refs))
    send_sem, recv_sem, sum_sem, load_sem, store_sem = refs[len(names) :]
    place = Place()
    loads = [
        pltpu.make_async_copy(r[far], r[near], load_sem.at[index])
        for index, (far, near) in enumerate(
            (("expand_far", "expand_in"), ("shrink_far", "shrink_in"), ("cotangent_far", "cotangent"))
        )
    ]
    for load in loads:
        load.start()

    barrier = pltpu.get_barrier_semaphore()
    for offset in OFFSETS:
        pl.semaphore_signal(barrier, inc=1, device_id=place.at(offset), device_id_type=MESH)

    early, late = Sum("early", EARLY, place, r, sum_sem.at[0]), Sum("late", LATE, place, r, sum_sem.at[1])

    def sent(kind, crop, index):
        exchange_wait(r[kind].at[crop], send_sem.at[index + crop])

    def second_sent(kind, crop, index):
        if not isinstance(crop, int):
            pl.when(crop == 1)(lambda: sent(kind, 1, index))
        elif crop:
            sent(kind, 1, index)

    def begin(kind, crop, recv, index, alone=False):
        if alone and not isinstance(crop, int):
            pl.when(crop == 1)(lambda: sent(kind, 0, index))
        elif alone and crop:
            sent(kind, 0, index)
        exchange_start(place, r[kind].at[crop], recv, send_sem.at[index + crop], recv_sem.at[index + crop])

    def project(layer, crop, step, x):
        project_step(
            x, r["mask"][crop, :, lanes_of(step)], r["five"].at[layer], Norms(r["norms"], layer), r["tiles_a"], r["tiles_b"],
            r["gate"].at[layer, crop], step,
        )

    def send_sides(layer, crop):
        if layer:
            sent("send_wide", crop, 0)
        pack_tiles(r["tiles_a"], r["send_wide"].at[crop], 0)
        pack_tiles(r["tiles_b"], r["send_wide"].at[crop], TILES)
        begin("send_wide", crop, r["recv_ab"].at[crop], layer * 8)

    def update(layer, crop, step):
        lanes = lanes_of(step)
        gate = r["gate"][layer, crop, :, lanes].astype(F32)
        gains = Norms(r["norms"], layer)
        parts = update_step(
            r["x"][layer, crop, :, lanes], gate, gather_tiles(r["tiles_z"], step), r["out_t"].at[layer], r["expand_t"].at[layer], gains
        )
        return gate, gains, parts

    def back(layer, crop, step, upstream, gate, gains, parts, hidden_parts):
        lanes = lanes_of(step)
        weights = (r["shrink"].at[layer], r["expand"].at[layer], r["out_n"].at[layer])
        middle, out_gate, grad_z = back_step(
            upstream, parts, hidden_parts, gate, weights, gains, r, lanes, r["g_norm"].at[layer]
        )
        r["mid"][crop, :, lanes] = middle
        r["out_gate"][crop, :, lanes] = out_gate
        scatter_tiles(r["tiles_z"], step, grad_z)

    def project_back(layer, crop, step):
        lanes = lanes_of(step)
        return project_back_step(
            r["x"][layer, crop, :, lanes], r["mask"][crop, :, lanes], gather_tiles(r["tiles_a"], step), gather_tiles(r["tiles_b"], step),
            r["out_gate"][crop, :, lanes], r["mid"][crop, :, lanes], r["five"].at[layer], r["five_n"].at[layer],
            Norms(r["norms"], layer), (layer, r["grad_rows"], r["g_norm"].at[layer]),
        )

    def send_grad_z(layer, crop):
        if layer:
            second_sent("send_slim", crop, 10)
        else:
            sent("send_slim", crop, 12)
        pack_tiles(r["tiles_z"], r["send_slim"].at[crop], 0)
        begin("send_slim", crop, r["recv_dz"].at[crop], layer * 8 + 4)

    prepare_mask(r, place)
    prepare_triangle(r, 0)

    def first(crop):
        def steps(step):
            x = load_pairs(r["pair"].at[crop], step)
            r["x"][0, crop, :, lanes_of(step)] = x
            project(0, crop, step, x)

        for_steps(steps)

        @pl.when(crop == 0)
        def _():
            pl.semaphore_wait(barrier, DEVICES - 1)

        send_sides(0, crop)

    for_crops(first)
    for load in loads:
        load.wait()
    prepare_transition(r, 0)
    for layer in range(1, LAYERS):
        prepare_triangle(r, layer)
        prepare_transition(r, layer)
    zero(r["grad_rows"], r["g_norm"])

    stores = []

    def store(name, crop):
        near, far = r[name].at[crop], r[name + "_far"].at[crop]
        stores.append(pltpu.make_async_copy(near, far, store_sem.at[len(stores)]))
        stores[-1].start()

    def products(layer, crop):
        recv = r["recv_ab"].at[crop]
        exchange_wait(recv, recv_sem.at[layer * 8 + crop])
        if layer:
            second_sent("send_slim", crop, 2)
        join(recv, r["left"].at[layer, crop], r["right"].at[layer, crop], r["whole"], r["send_slim"].at[crop])
        begin("send_slim", crop, r["recv_z"].at[layer, crop], layer * 8 + 2, alone=True)

    def onward(crop):
        recv = r["recv_z"].at[0, crop]
        exchange_wait(recv, recv_sem.at[2 + crop])
        unpack_tiles(recv, 0, r["tiles_z"])

        def forward(step):
            gate, gains, parts = update(0, crop, step)
            x_new = parts[4] + dot(r["shrink_t"][0], swiglu(parts[-1])[2])
            r["x"][1, crop, :, lanes_of(step)] = x_new
            project(1, crop, step, x_new)

        for_steps(forward)
        send_sides(1, crop)

    def turn(crop):
        recv = r["recv_z"].at[1, crop]
        exchange_wait(recv, recv_sem.at[10 + crop])
        unpack_tiles(recv, 0, r["tiles_z"])

        def steps(step):
            gate, gains, parts = update(1, crop, step)
            r["level"][:, lanes_of(step)] = parts[4]
            back(1, crop, step, load_pairs(r["cotangent"].at[crop], step), gate, gains, parts, swiglu(parts[-1]))

        for_steps(steps)
        send_grad_z(1, crop)

    def after_turn(crop):
        weight_grads(1, r, r["grad_rows"])

        def steps(step):
            lanes = lanes_of(step)
            store_pairs(r["level"][:, lanes] + dot(r["shrink_t"][1], r["hidden"][:, lanes]), step, r["pair_out"].at[crop])

        for_steps(steps)
        store("pair_out", crop)

    def products_back(layer, crop):
        recv = r["recv_dz"].at[crop]
        exchange_wait(recv, recv_sem.at[layer * 8 + 4 + crop])
        if layer:
            sent("send_wide", crop, 8)
        else:
            second_sent("send_wide", crop, 14)
        join_back(recv, r["left"].at[layer, crop], r["right"].at[layer, crop], r["whole"], r["result"], r["send_wide"].at[crop])
        begin("send_wide", crop, r["recv_ab"].at[crop], layer * 8 + 6, alone=layer == 1)

    def receive_sides_grad(layer, crop):
        recv = r["recv_ab"].at[crop]
        exchange_wait(recv, recv_sem.at[layer * 8 + 6 + crop])
        unpack_tiles(recv, 0, r["tiles_a"])
        unpack_tiles(recv, TILES, r["tiles_b"])

    def deep(crop):
        receive_sides_grad(1, crop)
        unpack_tiles(r["recv_z"].at[0, crop], 0, r["tiles_z"])

        def steps(step):
            upstream = project_back(1, crop, step)
            gate, gains, parts = update(0, crop, step)
            back(0, crop, step, upstream, gate, gains, parts, swiglu(parts[-1]))

        for_steps(steps)
        send_grad_z(0, crop)

    def last(crop):
        receive_sides_grad(0, crop)
        for_steps(lambda step: store_pairs(project_back(0, crop, step), step, r["pair_grad"].at[crop]))
        store("pair_grad", crop)

    for_crops(lambda crop: products(0, crop))
    for_crops(onward)
    for_crops(lambda crop: products(1, crop))
    turn(0)
    after_turn(0)
    turn(1)
    products_back(1, 0)
    after_turn(1)
    products_back(1, 1)
    deep(0)
    weight_grads(0, r, r["grad_rows"])
    deep(1)
    products_back(0, 0)
    weight_grads(0, r, r["grad_rows"])
    early.share()
    products_back(0, 1)
    last(0)
    early.scatter()
    last(1)
    for layer in range(LAYERS):
        for index in range(6):
            row = NORM_ROW + index * LAYERS + layer
            r["grad_rows"][row : row + 1, :] = jnp.sum(r["g_norm"][layer, index].T, axis=0, keepdims=True)
    late.share()
    late.scatter()
    early.spread()
    late.spread()
    early.gather()
    late.gather()
    early.finish()
    late.finish()
    for crop in range(CROPS):
        sent("send_slim", crop, 4)
        sent("send_wide", crop, 6)
    for store in stores:
        store.wait()


class Sum:
    def __init__(self, name, group, place, r, sem):
        self.first, self.count, self.piece = group
        self.half = self.count * self.piece
        self.place, self.r, self.sem = place, r, sem
        self.share_ref, self.sibling, self.pieces, self.landed, self.summed = (
            r[name + suffix] for suffix in ("_share", "_sibling", "_pieces", "_landed", "_summed")
        )
        self.owner = place.chip < self.count
        self.offsets = [offset for offset in OFFSETS if offset[3] == 0]

    def rows(self, core):
        return pl.ds(pl.multiple_of(self.first + core * self.half, 16), self.half)

    def swap(self, source, target, index):
        return pltpu.make_async_remote_copy(
            source, target, self.sem.at[index], self.sem.at[index + 1], device_id=self.place.at((0, 0, 0, 1)), device_id_type=MESH
        )

    def push(self, source, target, index, offset):
        pltpu.make_async_remote_copy(
            source, target, self.sem.at[index], self.sem.at[index + 1], device_id=self.place.at(offset), device_id_type=MESH
        ).start()

    def wait(self, ref, count, index):
        some = ref.at[pl.ds(0, count)]
        pltpu.make_async_copy(some, some, self.sem.at[index]).wait()

    def share(self):
        self.share_ref[...] = self.r["grad_rows"][self.rows(1 - self.place.core), :].astype(BF)
        self.swap(self.share_ref, self.sibling, 0).start()

    def scatter(self):
        self.swap(self.share_ref, self.sibling, 0).wait()
        both = self.r["grad_rows"][self.rows(self.place.core), :] + self.sibling[...].astype(F32)
        self.pieces[...] = both.astype(BF).reshape(self.count, self.piece, 128)
        for offset in self.offsets:
            row, col = self.place.at(offset)
            piece = row // 2 * COLS + col

            @pl.when(piece < self.count)
            def _():
                self.push(self.pieces.at[piece], self.landed.at[self.place.chip], 2, offset)

    def spread(self):
        chip, chips = self.place.chip, DEVICES // 2

        @pl.when(self.owner)
        def _():
            self.landed[chip] = self.pieces[chip]
            self.wait(self.landed, chips - 1, 3)

            def add(index, carry):
                return carry + self.landed[index].astype(F32)

            self.summed[chip] = lax.fori_loop(1, chips, add, self.landed[0].astype(F32)).astype(BF)
            for offset in self.offsets:
                self.push(self.summed.at[chip], self.summed.at[chip], 4, offset)

    def gather(self):
        @pl.when(self.owner)
        def _():
            self.wait(self.pieces, self.count - 1, 2)
            self.wait(self.landed, DEVICES // 2 - 1, 4)
            self.wait(self.summed, self.count - 1, 5)

        @pl.when(jnp.logical_not(self.owner))
        def _():
            self.wait(self.pieces, self.count, 2)
            self.wait(self.summed, self.count, 5)

        own = self.r["total"].at[self.rows(self.place.core)]
        own[...] = self.summed[...].reshape(self.half, 128)
        self.swap(own, own, 6).start()

    def finish(self):
        own = self.r["total"].at[self.rows(self.place.core)]
        self.swap(own, own, 6).wait()


def window(outs, lengths, *args):
    return pl.pallas_call(
        window_kernel,
        out_shape=[jax.ShapeDtypeStruct(shape, dtype) for shape, dtype in outs],
        in_specs=[pl.BlockSpec(memory_space=pltpu.SMEM)] + [pl.BlockSpec(memory_space=pltpu.VMEM)] * (len(args) - FAR)
        + [pl.BlockSpec(memory_space=pl.ANY)] * FAR,
        out_specs=[pl.BlockSpec(memory_space=pl.ANY)] * 2 + [pl.BlockSpec(memory_space=pltpu.VMEM)],
        scratch_shapes=[pltpu.VMEM(shape, dtype) for shape, dtype in SCRATCH.values()]
        + [pltpu.SemaphoreType.DMA((8 * LAYERS,))] * 2
        + [pltpu.SemaphoreType.DMA((2, 8)), pltpu.SemaphoreType.DMA((FAR,)), pltpu.SemaphoreType.DMA((2 * CROPS,))],
        compiler_params=pltpu.CompilerParams(collective_id=1, has_side_effects=True, vmem_limit_bytes=VMEM_LIMIT),
        name="window",
    )(lengths, *args)


def adamw(gradient, weight, first, second, clip_factor, step_rate, decay_rate, outs):
    clipped = gradient * clip_factor
    moment = BETA_ONE * first + (1.0 - BETA_ONE) * clipped
    square = BETA_TWO * second + (1.0 - BETA_TWO) * clipped * clipped
    correct_one = 1.0 - BETA_ONE**STEP
    correct_two = 1.0 - BETA_TWO**STEP
    update = moment * (step_rate / correct_one) / (jnp.sqrt(square * (1.0 / correct_two)) + ADAM_EPS)
    renewed = weight * (1.0 - step_rate * decay_rate) - update
    for (ref, place), value in zip(outs, (moment, square, renewed, renewed)):
        ref[place] = value.astype(ref.dtype)


def settle_kernel(*refs):
    total_in, ins = refs[0], refs[1:13]
    outs, norm_ref = refs[13:28], refs[28]
    total, held, made = refs[29], refs[30:42], refs[42:57]
    total_sem, in_sem, out_sem = refs[57:]

    first = pltpu.make_async_copy(total_in, total, total_sem)
    first.start()
    loads = {}
    for part in range(LAYERS):
        for index in range(9):
            loads[part, index] = pltpu.make_async_copy(ins[index].at[part], held[index].at[part], in_sem.at[part * 9 + index])
            loads[part, index].start()
    for index in range(9, 12):
        loads[0, index] = pltpu.make_async_copy(ins[index], held[index], in_sem.at[9 * LAYERS + index - 9])
        loads[0, index].start()
    first.wait()

    def square(step, carry):
        rows = total[pl.ds(pl.multiple_of(step * 464, 16), 464), :].astype(F32)
        return carry + jnp.sum((rows * rows).reshape(58, 8, 128), axis=0)

    squares = lax.fori_loop(0, ROWS // 464, square, jnp.zeros((8, 128), F32))
    grad_norm = jnp.sqrt(jnp.sum(jnp.sum(squares, axis=1, keepdims=True), axis=0, keepdims=True))
    norm_ref[...] = grad_norm
    factor = jnp.minimum(1.0, CLIP / (grad_norm + 1e-06))
    stores = []

    def store(index, part):
        pieces = (made[index], outs[index]) if part is None else (made[index].at[part], outs[index].at[part])
        copy = pltpu.make_async_copy(*pieces, out_sem.at[len(stores)])
        copy.start()
        stores.append(copy)

    def run(kind, start, size, place):
        values = [ref[place] for ref in held[3 * kind : 3 * kind + 3]]
        gradient = total[start : start + size, :].astype(F32)
        adamw(gradient, *values, factor, RATE, DECAY_RATE, [(ref, place) for ref in made[4 * kind : 4 * kind + 4]])

    for part in range(LAYERS):
        for kind in range(3):
            for index in range(3):
                loads[part, 3 * kind + index].wait()
            for block in range((6, 8, 4)[kind]):
                if kind == 0:
                    run(kind, triangle_start(part, block), C, (part, block))
                elif kind == 1:
                    place = (part, block // 4, slice(None), slice(block % 4 * C, block % 4 * C + C))
                    run(kind, EXPAND_ROW + (part * 8 + block) * C, C, place)
                else:
                    run(kind, SHRINK_ROW + part * HID + block * C, C, (part, slice(block * C, block * C + C)))
            for index in range(4):
                store(4 * kind + index, part)
    for index in range(9, 12):
        loads[0, index].wait()
    rows = total[NORM_ROW : NORM_ROW + 16, :].astype(F32)
    for index in range(6):
        values = [ref[index] for ref in held[9:12]]
        outputs = [(ref, index) for ref in made[12:15]]
        adamw(rows[index * LAYERS : index * LAYERS + LAYERS], *values, factor, NORM_RATE, 0.0, outputs)
    for index in range(12, 15):
        store(index, None)
    for copy in stores:
        copy.wait()


def settle(total, kinds):
    arrays = [array for kind in kinds for array in kind]
    made = [(kind[0].shape, dtype) for kind in kinds[:3] for dtype in (F32, F32, F32, BF)] + [(kinds[3][0].shape, F32)] * 3
    anywhere = pl.BlockSpec(memory_space=pl.ANY)
    shapes = [jax.ShapeDtypeStruct(*shape) for shape in made] + [jax.ShapeDtypeStruct((1, 1), F32)]
    return pl.pallas_call(
        settle_kernel,
        out_shape=shapes,
        in_specs=[anywhere] * (1 + len(arrays)),
        out_specs=[anywhere] * (len(shapes) - 1) + [pl.BlockSpec(memory_space=pltpu.VMEM)],
        scratch_shapes=[pltpu.VMEM(total.shape, total.dtype)]
        + [pltpu.VMEM(array.shape, array.dtype) for array in arrays]
        + [pltpu.VMEM(*shape) for shape in made]
        + [pltpu.SemaphoreType.DMA]
        + [pltpu.SemaphoreType.DMA((9 * LAYERS + 3,)), pltpu.SemaphoreType.DMA((12 * LAYERS + 3,))],
        compiler_params=pltpu.CompilerParams(vmem_limit_bytes=VMEM_LIMIT),
        name="settle",
    )(total, *arrays)


def local(
    pair_in, lengths, pair_cotangent, triangle_weights, expand_weights, shrink_weights, norm_params, triangle_first,
    triangle_second, expand_first, expand_second, shrink_first, shrink_second, norm_first, norm_second,
):
    norms = [jnp.swapaxes(array, 0, 1) for array in (norm_params, norm_first, norm_second)]
    outs = [(pair_in.shape, BF), (pair_in.shape, F32), ((ROWS, 128), BF)]
    pair_out, pair_grad, total = window(
        outs, lengths, pair_in, triangle_weights, norms[0], pair_cotangent, expand_weights, shrink_weights
    )
    kinds = (
        (triangle_weights, triangle_first, triangle_second),
        (expand_weights, expand_first, expand_second),
        (shrink_weights, shrink_first, shrink_second),
        norms,
    )
    new = settle(total, kinds)
    moments = [new[4 * kind + place] for kind in range(3) for place in range(3)]
    norms_new = [jnp.swapaxes(array, 0, 1) for array in new[12:15]]
    copies = [new[4 * kind + 3] for kind in range(3)]
    return (pair_out, pair_grad, *moments, *norms_new, *copies, new[15].reshape(()))


def solution(mesh):
    pair = P(None, "row", "col", None)
    return jax.shard_map(
        local,
        mesh=mesh,
        in_specs=(pair, P(), pair) + (P(),) * 12,
        out_specs=(pair, pair) + (P(),) * 16,
        check_vma=False,
    )
```

```python
import jax
import jax.numpy as jnp
from jax import lax
from jax.experimental import pallas as pl
from jax.experimental.pallas import tpu as pltpu
from jax.sharding import PartitionSpec as P

LAYERS = 2
STEP = 10
CROPS = 2
COLS = 8
DEVICES = 128

EPS_NORM = 1e-05
BETA_ONE = 0.9
BETA_TWO = 0.999
ADAM_EPS = 1e-08
RATE = 0.1
NORM_RATE = 0.5
DECAY_RATE = 0.01
CLIP = 1.0

MESH = pl.DeviceIdType.MESH
BF = jnp.bfloat16
F32 = jnp.float32

C = 128
HID = 512
TILES = 16
PAIRS = 2048
WIDE = 1024
CHUNKS = PAIRS // WIDE
PER = WIDE // 128
VMEM_LIMIT = 61 << 20

EXPAND_ROW = 7 * C
SHRINK_ROW = EXPAND_ROW + LAYERS * 2 * HID
LATE_ROW = SHRINK_ROW + LAYERS * HID
NORM_ROW = LATE_ROW + 5 * C
EARLY = (0, 62, 32)
LATE = (LATE_ROW, 21, 16)
ROWS = LATE_ROW + 2 * 21 * 16


def triangle_start(layer, matrix):
    if layer == 1:
        return matrix * C
    return 6 * C if matrix == 5 else LATE_ROW + matrix * C


def triangle_rows(layer, matrix):
    return pl.ds(triangle_start(layer, matrix), C)


def expand_rows(layer, matrix, block):
    return pl.ds(EXPAND_ROW + ((layer * 2 + matrix) * 4 + block) * C, C)


def shrink_rows(layer):
    return pl.ds(SHRINK_ROW + layer * HID, HID)


def dot(left, right):
    return lax.dot_general(left, right, (((1,), (0,)), ((), ())), preferred_element_type=F32)


def dot_nt(left, right):
    return lax.dot_general(left, right, (((1,), (1,)), ((), ())), preferred_element_type=F32)


def dot_tn(left, right):
    return lax.dot_general(left, right, (((0,), (0,)), ((), ())), preferred_element_type=F32)


def sigmoid(v):
    return 0.5 * jnp.tanh(0.5 * v) + 0.5


KEPT = ("hidden", "grad_gate_up", "normed", "upstream", "updated", "grad_branch")


def mean_rows(v):
    return jnp.sum(v, axis=0, keepdims=True) * (1.0 / C)


def normalize(v):
    centered = v - mean_rows(v)
    scale = lax.rsqrt(mean_rows(centered * centered) + EPS_NORM)
    return centered * scale, scale


def normalize_back(grad, gain, hat, scale):
    grad_hat = grad * gain
    return scale * (grad_hat - mean_rows(grad_hat) - hat * mean_rows(grad_hat * hat))


def lanes_of(step):
    return pl.ds(pl.multiple_of(step * WIDE, WIDE), WIDE)


def scatter_tiles(scratch, step, value):
    for part in range(PER):
        scratch[pl.ds(step * PER + part, C, stride=TILES), :] = value[:, part * 128 : part * 128 + 128]


def gather_tiles(scratch, step):
    return jnp.concatenate(
        [scratch[pl.ds(step * PER + part, C, stride=TILES), :] for part in range(PER)], axis=1
    )


def pack_tiles(scratch, send, offset):
    send[:, offset : offset + TILES, :] = scratch[...].astype(BF).reshape(C, TILES, 128)


def unpack_tiles(recv, offset, scratch):
    scratch[...] = recv[:, offset : offset + TILES, :].reshape(PAIRS, 128).astype(F32)


def swap_halves(first, second):
    low = jnp.concatenate([first[:, :64], second[:, :64]], axis=1)
    high = jnp.concatenate([first[:, 64:], second[:, 64:]], axis=1)
    return low, high


def assemble(recv, offset, whole):
    for row in range(16):
        base = row * 32
        for pair in range(4):
            low, high = swap_halves(
                recv[row * 8 + 2 * pair, offset : offset + TILES, :],
                recv[row * 8 + 2 * pair + 1, offset : offset + TILES, :],
            )
            whole[base : base + 16, pair * 128 : pair * 128 + 128] = low
            whole[base + 16 : base + 32, pair * 128 : pair * 128 + 128] = high


def disassemble(whole, send, offset):
    for row in range(16):
        base = row * 32
        for pair in range(4):
            first, second = swap_halves(
                whole[base : base + 16, pair * 128 : pair * 128 + 128],
                whole[base + 16 : base + 32, pair * 128 : pair * 128 + 128],
            )
            send[row * 8 + 2 * pair, offset : offset + TILES, :] = first
            send[row * 8 + 2 * pair + 1, offset : offset + TILES, :] = second


def load_pairs(pair_ref, step):
    parts = []
    for part in range(PER):
        tile = step * PER + part
        parts.append(jnp.concatenate([pair_ref[tile], pair_ref[tile + TILES]], axis=0).astype(F32).T)
    return jnp.concatenate(parts, axis=1)


def store_pairs(value, step, out_ref):
    for part in range(PER):
        rows = value[:, part * 128 : part * 128 + 128].T
        out_ref[step * PER + part] = rows[:64].astype(out_ref.dtype)
        out_ref[step * PER + part + TILES] = rows[64:].astype(out_ref.dtype)


def project_step(x, mask, five, norms, scratch_a, scratch_b, gate_ref, step):
    hat, _ = normalize(x)
    normed = (hat * norms[0] + norms[1]).astype(BF)
    projected = dot(five[...], normed)
    left = mask * sigmoid(projected[:C]) * projected[C : 2 * C]
    right = mask * sigmoid(projected[2 * C : 3 * C]) * projected[3 * C : 4 * C]
    scatter_tiles(scratch_a, step, left)
    scatter_tiles(scratch_b, step, right)
    gate_ref[:, lanes_of(step)] = sigmoid(projected[4 * C :]).astype(BF)


def update_step(x, gate, z, out_t, expand_t, norms):
    z_hat, z_scale = normalize(z)
    updated = (z_hat * norms[2] + norms[3]).astype(BF)
    branch = dot(out_t[...], updated)
    middle = x + gate * branch
    mid_hat, mid_scale = normalize(middle)
    normed = (mid_hat * norms[4] + norms[5]).astype(BF)
    gate_up = dot(expand_t[...], normed)
    return (z_hat, z_scale, updated, branch, middle, mid_hat, mid_scale, normed, gate_up)


def swiglu(gate_up):
    gate_half = gate_up[:HID]
    sig = sigmoid(gate_half)
    silu = gate_half * sig
    return (sig, silu, (silu * gate_up[HID:]).astype(BF))


def back_step(upstream, parts, hidden_parts, gate, weights, norms, kept, lanes, g_norm):
    z_hat, z_scale, updated, branch, middle, mid_hat, mid_scale, normed, gate_up = parts
    sig, silu, hidden = hidden_parts
    shrink, expand, out_n = weights
    upstream_low = upstream.astype(BF)
    grad_hidden = dot(shrink[...], upstream_low)
    grad_gate = (grad_hidden * gate_up[HID:] * (sig + silu * (1.0 - sig))).astype(BF)
    grad_up = (grad_hidden * silu).astype(BF)
    grad_gate_up = jnp.concatenate([grad_gate, grad_up], axis=0)
    grad_normed = dot(expand[...], grad_gate_up)
    add_norm(g_norm, 4, grad_normed * mid_hat, grad_normed)
    grad_middle = upstream + normalize_back(grad_normed, norms[4], mid_hat, mid_scale)
    scaled = grad_middle * gate
    grad_branch = scaled.astype(BF)
    grad_out_gate = (scaled * branch * (1.0 - gate)).astype(BF)
    grad_updated = dot(out_n[...], grad_branch)
    add_norm(g_norm, 2, grad_updated * z_hat, grad_updated)
    grad_z = normalize_back(grad_updated, norms[2], z_hat, z_scale)
    for name, value in zip(KEPT, (hidden, grad_gate_up, normed, upstream_low, updated, grad_branch)):
        kept[name][:, lanes] = value
    return (grad_middle, grad_out_gate, grad_z)


def weight_grads(layer, kept, grad_rows):
    def steps(step):
        hidden, grad_gate_up, normed, upstream, updated, grad_branch = (kept[name][:, lanes_of(step)] for name in KEPT)
        grad_rows[shrink_rows(layer), :] += dot_nt(hidden, upstream)
        term = dot_nt(normed, grad_gate_up)
        for block in range(8):
            grad_rows[expand_rows(layer, block // 4, block % 4), :] += term[:, block * C : block * C + C]
        grad_rows[triangle_rows(layer, 5), :] += dot_nt(updated, grad_branch)

    for_steps(steps)


def add_norm(g_norm, index, gain_term, bias_term):
    for place, term in ((index, gain_term), (index + 1, bias_term)):
        total = term[:, :128]
        for part in range(1, PER):
            total = total + term[:, part * 128 : part * 128 + 128]
        g_norm[place] += total


def project_back_step(
    x, mask, grad_left, grad_right, grad_out_gate, grad_middle, five, five_n, norms, grads
):
    layer, grad_rows, g_norm = grads
    hat, scale = normalize(x)
    normed = (hat * norms[0] + norms[1]).astype(BF)
    projected = dot(five[: 4 * C, :], normed)
    pieces = []
    for grad, base in ((grad_left, 0), (grad_right, 2 * C)):
        sig = sigmoid(projected[base : base + C])
        masked = grad * mask * sig
        pieces.append((masked * projected[base + C : base + 2 * C] * (1.0 - sig)).astype(BF))
        pieces.append(masked.astype(BF))
    pieces.append(grad_out_gate)
    grad_projected = jnp.concatenate(pieces, axis=0)
    term = dot_nt(normed, grad_projected)
    for matrix in range(5):
        grad_rows[triangle_rows(layer, matrix), :] += term[:, matrix * C : matrix * C + C]
    grad_normed = dot(five_n[...], grad_projected)
    add_norm(g_norm, 0, grad_normed * hat, grad_normed)
    return grad_middle + normalize_back(grad_normed, norms[0], hat, scale)


class Norms:
    def __init__(self, ref, layer):
        self.ref, self.layer = ref, layer

    def __getitem__(self, index):
        value = self.ref[self.layer, index]
        return jnp.concatenate([value] * PER, axis=1)


def zero(*refs):
    for ref in refs:
        ref[...] = jnp.zeros_like(ref)


def distance(offset):
    return sum(min(step, 4 - step) for step in offset[:3])


OFFSETS = [(i % 4, i // 4 % 4, i // 16 % 4, i // 64) for i in range(1, 128)]
OFFSETS = [o for _, _, o in sorted((-distance(o), (i * 53 + 17) % 127, o) for i, o in enumerate(OFFSETS))]


class Place:
    def __init__(self):
        self.row, self.col = lax.axis_index("row"), lax.axis_index("col")
        self.me = self.row * COLS + self.col
        self.core = lax.rem(self.row, 2)
        x, y, z = lax.rem(self.row // 2, 4), self.row // 8 * 2 + lax.rem(self.col, 2), self.col // 2
        self.chip = self.row // 2 * COLS + self.col
        xs = [lax.rem(x + step, 4) * 2 for step in range(4)]
        ys = [lax.rem(y + step, 4) for step in range(4)]
        zs = [lax.rem(z + step, 4) * 2 for step in range(4)]
        cores = [self.core, 1 - self.core]
        highs, lows = [v // 2 * 8 for v in ys], [lax.rem(v, 2) for v in ys]
        self.rows = {(a, b, d): highs[b] + xs[a] + cores[d] for a in range(4) for b in range(4) for d in range(2)}
        self.cols = {(b, c): zs[c] + lows[b] for b in range(4) for c in range(4)}

    def at(self, offset):
        a, b, c, d = offset
        return self.rows[a, b, d], self.cols[b, c]


def exchange_start(place, send, recv, send_sem, recv_sem):
    for offset in OFFSETS:
        row, col = place.at(offset)
        pltpu.make_async_remote_copy(
            send.at[row * COLS + col], recv.at[place.me], send_sem, recv_sem, device_id=(row, col), device_id_type=MESH
        ).start()
    recv[place.me] = send[place.me]


def exchange_wait(ref, sem):
    others = pl.ds(0, DEVICES - 1)
    pltpu.make_async_copy(ref.at[others], ref.at[others], sem).wait()


def join(recv, left, right, whole, send):
    assemble(recv, 0, left)
    assemble(recv, TILES, right)
    whole[...] = dot_nt(left[...], right[...]).astype(BF)
    disassemble(whole, send, 0)


def join_back(recv, left, right, whole, result, send):
    assemble(recv, 0, whole)
    result[...] = dot(whole[...], right[...]).astype(BF)
    disassemble(result, send, 0)
    result[...] = dot_tn(whole[...], left[...]).astype(BF)
    disassemble(result, send, TILES)


INPUTS = ("lengths", "pair", "triangle", "norms_in", "cotangent_far", "expand_far", "shrink_far")
FAR = 3
STORES = ("pair_out", "pair_grad")
OUTPUTS = ("pair_out_far", "pair_grad_far", "total")
SCRATCH = {
    "pair_out": ((CROPS, 32, 64, C), BF),
    "pair_grad": ((CROPS, 32, 64, C), F32),
    "cotangent": ((CROPS, 32, 64, C), BF),
    "expand_in": ((LAYERS, 2, C, HID), F32),
    "shrink_in": ((LAYERS, HID, C), F32),
    "mask": ((CROPS, 1, PAIRS), F32),
    "norms": ((LAYERS, 6, C, 128), F32),
    "five": ((LAYERS, 5 * C, C), BF),
    "five_n": ((LAYERS, C, 5 * C), BF),
    "out_t": ((LAYERS, C, C), BF),
    "out_n": ((LAYERS, C, C), BF),
    "expand_t": ((LAYERS, 2 * HID, C), BF),
    "expand": ((LAYERS, C, 2 * HID), BF),
    "shrink_t": ((LAYERS, C, HID), BF),
    "shrink": ((LAYERS, HID, C), BF),
    "x": ((LAYERS, CROPS, C, PAIRS), F32),
    "gate": ((LAYERS, CROPS, C, PAIRS), BF),
    "recv_ab": ((CROPS, C, 2 * TILES, 128), BF),
    "recv_z": ((LAYERS, CROPS, C, TILES, 128), BF),
    "recv_dz": ((CROPS, C, TILES, 128), BF),
    "send_wide": ((CROPS, C, 2 * TILES, 128), BF),
    "send_slim": ((CROPS, C, TILES, 128), BF),
    "left": ((LAYERS, CROPS, 512, 512), BF),
    "right": ((LAYERS, CROPS, 512, 512), BF),
    "mid": ((CROPS, C, PAIRS), F32),
    "out_gate": ((CROPS, C, PAIRS), BF),
    "tiles_a": ((PAIRS, 128), F32),
    "tiles_b": ((PAIRS, 128), F32),
    "tiles_z": ((PAIRS, 128), F32),
    "whole": ((512, 512), BF),
    "result": ((512, 512), BF),
    "hidden": ((HID, PAIRS), BF),
    "grad_gate_up": ((2 * HID, PAIRS), BF),
    "normed": ((C, PAIRS), BF),
    "upstream": ((C, PAIRS), BF),
    "updated": ((C, PAIRS), BF),
    "grad_branch": ((C, PAIRS), BF),
    "level": ((C, PAIRS), F32),
    "grad_rows": ((ROWS, 128), F32),
    "g_norm": ((LAYERS, 6, C, 128), F32),
}
for group, (_, pieces, piece) in (("early", EARLY), ("late", LATE)):
    SCRATCH.update({
        group + "_share": ((pieces * piece, 128), BF),
        group + "_sibling": ((pieces * piece, 128), BF),
        group + "_pieces": ((pieces, piece, 128), BF),
        group + "_landed": ((DEVICES // 2, piece, 128), BF),
        group + "_summed": ((pieces, piece, 128), BF),
    })


def prepare_triangle(r, layer):
    for index in range(6):
        row = r["norms_in"][index, layer : layer + 1, :]
        r["norms"][layer, index] = jnp.broadcast_to(row, (C, C)).T
    for matrix in range(5):
        weight = r["triangle"][layer, matrix]
        r["five"][layer, matrix * C : matrix * C + C, :] = weight.T.astype(BF)
        r["five_n"][layer, :, matrix * C : matrix * C + C] = weight.astype(BF)
    r["out_t"][layer] = r["triangle"][layer, 5].T.astype(BF)
    r["out_n"][layer] = r["triangle"][layer, 5].astype(BF)


def prepare_transition(r, layer):
    for matrix in range(2):
        for block in range(4):
            lanes = slice(block * C, block * C + C)
            rows = slice(matrix * HID + block * C, matrix * HID + block * C + C)
            weight = r["expand_in"][layer, matrix, :, lanes]
            r["expand_t"][layer, rows, :] = weight.T.astype(BF)
            r["expand"][layer, :, rows] = weight.astype(BF)
    for block in range(4):
        rows = slice(block * C, block * C + C)
        weight = r["shrink_in"][layer, rows, :]
        r["shrink_t"][layer, :, rows] = weight.T.astype(BF)
        r["shrink"][layer, rows, :] = weight.astype(BF)


def prepare_mask(r, place):
    pair = lax.broadcasted_iota(jnp.int32, (1, PAIRS), 1)
    tile, lane = pair // 128, lax.rem(pair, 128)
    first = place.row * 32 + lane // 64 * TILES + tile
    second = place.col * 64 + lax.rem(lane, 64)
    last = jnp.maximum(first, second)
    for crop in range(CROPS):
        r["mask"][crop] = jnp.clip(r["lengths"][crop] - last, 0, 1).astype(F32)


def for_crops(visit):
    def run(crop, carry):
        visit(crop)
        return carry

    lax.fori_loop(0, CROPS, run, 0)


def between_crops(visit, rest):
    def run(crop):
        visit(crop)
        pl.when(crop == 0)(rest)

    for_crops(run)


def for_steps(visit):
    def run(step, carry):
        visit(step)
        return carry

    lax.fori_loop(0, CHUNKS, run, 0)


def window_kernel(*refs):
    names = INPUTS + OUTPUTS + tuple(SCRATCH)
    r = dict(zip(names, refs))
    send_sem, recv_sem, sum_sem, load_sem, store_sem = refs[len(names) :]
    place = Place()
    loads = [
        pltpu.make_async_copy(r[far], r[near], load_sem.at[index])
        for index, (far, near) in enumerate(
            (("expand_far", "expand_in"), ("shrink_far", "shrink_in"), ("cotangent_far", "cotangent"))
        )
    ]
    for load in loads:
        load.start()

    barrier = pltpu.get_barrier_semaphore()
    for offset in OFFSETS:
        pl.semaphore_signal(barrier, inc=1, device_id=place.at(offset), device_id_type=MESH)

    early, late = Sum("early", EARLY, place, r, sum_sem.at[0]), Sum("late", LATE, place, r, sum_sem.at[1])

    def sent(kind, crop, index):
        exchange_wait(r[kind].at[crop], send_sem.at[index + crop])

    def second_sent(kind, crop, index):
        if not isinstance(crop, int):
            pl.when(crop == 1)(lambda: sent(kind, 1, index))
        elif crop:
            sent(kind, 1, index)

    def begin(kind, crop, recv, index, alone=False):
        if alone and not isinstance(crop, int):
            pl.when(crop == 1)(lambda: sent(kind, 0, index))
        elif alone and crop:
            sent(kind, 0, index)
        exchange_start(place, r[kind].at[crop], recv, send_sem.at[index + crop], recv_sem.at[index + crop])

    def project(layer, crop, step, x):
        project_step(
            x, r["mask"][crop, :, lanes_of(step)], r["five"].at[layer], Norms(r["norms"], layer), r["tiles_a"], r["tiles_b"],
            r["gate"].at[layer, crop], step,
        )

    def send_sides(layer, crop):
        if layer:
            sent("send_wide", crop, 0)
        pack_tiles(r["tiles_a"], r["send_wide"].at[crop], 0)
        pack_tiles(r["tiles_b"], r["send_wide"].at[crop], TILES)
        begin("send_wide", crop, r["recv_ab"].at[crop], layer * 8)

    def update(layer, crop, step):
        lanes = lanes_of(step)
        gate = r["gate"][layer, crop, :, lanes].astype(F32)
        gains = Norms(r["norms"], layer)
        parts = update_step(
            r["x"][layer, crop, :, lanes], gate, gather_tiles(r["tiles_z"], step), r["out_t"].at[layer], r["expand_t"].at[layer], gains
        )
        return gate, gains, parts

    def back(layer, crop, step, upstream, gate, gains, parts, hidden_parts):
        lanes = lanes_of(step)
        weights = (r["shrink"].at[layer], r["expand"].at[layer], r["out_n"].at[layer])
        middle, out_gate, grad_z = back_step(
            upstream, parts, hidden_parts, gate, weights, gains, r, lanes, r["g_norm"].at[layer]
        )
        r["mid"][crop, :, lanes] = middle
        r["out_gate"][crop, :, lanes] = out_gate
        scatter_tiles(r["tiles_z"], step, grad_z)

    def project_back(layer, crop, step):
        lanes = lanes_of(step)
        return project_back_step(
            r["x"][layer, crop, :, lanes], r["mask"][crop, :, lanes], gather_tiles(r["tiles_a"], step), gather_tiles(r["tiles_b"], step),
            r["out_gate"][crop, :, lanes], r["mid"][crop, :, lanes], r["five"].at[layer], r["five_n"].at[layer],
            Norms(r["norms"], layer), (layer, r["grad_rows"], r["g_norm"].at[layer]),
        )

    def send_grad_z(layer, crop):
        if layer:
            second_sent("send_slim", crop, 10)
        else:
            sent("send_slim", crop, 12)
        pack_tiles(r["tiles_z"], r["send_slim"].at[crop], 0)
        begin("send_slim", crop, r["recv_dz"].at[crop], layer * 8 + 4)

    prepare_mask(r, place)
    prepare_triangle(r, 0)

    def first(crop):
        def steps(step):
            x = load_pairs(r["pair"].at[crop], step)
            r["x"][0, crop, :, lanes_of(step)] = x
            project(0, crop, step, x)

        for_steps(steps)

        @pl.when(crop == 0)
        def _():
            pl.semaphore_wait(barrier, DEVICES - 1)

        send_sides(0, crop)

    for_crops(first)
    for load in loads:
        load.wait()
    prepare_transition(r, 0)
    for layer in range(1, LAYERS):
        prepare_triangle(r, layer)
        prepare_transition(r, layer)
    zero(r["grad_rows"], r["g_norm"])

    def store(name, crop):
        near, far = r[name].at[crop], r[name + "_far"].at[crop]
        pltpu.make_async_copy(near, far, store_sem.at[STORES.index(name) * CROPS + crop]).start()

    def products(layer, crop):
        recv = r["recv_ab"].at[crop]
        exchange_wait(recv, recv_sem.at[layer * 8 + crop])
        if layer:
            second_sent("send_slim", crop, 2)
        join(recv, r["left"].at[layer, crop], r["right"].at[layer, crop], r["whole"], r["send_slim"].at[crop])
        begin("send_slim", crop, r["recv_z"].at[layer, crop], layer * 8 + 2, alone=True)

    def onward(crop):
        recv = r["recv_z"].at[0, crop]
        exchange_wait(recv, recv_sem.at[2 + crop])
        unpack_tiles(recv, 0, r["tiles_z"])

        def forward(step):
            gate, gains, parts = update(0, crop, step)
            x_new = parts[4] + dot(r["shrink_t"][0], swiglu(parts[-1])[2])
            r["x"][1, crop, :, lanes_of(step)] = x_new
            project(1, crop, step, x_new)

        for_steps(forward)
        send_sides(1, crop)

    def turn(crop):
        recv = r["recv_z"].at[1, crop]
        exchange_wait(recv, recv_sem.at[10 + crop])
        unpack_tiles(recv, 0, r["tiles_z"])

        def steps(step):
            gate, gains, parts = update(1, crop, step)
            r["level"][:, lanes_of(step)] = parts[4]
            back(1, crop, step, load_pairs(r["cotangent"].at[crop], step), gate, gains, parts, swiglu(parts[-1]))

        for_steps(steps)
        send_grad_z(1, crop)

    def after_turn(crop):
        weight_grads(1, r, r["grad_rows"])

        def steps(step):
            lanes = lanes_of(step)
            store_pairs(r["level"][:, lanes] + dot(r["shrink_t"][1], r["hidden"][:, lanes]), step, r["pair_out"].at[crop])

        for_steps(steps)
        store("pair_out", crop)

    def products_back(layer, crop):
        recv = r["recv_dz"].at[crop]
        exchange_wait(recv, recv_sem.at[layer * 8 + 4 + crop])
        if layer:
            sent("send_wide", crop, 8)
        else:
            second_sent("send_wide", crop, 14)
        join_back(recv, r["left"].at[layer, crop], r["right"].at[layer, crop], r["whole"], r["result"], r["send_wide"].at[crop])
        begin("send_wide", crop, r["recv_ab"].at[crop], layer * 8 + 6, alone=layer == 1)

    def receive_sides_grad(layer, crop):
        recv = r["recv_ab"].at[crop]
        exchange_wait(recv, recv_sem.at[layer * 8 + 6 + crop])
        unpack_tiles(recv, 0, r["tiles_a"])
        unpack_tiles(recv, TILES, r["tiles_b"])

    def deep(crop):
        receive_sides_grad(1, crop)
        unpack_tiles(r["recv_z"].at[0, crop], 0, r["tiles_z"])

        def steps(step):
            upstream = project_back(1, crop, step)
            gate, gains, parts = update(0, crop, step)
            back(0, crop, step, upstream, gate, gains, parts, swiglu(parts[-1]))

        for_steps(steps)
        send_grad_z(0, crop)

    def last(crop):
        receive_sides_grad(0, crop)
        for_steps(lambda step: store_pairs(project_back(0, crop, step), step, r["pair_grad"].at[crop]))
        store("pair_grad", crop)

    for_crops(lambda crop: products(0, crop))
    for_crops(onward)
    for_crops(lambda crop: products(1, crop))

    def after_deep():
        weight_grads(0, r, r["grad_rows"])

    def after_both():
        after_deep()
        early.share()

    between_crops(turn, lambda: after_turn(0))
    between_crops(lambda crop: products_back(1, crop), lambda: after_turn(1))
    between_crops(deep, after_deep)
    between_crops(lambda crop: products_back(0, crop), after_both)
    between_crops(last, early.scatter)
    for layer in range(LAYERS):
        for index in range(6):
            row = NORM_ROW + index * LAYERS + layer
            r["grad_rows"][row : row + 1, :] = jnp.sum(r["g_norm"][layer, index].T, axis=0, keepdims=True)
    late.share()
    late.scatter()
    early.spread()
    late.spread()
    early.gather()
    late.gather()
    early.finish()
    late.finish()
    for crop in range(CROPS):
        sent("send_slim", crop, 4)
        sent("send_wide", crop, 6)
        for name in STORES:
            near, far = r[name].at[crop], r[name + "_far"].at[crop]
            pltpu.make_async_copy(near, far, store_sem.at[STORES.index(name) * CROPS + crop]).wait()


class Sum:
    def __init__(self, name, group, place, r, sem):
        self.first, self.count, self.piece = group
        self.half = self.count * self.piece
        self.place, self.r, self.sem = place, r, sem
        self.share_ref, self.sibling, self.pieces, self.landed, self.summed = (
            r[name + suffix] for suffix in ("_share", "_sibling", "_pieces", "_landed", "_summed")
        )
        self.owner = place.chip < self.count
        self.offsets = [offset for offset in OFFSETS if offset[3] == 0]

    def rows(self, core):
        return pl.ds(pl.multiple_of(self.first + core * self.half, 16), self.half)

    def swap(self, source, target, index):
        return pltpu.make_async_remote_copy(
            source, target, self.sem.at[index], self.sem.at[index + 1], device_id=self.place.at((0, 0, 0, 1)), device_id_type=MESH
        )

    def push(self, source, target, index, offset):
        pltpu.make_async_remote_copy(
            source, target, self.sem.at[index], self.sem.at[index + 1], device_id=self.place.at(offset), device_id_type=MESH
        ).start()

    def wait(self, ref, count, index):
        some = ref.at[pl.ds(0, count)]
        pltpu.make_async_copy(some, some, self.sem.at[index]).wait()

    def share(self):
        self.share_ref[...] = self.r["grad_rows"][self.rows(1 - self.place.core), :].astype(BF)
        self.swap(self.share_ref, self.sibling, 0).start()

    def scatter(self):
        self.swap(self.share_ref, self.sibling, 0).wait()
        both = self.r["grad_rows"][self.rows(self.place.core), :] + self.sibling[...].astype(F32)
        self.pieces[...] = both.astype(BF).reshape(self.count, self.piece, 128)
        for offset in self.offsets:
            row, col = self.place.at(offset)
            piece = row // 2 * COLS + col

            @pl.when(piece < self.count)
            def _():
                self.push(self.pieces.at[piece], self.landed.at[self.place.chip], 2, offset)

    def spread(self):
        chip, chips = self.place.chip, DEVICES // 2

        @pl.when(self.owner)
        def _():
            self.landed[chip] = self.pieces[chip]
            self.wait(self.landed, chips - 1, 3)

            self.summed[chip] = jnp.sum(self.landed[...].astype(F32), axis=0).astype(BF)
            for offset in self.offsets:
                self.push(self.summed.at[chip], self.summed.at[chip], 4, offset)

    def gather(self):
        @pl.when(self.owner)
        def _():
            self.wait(self.pieces, self.count - 1, 2)
            self.wait(self.landed, DEVICES // 2 - 1, 4)
            self.wait(self.summed, self.count - 1, 5)

        @pl.when(jnp.logical_not(self.owner))
        def _():
            self.wait(self.pieces, self.count, 2)
            self.wait(self.summed, self.count, 5)

        own = self.r["total"].at[self.rows(self.place.core)]
        own[...] = self.summed[...].reshape(self.half, 128)
        self.swap(own, own, 6).start()

    def finish(self):
        own = self.r["total"].at[self.rows(self.place.core)]
        self.swap(own, own, 6).wait()


def window(outs, lengths, *args):
    return pl.pallas_call(
        window_kernel,
        out_shape=[jax.ShapeDtypeStruct(shape, dtype) for shape, dtype in outs],
        in_specs=[pl.BlockSpec(memory_space=pltpu.SMEM)] + [pl.BlockSpec(memory_space=pltpu.VMEM)] * (len(args) - FAR)
        + [pl.BlockSpec(memory_space=pl.ANY)] * FAR,
        out_specs=[pl.BlockSpec(memory_space=pl.ANY)] * 2 + [pl.BlockSpec(memory_space=pltpu.VMEM)],
        scratch_shapes=[pltpu.VMEM(shape, dtype) for shape, dtype in SCRATCH.values()]
        + [pltpu.SemaphoreType.DMA((8 * LAYERS,))] * 2
        + [pltpu.SemaphoreType.DMA((2, 8)), pltpu.SemaphoreType.DMA((FAR,)), pltpu.SemaphoreType.DMA((2 * CROPS,))],
        compiler_params=pltpu.CompilerParams(collective_id=1, has_side_effects=True, vmem_limit_bytes=VMEM_LIMIT),
        name="window",
    )(lengths, *args)


def adamw(gradient, weight, first, second, clip_factor, step_rate, decay_rate, outs):
    clipped = gradient * clip_factor
    moment = BETA_ONE * first + (1.0 - BETA_ONE) * clipped
    square = BETA_TWO * second + (1.0 - BETA_TWO) * clipped * clipped
    correct_one = 1.0 - BETA_ONE**STEP
    correct_two = 1.0 - BETA_TWO**STEP
    update = moment * (step_rate / correct_one) / (jnp.sqrt(square * (1.0 / correct_two)) + ADAM_EPS)
    renewed = weight * (1.0 - step_rate * decay_rate) - update
    for (ref, place), value in zip(outs, (moment, square, renewed, renewed)):
        ref[place] = value.astype(ref.dtype)


def settle_kernel(*refs):
    total_in, ins = refs[0], refs[1:13]
    outs, norm_ref = refs[13:28], refs[28]
    total, held, made = refs[29], refs[30:42], refs[42:57]
    total_sem, in_sem, out_sem = refs[57:]

    first = pltpu.make_async_copy(total_in, total, total_sem)
    first.start()
    loads = {}
    for part in range(LAYERS):
        for index in range(9):
            loads[part, index] = pltpu.make_async_copy(ins[index].at[part], held[index].at[part], in_sem.at[part * 9 + index])
            loads[part, index].start()
    for index in range(9, 12):
        loads[0, index] = pltpu.make_async_copy(ins[index], held[index], in_sem.at[9 * LAYERS + index - 9])
        loads[0, index].start()
    first.wait()

    def square(step, carry):
        rows = total[pl.ds(pl.multiple_of(step * 464, 16), 464), :].astype(F32)
        return carry + jnp.sum((rows * rows).reshape(58, 8, 128), axis=0)

    squares = lax.fori_loop(0, ROWS // 464, square, jnp.zeros((8, 128), F32))
    grad_norm = jnp.sqrt(jnp.sum(jnp.sum(squares, axis=1, keepdims=True), axis=0, keepdims=True))
    norm_ref[...] = grad_norm
    factor = jnp.minimum(1.0, CLIP / (grad_norm + 1e-06))
    stores = []

    def store(index, part):
        pieces = (made[index], outs[index]) if part is None else (made[index].at[part], outs[index].at[part])
        copy = pltpu.make_async_copy(*pieces, out_sem.at[len(stores)])
        copy.start()
        stores.append(copy)

    def run(kind, start, size, place):
        values = [ref[place] for ref in held[3 * kind : 3 * kind + 3]]
        gradient = total[start : start + size, :].astype(F32)
        adamw(gradient, *values, factor, RATE, DECAY_RATE, [(ref, place) for ref in made[4 * kind : 4 * kind + 4]])

    for part in range(LAYERS):
        for kind in range(3):
            for index in range(3):
                loads[part, 3 * kind + index].wait()
            for block in range((6, 8, 4)[kind]):
                if kind == 0:
                    run(kind, triangle_start(part, block), C, (part, block))
                elif kind == 1:
                    place = (part, block // 4, slice(None), slice(block % 4 * C, block % 4 * C + C))
                    run(kind, EXPAND_ROW + (part * 8 + block) * C, C, place)
                else:
                    run(kind, SHRINK_ROW + part * HID + block * C, C, (part, slice(block * C, block * C + C)))
            for index in range(4):
                store(4 * kind + index, part)
    for index in range(9, 12):
        loads[0, index].wait()
    rows = total[NORM_ROW : NORM_ROW + 16, :].astype(F32)
    for index in range(6):
        values = [ref[index] for ref in held[9:12]]
        outputs = [(ref, index) for ref in made[12:15]]
        adamw(rows[index * LAYERS : index * LAYERS + LAYERS], *values, factor, NORM_RATE, 0.0, outputs)
    for index in range(12, 15):
        store(index, None)
    for copy in stores:
        copy.wait()


def settle(total, kinds):
    arrays = [array for kind in kinds for array in kind]
    made = [(kind[0].shape, dtype) for kind in kinds[:3] for dtype in (F32, F32, F32, BF)] + [(kinds[3][0].shape, F32)] * 3
    anywhere = pl.BlockSpec(memory_space=pl.ANY)
    shapes = [jax.ShapeDtypeStruct(*shape) for shape in made] + [jax.ShapeDtypeStruct((1, 1), F32)]
    return pl.pallas_call(
        settle_kernel,
        out_shape=shapes,
        in_specs=[anywhere] * (1 + len(arrays)),
        out_specs=[anywhere] * (len(shapes) - 1) + [pl.BlockSpec(memory_space=pltpu.VMEM)],
        scratch_shapes=[pltpu.VMEM(total.shape, total.dtype)]
        + [pltpu.VMEM(array.shape, array.dtype) for array in arrays]
        + [pltpu.VMEM(*shape) for shape in made]
        + [pltpu.SemaphoreType.DMA]
        + [pltpu.SemaphoreType.DMA((9 * LAYERS + 3,)), pltpu.SemaphoreType.DMA((12 * LAYERS + 3,))],
        compiler_params=pltpu.CompilerParams(vmem_limit_bytes=VMEM_LIMIT),
        name="settle",
    )(total, *arrays)


def local(
    pair_in, lengths, pair_cotangent, triangle_weights, expand_weights, shrink_weights, norm_params, triangle_first,
    triangle_second, expand_first, expand_second, shrink_first, shrink_second, norm_first, norm_second,
):
    norms = [jnp.swapaxes(array, 0, 1) for array in (norm_params, norm_first, norm_second)]
    outs = [(pair_in.shape, BF), (pair_in.shape, F32), ((ROWS, 128), BF)]
    pair_out, pair_grad, total = window(
        outs, lengths, pair_in, triangle_weights, norms[0], pair_cotangent, expand_weights, shrink_weights
    )
    kinds = (
        (triangle_weights, triangle_first, triangle_second),
        (expand_weights, expand_first, expand_second),
        (shrink_weights, shrink_first, shrink_second),
        norms,
    )
    new = settle(total, kinds)
    moments = [new[4 * kind + place] for kind in range(3) for place in range(3)]
    norms_new = [jnp.swapaxes(array, 0, 1) for array in new[12:15]]
    copies = [new[4 * kind + 3] for kind in range(3)]
    return (pair_out, pair_grad, *moments, *norms_new, *copies, new[15].reshape(()))


def solution(mesh):
    pair = P(None, "row", "col", None)
    return jax.shard_map(
        local,
        mesh=mesh,
        in_specs=(pair, P(), pair) + (P(),) * 12,
        out_specs=(pair, pair) + (P(),) * 16,
        check_vma=False,
    )
```

```python
import jax
import jax.numpy as jnp
from jax import lax
from jax.experimental import pallas as pl
from jax.experimental.pallas import tpu as pltpu
from jax.sharding import PartitionSpec as P

LAYERS = 2
STEP = 10
CROPS = 2
COLS = 8
DEVICES = 128

EPS_NORM = 1e-05
BETA_ONE = 0.9
BETA_TWO = 0.999
ADAM_EPS = 1e-08
RATE = 0.1
NORM_RATE = 0.5
DECAY_RATE = 0.01
CLIP = 1.0

MESH = pl.DeviceIdType.MESH
BF = jnp.bfloat16
F32 = jnp.float32

C = 128
HID = 512
TILES = 16
PAIRS = 2048
WIDE = 1024
CHUNKS = PAIRS // WIDE
PER = WIDE // 128
VMEM_LIMIT = 61 << 20

EXPAND_ROW = 7 * C
SHRINK_ROW = EXPAND_ROW + LAYERS * 2 * HID
LATE_ROW = SHRINK_ROW + LAYERS * HID
NORM_ROW = LATE_ROW + 5 * C
EARLY = (0, 62, 32)
LATE = (LATE_ROW, 21, 16)
ROWS = LATE_ROW + 2 * 21 * 16


def triangle_start(layer, matrix):
    if layer == 1:
        return matrix * C
    return 6 * C if matrix == 5 else LATE_ROW + matrix * C


def triangle_rows(layer, matrix):
    return pl.ds(triangle_start(layer, matrix), C)


def expand_rows(layer, matrix, block):
    return pl.ds(EXPAND_ROW + ((layer * 2 + matrix) * 4 + block) * C, C)


def shrink_rows(layer):
    return pl.ds(SHRINK_ROW + layer * HID, HID)


def dot(left, right):
    return lax.dot_general(left, right, (((1,), (0,)), ((), ())), preferred_element_type=F32)


def dot_nt(left, right):
    return lax.dot_general(left, right, (((1,), (1,)), ((), ())), preferred_element_type=F32)


def dot_tn(left, right):
    return lax.dot_general(left, right, (((0,), (0,)), ((), ())), preferred_element_type=F32)


def sigmoid(v):
    return 0.5 * jnp.tanh(0.5 * v) + 0.5


KEPT = ("hidden", "grad_gate_up", "normed", "upstream", "updated", "grad_branch")


def mean_rows(v):
    return jnp.sum(v, axis=0, keepdims=True) * (1.0 / C)


def normalize(v):
    centered = v - mean_rows(v)
    scale = lax.rsqrt(mean_rows(centered * centered) + EPS_NORM)
    return centered * scale, scale


def normalize_back(grad, gain, hat, scale):
    grad_hat = grad * gain
    return scale * (grad_hat - mean_rows(grad_hat) - hat * mean_rows(grad_hat * hat))


def lanes_of(step):
    return pl.ds(pl.multiple_of(step * WIDE, WIDE), WIDE)


def scatter_tiles(scratch, step, value):
    for part in range(PER):
        scratch[pl.ds(step * PER + part, C, stride=TILES), :] = value[:, part * 128 : part * 128 + 128]


def gather_tiles(scratch, step):
    return jnp.concatenate(
        [scratch[pl.ds(step * PER + part, C, stride=TILES), :] for part in range(PER)], axis=1
    )


def pack_tiles(scratch, send, offset):
    send[:, offset : offset + TILES, :] = scratch[...].astype(BF).reshape(C, TILES, 128)


def unpack_tiles(recv, offset, scratch):
    scratch[...] = recv[:, offset : offset + TILES, :].reshape(PAIRS, 128).astype(F32)


def swap_halves(first, second):
    low = jnp.concatenate([first[:, :64], second[:, :64]], axis=1)
    high = jnp.concatenate([first[:, 64:], second[:, 64:]], axis=1)
    return low, high


def assemble(recv, offset, whole):
    for row in range(16):
        base = row * 32
        for pair in range(4):
            low, high = swap_halves(
                recv[row * 8 + 2 * pair, offset : offset + TILES, :],
                recv[row * 8 + 2 * pair + 1, offset : offset + TILES, :],
            )
            whole[base : base + 16, pair * 128 : pair * 128 + 128] = low
            whole[base + 16 : base + 32, pair * 128 : pair * 128 + 128] = high


def disassemble(whole, send, offset):
    for row in range(16):
        base = row * 32
        for pair in range(4):
            first, second = swap_halves(
                whole[base : base + 16, pair * 128 : pair * 128 + 128],
                whole[base + 16 : base + 32, pair * 128 : pair * 128 + 128],
            )
            send[row * 8 + 2 * pair, offset : offset + TILES, :] = first
            send[row * 8 + 2 * pair + 1, offset : offset + TILES, :] = second


def load_pairs(pair_ref, step):
    parts = []
    for part in range(PER):
        tile = step * PER + part
        parts.append(jnp.concatenate([pair_ref[tile], pair_ref[tile + TILES]], axis=0).astype(F32).T)
    return jnp.concatenate(parts, axis=1)


def store_pairs(value, step, out_ref):
    for part in range(PER):
        rows = value[:, part * 128 : part * 128 + 128].T
        out_ref[step * PER + part] = rows[:64].astype(out_ref.dtype)
        out_ref[step * PER + part + TILES] = rows[64:].astype(out_ref.dtype)


def project_step(x, mask, five, norms, scratch_a, scratch_b, gate_ref, step):
    hat, _ = normalize(x)
    normed = (hat * norms[0] + norms[1]).astype(BF)
    projected = dot(five[...], normed)
    left = mask * sigmoid(projected[:C]) * projected[C : 2 * C]
    right = mask * sigmoid(projected[2 * C : 3 * C]) * projected[3 * C : 4 * C]
    scatter_tiles(scratch_a, step, left)
    scatter_tiles(scratch_b, step, right)
    gate_ref[:, lanes_of(step)] = sigmoid(projected[4 * C :]).astype(BF)


def update_step(x, gate, z, out_t, expand_t, norms):
    z_hat, z_scale = normalize(z)
    updated = (z_hat * norms[2] + norms[3]).astype(BF)
    branch = dot(out_t[...], updated)
    middle = x + gate * branch
    mid_hat, mid_scale = normalize(middle)
    normed = (mid_hat * norms[4] + norms[5]).astype(BF)
    gate_up = dot(expand_t[...], normed)
    return (z_hat, z_scale, updated, branch, middle, mid_hat, mid_scale, normed, gate_up)


def swiglu(gate_up):
    gate_half = gate_up[:HID]
    sig = sigmoid(gate_half)
    silu = gate_half * sig
    return (sig, silu, (silu * gate_up[HID:]).astype(BF))


def back_step(upstream, parts, hidden_parts, gate, weights, norms, kept, lanes, g_norm):
    z_hat, z_scale, updated, branch, middle, mid_hat, mid_scale, normed, gate_up = parts
    sig, silu, hidden = hidden_parts
    shrink, expand, out_n = weights
    upstream_low = upstream.astype(BF)
    grad_hidden = dot(shrink[...], upstream_low)
    grad_gate = (grad_hidden * gate_up[HID:] * (sig + silu * (1.0 - sig))).astype(BF)
    grad_up = (grad_hidden * silu).astype(BF)
    grad_gate_up = jnp.concatenate([grad_gate, grad_up], axis=0)
    grad_normed = dot(expand[...], grad_gate_up)
    add_norm(g_norm, 4, grad_normed * mid_hat, grad_normed)
    grad_middle = upstream + normalize_back(grad_normed, norms[4], mid_hat, mid_scale)
    scaled = grad_middle * gate
    grad_branch = scaled.astype(BF)
    grad_out_gate = (scaled * branch * (1.0 - gate)).astype(BF)
    grad_updated = dot(out_n[...], grad_branch)
    add_norm(g_norm, 2, grad_updated * z_hat, grad_updated)
    grad_z = normalize_back(grad_updated, norms[2], z_hat, z_scale)
    for name, value in zip(KEPT, (hidden, grad_gate_up, normed, upstream_low, updated, grad_branch)):
        kept[name][:, lanes] = value
    return (grad_middle, grad_out_gate, grad_z)


def weight_grads(layer, kept, grad_rows):
    def steps(step):
        hidden, grad_gate_up, normed, upstream, updated, grad_branch = (kept[name][:, lanes_of(step)] for name in KEPT)
        grad_rows[shrink_rows(layer), :] += dot_nt(hidden, upstream)
        term = dot_nt(normed, grad_gate_up)
        for block in range(8):
            grad_rows[expand_rows(layer, block // 4, block % 4), :] += term[:, block * C : block * C + C]
        grad_rows[triangle_rows(layer, 5), :] += dot_nt(updated, grad_branch)

    for_steps(steps)


def add_norm(g_norm, index, gain_term, bias_term):
    for place, term in ((index, gain_term), (index + 1, bias_term)):
        total = term[:, :128]
        for part in range(1, PER):
            total = total + term[:, part * 128 : part * 128 + 128]
        g_norm[place] += total


def project_back_step(
    x, mask, grad_left, grad_right, grad_out_gate, grad_middle, five, five_n, norms, grads
):
    layer, grad_rows, g_norm = grads
    hat, scale = normalize(x)
    normed = (hat * norms[0] + norms[1]).astype(BF)
    projected = dot(five[: 4 * C, :], normed)
    pieces = []
    for grad, base in ((grad_left, 0), (grad_right, 2 * C)):
        sig = sigmoid(projected[base : base + C])
        masked = grad * mask * sig
        pieces.append((masked * projected[base + C : base + 2 * C] * (1.0 - sig)).astype(BF))
        pieces.append(masked.astype(BF))
    pieces.append(grad_out_gate)
    grad_projected = jnp.concatenate(pieces, axis=0)
    term = dot_nt(normed, grad_projected)
    for matrix in range(5):
        grad_rows[triangle_rows(layer, matrix), :] += term[:, matrix * C : matrix * C + C]
    grad_normed = dot(five_n[...], grad_projected)
    add_norm(g_norm, 0, grad_normed * hat, grad_normed)
    return grad_middle + normalize_back(grad_normed, norms[0], hat, scale)


class Norms:
    def __init__(self, ref, layer):
        self.ref, self.layer = ref, layer

    def __getitem__(self, index):
        value = self.ref[self.layer, index]
        return jnp.concatenate([value] * PER, axis=1)


def zero(*refs):
    for ref in refs:
        ref[...] = jnp.zeros_like(ref)


def distance(offset):
    return sum(min(step, 4 - step) for step in offset[:3])


OFFSETS = [(i % 4, i // 4 % 4, i // 16 % 4, i // 64) for i in range(1, 128)]
OFFSETS = [o for _, _, o in sorted((-distance(o), (i * 53 + 17) % 127, o) for i, o in enumerate(OFFSETS))]


class Place:
    def __init__(self):
        self.row, self.col = lax.axis_index("row"), lax.axis_index("col")
        self.me = self.row * COLS + self.col
        self.core = lax.rem(self.row, 2)
        x, y, z = lax.rem(self.row // 2, 4), self.row // 8 * 2 + lax.rem(self.col, 2), self.col // 2
        self.chip = self.row // 2 * COLS + self.col
        xs = [lax.rem(x + step, 4) * 2 for step in range(4)]
        ys = [lax.rem(y + step, 4) for step in range(4)]
        zs = [lax.rem(z + step, 4) * 2 for step in range(4)]
        cores = [self.core, 1 - self.core]
        highs, lows = [v // 2 * 8 for v in ys], [lax.rem(v, 2) for v in ys]
        self.rows = {(a, b, d): highs[b] + xs[a] + cores[d] for a in range(4) for b in range(4) for d in range(2)}
        self.cols = {(b, c): zs[c] + lows[b] for b in range(4) for c in range(4)}

    def at(self, offset):
        a, b, c, d = offset
        return self.rows[a, b, d], self.cols[b, c]


def exchange_start(place, send, recv, send_sem, recv_sem):
    for offset in OFFSETS:
        row, col = place.at(offset)
        pltpu.make_async_remote_copy(
            send.at[row * COLS + col], recv.at[place.me], send_sem, recv_sem, device_id=(row, col), device_id_type=MESH
        ).start()
    recv[place.me] = send[place.me]


def exchange_wait(ref, sem):
    others = pl.ds(0, DEVICES - 1)
    pltpu.make_async_copy(ref.at[others], ref.at[others], sem).wait()


def join(recv, left, right, whole, send):
    assemble(recv, 0, left)
    assemble(recv, TILES, right)
    whole[...] = dot_nt(left[...], right[...]).astype(BF)
    disassemble(whole, send, 0)


def join_back(recv, left, right, whole, result, send):
    assemble(recv, 0, whole)
    result[...] = dot(whole[...], right[...]).astype(BF)
    disassemble(result, send, 0)
    result[...] = dot_tn(whole[...], left[...]).astype(BF)
    disassemble(result, send, TILES)


INPUTS = ("lengths", "pair", "triangle", "norms_in", "cotangent_far", "expand_far", "shrink_far")
FAR = 3
STORES = ("pair_out", "pair_grad")
OUTPUTS = ("pair_out_far", "pair_grad_far", "total")
SCRATCH = {
    "pair_out": ((CROPS, 32, 64, C), BF),
    "pair_grad": ((CROPS, 32, 64, C), F32),
    "cotangent": ((CROPS, 32, 64, C), BF),
    "expand_in": ((LAYERS, 2, C, HID), F32),
    "shrink_in": ((LAYERS, HID, C), F32),
    "mask": ((CROPS, 1, PAIRS), F32),
    "norms": ((LAYERS, 6, C, 128), F32),
    "five": ((LAYERS, 5 * C, C), BF),
    "five_n": ((LAYERS, C, 5 * C), BF),
    "out_t": ((LAYERS, C, C), BF),
    "out_n": ((LAYERS, C, C), BF),
    "expand_t": ((LAYERS, 2 * HID, C), BF),
    "expand": ((LAYERS, C, 2 * HID), BF),
    "shrink_t": ((LAYERS, C, HID), BF),
    "shrink": ((LAYERS, HID, C), BF),
    "x": ((LAYERS, CROPS, C, PAIRS), F32),
    "gate": ((LAYERS, CROPS, C, PAIRS), BF),
    "recv_ab": ((CROPS, C, 2 * TILES, 128), BF),
    "recv_z": ((LAYERS, CROPS, C, TILES, 128), BF),
    "recv_dz": ((CROPS, C, TILES, 128), BF),
    "send_wide": ((CROPS, C, 2 * TILES, 128), BF),
    "send_slim": ((CROPS, C, TILES, 128), BF),
    "left": ((LAYERS, CROPS, 512, 512), BF),
    "right": ((LAYERS, CROPS, 512, 512), BF),
    "mid": ((CROPS, C, PAIRS), F32),
    "out_gate": ((CROPS, C, PAIRS), BF),
    "tiles_a": ((PAIRS, 128), F32),
    "tiles_b": ((PAIRS, 128), F32),
    "tiles_z": ((PAIRS, 128), F32),
    "whole": ((512, 512), BF),
    "result": ((512, 512), BF),
    "hidden": ((HID, PAIRS), BF),
    "grad_gate_up": ((2 * HID, PAIRS), BF),
    "normed": ((C, PAIRS), BF),
    "upstream": ((C, PAIRS), BF),
    "updated": ((C, PAIRS), BF),
    "grad_branch": ((C, PAIRS), BF),
    "level": ((C, PAIRS), F32),
    "grad_rows": ((ROWS, 128), F32),
    "g_norm": ((LAYERS, 6, C, 128), F32),
}
for group, (_, pieces, piece) in (("early", EARLY), ("late", LATE)):
    SCRATCH.update({
        group + "_share": ((pieces * piece, 128), BF),
        group + "_sibling": ((pieces * piece, 128), BF),
        group + "_pieces": ((pieces, piece, 128), BF),
        group + "_landed": ((DEVICES // 2, piece, 128), BF),
        group + "_summed": ((pieces, piece, 128), BF),
    })


def prepare_triangle(r, layer):
    for index in range(6):
        row = r["norms_in"][index, layer : layer + 1, :]
        r["norms"][layer, index] = jnp.broadcast_to(row, (C, C)).T
    for matrix in range(5):
        weight = r["triangle"][layer, matrix]
        r["five"][layer, matrix * C : matrix * C + C, :] = weight.T.astype(BF)
        r["five_n"][layer, :, matrix * C : matrix * C + C] = weight.astype(BF)
    r["out_t"][layer] = r["triangle"][layer, 5].T.astype(BF)
    r["out_n"][layer] = r["triangle"][layer, 5].astype(BF)


def prepare_transition(r, layer):
    for matrix in range(2):
        for block in range(4):
            lanes = slice(block * C, block * C + C)
            rows = slice(matrix * HID + block * C, matrix * HID + block * C + C)
            weight = r["expand_in"][layer, matrix, :, lanes]
            r["expand_t"][layer, rows, :] = weight.T.astype(BF)
            r["expand"][layer, :, rows] = weight.astype(BF)
    for block in range(4):
        rows = slice(block * C, block * C + C)
        weight = r["shrink_in"][layer, rows, :]
        r["shrink_t"][layer, :, rows] = weight.T.astype(BF)
        r["shrink"][layer, rows, :] = weight.astype(BF)


def prepare_mask(r, place):
    pair = lax.broadcasted_iota(jnp.int32, (1, PAIRS), 1)
    tile, lane = pair // 128, lax.rem(pair, 128)
    first = place.row * 32 + lane // 64 * TILES + tile
    second = place.col * 64 + lax.rem(lane, 64)
    last = jnp.maximum(first, second)
    for crop in range(CROPS):
        r["mask"][crop] = jnp.clip(r["lengths"][crop] - last, 0, 1).astype(F32)


def for_crops(visit):
    def run(crop, carry):
        visit(crop)
        return carry

    lax.fori_loop(0, CROPS, run, 0)


def between_crops(visit, rest):
    def run(crop):
        visit(crop)
        pl.when(crop == 0)(rest)

    for_crops(run)


def for_steps(visit):
    def run(step, carry):
        visit(step)
        return carry

    lax.fori_loop(0, CHUNKS, run, 0)


def window_kernel(*refs):
    names = INPUTS + OUTPUTS + tuple(SCRATCH)
    r = dict(zip(names, refs))
    send_sem, recv_sem, sum_sem, load_sem, store_sem = refs[len(names) :]
    place = Place()
    loads = [
        pltpu.make_async_copy(r[far], r[near], load_sem.at[index])
        for index, (far, near) in enumerate(
            (("expand_far", "expand_in"), ("shrink_far", "shrink_in"), ("cotangent_far", "cotangent"))
        )
    ]
    for load in loads:
        load.start()

    barrier = pltpu.get_barrier_semaphore()
    for offset in OFFSETS:
        pl.semaphore_signal(barrier, inc=1, device_id=place.at(offset), device_id_type=MESH)

    early, late = Sum("early", EARLY, place, r, sum_sem.at[0]), Sum("late", LATE, place, r, sum_sem.at[1])

    def sent(kind, crop, index):
        exchange_wait(r[kind].at[crop], send_sem.at[index + crop])

    def second_sent(kind, crop, index):
        if not isinstance(crop, int):
            pl.when(crop == 1)(lambda: sent(kind, 1, index))
        elif crop:
            sent(kind, 1, index)

    def begin(kind, crop, recv, index, alone=False):
        if alone and not isinstance(crop, int):
            pl.when(crop == 1)(lambda: sent(kind, 0, index))
        elif alone and crop:
            sent(kind, 0, index)
        exchange_start(place, r[kind].at[crop], recv, send_sem.at[index + crop], recv_sem.at[index + crop])

    def project(layer, crop, step, x):
        project_step(
            x, r["mask"][crop, :, lanes_of(step)], r["five"].at[layer], Norms(r["norms"], layer), r["tiles_a"], r["tiles_b"],
            r["gate"].at[layer, crop], step,
        )

    def send_sides(layer, crop):
        if layer:
            second_sent("send_wide", crop, 0)
        pack_tiles(r["tiles_a"], r["send_wide"].at[crop], 0)
        pack_tiles(r["tiles_b"], r["send_wide"].at[crop], TILES)
        begin("send_wide", crop, r["recv_ab"].at[crop], layer * 8, alone=True)

    def update(layer, crop, step):
        lanes = lanes_of(step)
        gate = r["gate"][layer, crop, :, lanes].astype(F32)
        gains = Norms(r["norms"], layer)
        parts = update_step(
            r["x"][layer, crop, :, lanes], gate, gather_tiles(r["tiles_z"], step), r["out_t"].at[layer], r["expand_t"].at[layer], gains
        )
        return gate, gains, parts

    def back(layer, crop, step, upstream, gate, gains, parts, hidden_parts):
        lanes = lanes_of(step)
        weights = (r["shrink"].at[layer], r["expand"].at[layer], r["out_n"].at[layer])
        middle, out_gate, grad_z = back_step(
            upstream, parts, hidden_parts, gate, weights, gains, r, lanes, r["g_norm"].at[layer]
        )
        r["mid"][crop, :, lanes] = middle
        r["out_gate"][crop, :, lanes] = out_gate
        scatter_tiles(r["tiles_z"], step, grad_z)

    def project_back(layer, crop, step):
        lanes = lanes_of(step)
        return project_back_step(
            r["x"][layer, crop, :, lanes], r["mask"][crop, :, lanes], gather_tiles(r["tiles_a"], step), gather_tiles(r["tiles_b"], step),
            r["out_gate"][crop, :, lanes], r["mid"][crop, :, lanes], r["five"].at[layer], r["five_n"].at[layer],
            Norms(r["norms"], layer), (layer, r["grad_rows"], r["g_norm"].at[layer]),
        )

    def send_grad_z(layer, crop):
        if layer:
            second_sent("send_slim", crop, 10)
        else:
            sent("send_slim", crop, 12)
        pack_tiles(r["tiles_z"], r["send_slim"].at[crop], 0)
        begin("send_slim", crop, r["recv_dz"].at[crop], layer * 8 + 4)

    prepare_mask(r, place)
    prepare_triangle(r, 0)

    def first(crop):
        def steps(step):
            x = load_pairs(r["pair"].at[crop], step)
            r["x"][0, crop, :, lanes_of(step)] = x
            project(0, crop, step, x)

        for_steps(steps)

        @pl.when(crop == 0)
        def _():
            pl.semaphore_wait(barrier, DEVICES - 1)

        send_sides(0, crop)

    for_crops(first)
    for load in loads:
        load.wait()
    prepare_transition(r, 0)
    for layer in range(1, LAYERS):
        prepare_triangle(r, layer)
        prepare_transition(r, layer)
    zero(r["grad_rows"], r["g_norm"])

    def store(name, crop):
        near, far = r[name].at[crop], r[name + "_far"].at[crop]
        pltpu.make_async_copy(near, far, store_sem.at[STORES.index(name) * CROPS + crop]).start()

    def products(layer, crop):
        recv = r["recv_ab"].at[crop]
        exchange_wait(recv, recv_sem.at[layer * 8 + crop])
        if layer:
            second_sent("send_slim", crop, 2)
        join(recv, r["left"].at[layer, crop], r["right"].at[layer, crop], r["whole"], r["send_slim"].at[crop])
        begin("send_slim", crop, r["recv_z"].at[layer, crop], layer * 8 + 2, alone=True)

    def onward(crop):
        recv = r["recv_z"].at[0, crop]
        exchange_wait(recv, recv_sem.at[2 + crop])
        unpack_tiles(recv, 0, r["tiles_z"])

        def forward(step):
            gate, gains, parts = update(0, crop, step)
            x_new = parts[4] + dot(r["shrink_t"][0], swiglu(parts[-1])[2])
            r["x"][1, crop, :, lanes_of(step)] = x_new
            project(1, crop, step, x_new)

        for_steps(forward)
        send_sides(1, crop)

    def turn(crop):
        recv = r["recv_z"].at[1, crop]
        exchange_wait(recv, recv_sem.at[10 + crop])
        unpack_tiles(recv, 0, r["tiles_z"])

        def steps(step):
            gate, gains, parts = update(1, crop, step)
            r["level"][:, lanes_of(step)] = parts[4]
            back(1, crop, step, load_pairs(r["cotangent"].at[crop], step), gate, gains, parts, swiglu(parts[-1]))

        for_steps(steps)
        send_grad_z(1, crop)

    def after_turn(crop):
        weight_grads(1, r, r["grad_rows"])

        def steps(step):
            lanes = lanes_of(step)
            store_pairs(r["level"][:, lanes] + dot(r["shrink_t"][1], r["hidden"][:, lanes]), step, r["pair_out"].at[crop])

        for_steps(steps)
        store("pair_out", crop)

    def products_back(layer, crop):
        recv = r["recv_dz"].at[crop]
        exchange_wait(recv, recv_sem.at[layer * 8 + 4 + crop])
        second_sent("send_wide", crop, 8 if layer else 14)
        join_back(recv, r["left"].at[layer, crop], r["right"].at[layer, crop], r["whole"], r["result"], r["send_wide"].at[crop])
        begin("send_wide", crop, r["recv_ab"].at[crop], layer * 8 + 6, alone=True)

    def receive_sides_grad(layer, crop):
        recv = r["recv_ab"].at[crop]
        exchange_wait(recv, recv_sem.at[layer * 8 + 6 + crop])
        unpack_tiles(recv, 0, r["tiles_a"])
        unpack_tiles(recv, TILES, r["tiles_b"])

    def deep(crop):
        receive_sides_grad(1, crop)
        unpack_tiles(r["recv_z"].at[0, crop], 0, r["tiles_z"])

        def steps(step):
            upstream = project_back(1, crop, step)
            gate, gains, parts = update(0, crop, step)
            back(0, crop, step, upstream, gate, gains, parts, swiglu(parts[-1]))

        for_steps(steps)
        send_grad_z(0, crop)

    def last(crop):
        receive_sides_grad(0, crop)
        for_steps(lambda step: store_pairs(project_back(0, crop, step), step, r["pair_grad"].at[crop]))
        store("pair_grad", crop)

    for_crops(lambda crop: products(0, crop))
    for_crops(onward)
    for_crops(lambda crop: products(1, crop))

    def after_deep():
        weight_grads(0, r, r["grad_rows"])

    def after_both():
        after_deep()
        early.share()

    between_crops(turn, lambda: after_turn(0))
    between_crops(lambda crop: products_back(1, crop), lambda: after_turn(1))
    between_crops(deep, after_deep)
    between_crops(lambda crop: products_back(0, crop), after_both)
    between_crops(last, early.scatter)
    for layer in range(LAYERS):
        for index in range(6):
            row = NORM_ROW + index * LAYERS + layer
            r["grad_rows"][row : row + 1, :] = jnp.sum(r["g_norm"][layer, index].T, axis=0, keepdims=True)
    late.share()
    late.scatter()
    early.spread()
    late.spread()
    early.gather()
    late.gather()
    early.finish()
    late.finish()
    for crop in range(CROPS):
        sent("send_slim", crop, 4)
    sent("send_wide", 1, 6)
    for crop in range(CROPS):
        for name in STORES:
            near, far = r[name].at[crop], r[name + "_far"].at[crop]
            pltpu.make_async_copy(near, far, store_sem.at[STORES.index(name) * CROPS + crop]).wait()


class Sum:
    def __init__(self, name, group, place, r, sem):
        self.first, self.count, self.piece = group
        self.half = self.count * self.piece
        self.place, self.r, self.sem = place, r, sem
        self.share_ref, self.sibling, self.pieces, self.landed, self.summed = (
            r[name + suffix] for suffix in ("_share", "_sibling", "_pieces", "_landed", "_summed")
        )
        self.owner = place.chip < self.count
        self.offsets = [offset for offset in OFFSETS if offset[3] == 0]

    def rows(self, core):
        return pl.ds(pl.multiple_of(self.first + core * self.half, 16), self.half)

    def swap(self, source, target, index):
        return pltpu.make_async_remote_copy(
            source, target, self.sem.at[index], self.sem.at[index + 1], device_id=self.place.at((0, 0, 0, 1)), device_id_type=MESH
        )

    def push(self, source, target, index, offset):
        pltpu.make_async_remote_copy(
            source, target, self.sem.at[index], self.sem.at[index + 1], device_id=self.place.at(offset), device_id_type=MESH
        ).start()

    def wait(self, ref, count, index):
        some = ref.at[pl.ds(0, count)]
        pltpu.make_async_copy(some, some, self.sem.at[index]).wait()

    def share(self):
        self.share_ref[...] = self.r["grad_rows"][self.rows(1 - self.place.core), :].astype(BF)
        self.swap(self.share_ref, self.sibling, 0).start()

    def scatter(self):
        self.swap(self.share_ref, self.sibling, 0).wait()
        both = self.r["grad_rows"][self.rows(self.place.core), :] + self.sibling[...].astype(F32)
        self.pieces[...] = both.astype(BF).reshape(self.count, self.piece, 128)
        for offset in self.offsets:
            row, col = self.place.at(offset)
            piece = row // 2 * COLS + col

            @pl.when(piece < self.count)
            def _():
                self.push(self.pieces.at[piece], self.landed.at[self.place.chip], 2, offset)

    def spread(self):
        chip, chips = self.place.chip, DEVICES // 2

        @pl.when(self.owner)
        def _():
            self.landed[chip] = self.pieces[chip]
            self.wait(self.landed, chips - 1, 3)

            self.summed[chip] = jnp.sum(self.landed[...].astype(F32), axis=0).astype(BF)
            for offset in self.offsets:
                self.push(self.summed.at[chip], self.summed.at[chip], 4, offset)

    def gather(self):
        @pl.when(self.owner)
        def _():
            self.wait(self.pieces, self.count - 1, 2)
            self.wait(self.landed, DEVICES // 2 - 1, 4)
            self.wait(self.summed, self.count - 1, 5)

        @pl.when(jnp.logical_not(self.owner))
        def _():
            self.wait(self.pieces, self.count, 2)
            self.wait(self.summed, self.count, 5)

        own = self.r["total"].at[self.rows(self.place.core)]
        own[...] = self.summed[...].reshape(self.half, 128)
        self.swap(own, own, 6).start()

    def finish(self):
        own = self.r["total"].at[self.rows(self.place.core)]
        self.swap(own, own, 6).wait()


def window(outs, lengths, *args):
    return pl.pallas_call(
        window_kernel,
        out_shape=[jax.ShapeDtypeStruct(shape, dtype) for shape, dtype in outs],
        in_specs=[pl.BlockSpec(memory_space=pltpu.SMEM)] + [pl.BlockSpec(memory_space=pltpu.VMEM)] * (len(args) - FAR)
        + [pl.BlockSpec(memory_space=pl.ANY)] * FAR,
        out_specs=[pl.BlockSpec(memory_space=pl.ANY)] * 2 + [pl.BlockSpec(memory_space=pltpu.VMEM)],
        scratch_shapes=[pltpu.VMEM(shape, dtype) for shape, dtype in SCRATCH.values()]
        + [pltpu.SemaphoreType.DMA((8 * LAYERS,))] * 2
        + [pltpu.SemaphoreType.DMA((2, 8)), pltpu.SemaphoreType.DMA((FAR,)), pltpu.SemaphoreType.DMA((2 * CROPS,))],
        compiler_params=pltpu.CompilerParams(collective_id=1, has_side_effects=True, vmem_limit_bytes=VMEM_LIMIT),
        name="window",
    )(lengths, *args)


def adamw(gradient, weight, first, second, clip_factor, step_rate, decay_rate, outs):
    clipped = gradient * clip_factor
    moment = BETA_ONE * first + (1.0 - BETA_ONE) * clipped
    square = BETA_TWO * second + (1.0 - BETA_TWO) * clipped * clipped
    correct_one = 1.0 - BETA_ONE**STEP
    correct_two = 1.0 - BETA_TWO**STEP
    update = moment * (step_rate / correct_one) / (jnp.sqrt(square * (1.0 / correct_two)) + ADAM_EPS)
    renewed = weight * (1.0 - step_rate * decay_rate) - update
    for (ref, place), value in zip(outs, (moment, square, renewed, renewed)):
        ref[place] = value.astype(ref.dtype)


def settle_kernel(*refs):
    total_in, pair_ins, ins = refs[0], refs[1:3], refs[3:15]
    pair_outs, outs, norm_ref = refs[15:17], refs[17:32], refs[32]
    total, pairs, held, made = refs[33], refs[34:36], refs[36:48], refs[48:63]
    total_sem, pair_sem, in_sem, out_sem = refs[63:]

    pair_loads = [pltpu.make_async_copy(*refs_in, pair_sem.at[index]) for index, refs_in in enumerate(zip(pair_ins, pairs))]
    pair_stores = [pltpu.make_async_copy(*refs_out, pair_sem.at[2 + index]) for index, refs_out in enumerate(zip(pairs, pair_outs))]
    first = pltpu.make_async_copy(total_in, total, total_sem)
    first.start()
    for copy in pair_loads:
        copy.start()
    loads = {}
    for part in range(LAYERS):
        for index in range(9):
            loads[part, index] = pltpu.make_async_copy(ins[index].at[part], held[index].at[part], in_sem.at[part * 9 + index])
            loads[part, index].start()
    for index in range(9, 12):
        loads[0, index] = pltpu.make_async_copy(ins[index], held[index], in_sem.at[9 * LAYERS + index - 9])
        loads[0, index].start()
    first.wait()
    for load, copy in zip(pair_loads, pair_stores):
        load.wait()
        copy.start()

    def square(step, carry):
        rows = total[pl.ds(pl.multiple_of(step * 464, 16), 464), :].astype(F32)
        return carry + jnp.sum((rows * rows).reshape(58, 8, 128), axis=0)

    squares = lax.fori_loop(0, ROWS // 464, square, jnp.zeros((8, 128), F32))
    grad_norm = jnp.sqrt(jnp.sum(jnp.sum(squares, axis=1, keepdims=True), axis=0, keepdims=True))
    norm_ref[...] = grad_norm
    factor = jnp.minimum(1.0, CLIP / (grad_norm + 1e-06))
    stores = []

    def store(index, part):
        pieces = (made[index], outs[index]) if part is None else (made[index].at[part], outs[index].at[part])
        copy = pltpu.make_async_copy(*pieces, out_sem.at[len(stores)])
        copy.start()
        stores.append(copy)

    def run(kind, start, size, place):
        values = [ref[place] for ref in held[3 * kind : 3 * kind + 3]]
        gradient = total[start : start + size, :].astype(F32)
        adamw(gradient, *values, factor, RATE, DECAY_RATE, [(ref, place) for ref in made[4 * kind : 4 * kind + 4]])

    for part in range(LAYERS):
        for kind in range(3):
            for index in range(3):
                loads[part, 3 * kind + index].wait()
            for block in range((6, 8, 4)[kind]):
                if kind == 0:
                    run(kind, triangle_start(part, block), C, (part, block))
                elif kind == 1:
                    place = (part, block // 4, slice(None), slice(block % 4 * C, block % 4 * C + C))
                    run(kind, EXPAND_ROW + (part * 8 + block) * C, C, place)
                else:
                    run(kind, SHRINK_ROW + part * HID + block * C, C, (part, slice(block * C, block * C + C)))
            for index in range(4):
                store(4 * kind + index, part)
    for index in range(9, 12):
        loads[0, index].wait()
    rows = total[NORM_ROW : NORM_ROW + 16, :].astype(F32)
    for index in range(6):
        values = [ref[index] for ref in held[9:12]]
        outputs = [(ref, index) for ref in made[12:15]]
        adamw(rows[index * LAYERS : index * LAYERS + LAYERS], *values, factor, NORM_RATE, 0.0, outputs)
    for index in range(12, 15):
        store(index, None)
    for copy in stores + pair_stores:
        copy.wait()


def settle(total, pair_maps, kinds):
    arrays = [array for kind in kinds for array in kind]
    made = [(kind[0].shape, dtype) for kind in kinds[:3] for dtype in (F32, F32, F32, BF)] + [(kinds[3][0].shape, F32)] * 3
    anywhere = pl.BlockSpec(memory_space=pl.ANY)
    shapes = [jax.ShapeDtypeStruct(pair.shape, pair.dtype) for pair in pair_maps]
    shapes += [jax.ShapeDtypeStruct(*shape) for shape in made] + [jax.ShapeDtypeStruct((1, 1), F32)]
    return pl.pallas_call(
        settle_kernel,
        out_shape=shapes,
        in_specs=[anywhere] * (3 + len(arrays)),
        out_specs=[anywhere] * (len(shapes) - 1) + [pl.BlockSpec(memory_space=pltpu.VMEM)],
        scratch_shapes=[pltpu.VMEM(total.shape, total.dtype)]
        + [pltpu.VMEM(pair.shape, pair.dtype) for pair in pair_maps]
        + [pltpu.VMEM(array.shape, array.dtype) for array in arrays]
        + [pltpu.VMEM(*shape) for shape in made]
        + [pltpu.SemaphoreType.DMA, pltpu.SemaphoreType.DMA((4,))]
        + [pltpu.SemaphoreType.DMA((9 * LAYERS + 3,)), pltpu.SemaphoreType.DMA((12 * LAYERS + 3,))],
        compiler_params=pltpu.CompilerParams(vmem_limit_bytes=VMEM_LIMIT),
        name="settle",
    )(total, *pair_maps, *arrays)


def local(
    pair_in, lengths, pair_cotangent, triangle_weights, expand_weights, shrink_weights, norm_params, triangle_first,
    triangle_second, expand_first, expand_second, shrink_first, shrink_second, norm_first, norm_second,
):
    norms = [jnp.swapaxes(array, 0, 1) for array in (norm_params, norm_first, norm_second)]
    outs = [(pair_in.shape, BF), (pair_in.shape, F32), ((ROWS, 128), BF)]
    pair_out, pair_grad, total = window(
        outs, lengths, pair_in, triangle_weights, norms[0], pair_cotangent, expand_weights, shrink_weights
    )
    kinds = (
        (triangle_weights, triangle_first, triangle_second),
        (expand_weights, expand_first, expand_second),
        (shrink_weights, shrink_first, shrink_second),
        norms,
    )
    pair_out, pair_grad, *new = settle(total, (pair_out, pair_grad), kinds)
    moments = [new[4 * kind + place] for kind in range(3) for place in range(3)]
    norms_new = [jnp.swapaxes(array, 0, 1) for array in new[12:15]]
    copies = [new[4 * kind + 3] for kind in range(3)]
    return (pair_out, pair_grad, *moments, *norms_new, *copies, new[15].reshape(()))


def solution(mesh):
    pair = P(None, "row", "col", None)
    return jax.shard_map(
        local,
        mesh=mesh,
        in_specs=(pair, P(), pair) + (P(),) * 12,
        out_specs=(pair, pair) + (P(),) * 16,
        check_vma=False,
    )
```

```python
import jax
import jax.numpy as jnp
from jax import lax
from jax.experimental import pallas as pl
from jax.experimental.pallas import tpu as pltpu
from jax.sharding import PartitionSpec as P

LAYERS = 2
STEP = 10
CROPS = 2
COLS = 8
DEVICES = 128

EPS_NORM = 1e-05
BETA_ONE = 0.9
BETA_TWO = 0.999
ADAM_EPS = 1e-08
RATE = 0.1
NORM_RATE = 0.5
DECAY_RATE = 0.01
CLIP = 1.0

MESH = pl.DeviceIdType.MESH
BF = jnp.bfloat16
F32 = jnp.float32

C = 128
HID = 512
TILES = 16
PAIRS = 2048
WIDE = 1024
CHUNKS = PAIRS // WIDE
PER = WIDE // 128
VMEM_LIMIT = 61 << 20

EXPAND_ROW = 7 * C
SHRINK_ROW = EXPAND_ROW + LAYERS * 2 * HID
LATE_ROW = SHRINK_ROW + LAYERS * HID
NORM_ROW = LATE_ROW + 5 * C
EARLY = (0, 62, 32)
LATE = (LATE_ROW, 21, 16)
ROWS = LATE_ROW + 2 * 21 * 16


def triangle_start(layer, matrix):
    if layer == 1:
        return matrix * C
    return 6 * C if matrix == 5 else LATE_ROW + matrix * C


def triangle_rows(layer, matrix):
    return pl.ds(triangle_start(layer, matrix), C)


def expand_rows(layer, matrix, block):
    return pl.ds(EXPAND_ROW + ((layer * 2 + matrix) * 4 + block) * C, C)


def shrink_rows(layer):
    return pl.ds(SHRINK_ROW + layer * HID, HID)


def dot(left, right):
    return lax.dot_general(left, right, (((1,), (0,)), ((), ())), preferred_element_type=F32)


def dot_nt(left, right):
    return lax.dot_general(left, right, (((1,), (1,)), ((), ())), preferred_element_type=F32)


def dot_tn(left, right):
    return lax.dot_general(left, right, (((0,), (0,)), ((), ())), preferred_element_type=F32)


def sigmoid(v):
    return 0.5 * jnp.tanh(0.5 * v) + 0.5


KEPT = ("hidden", "grad_gate_up", "normed", "upstream", "updated", "grad_branch")


def mean_rows(v):
    return jnp.sum(v, axis=0, keepdims=True) * (1.0 / C)


def normalize(v):
    centered = v - mean_rows(v)
    scale = lax.rsqrt(mean_rows(centered * centered) + EPS_NORM)
    return centered * scale, scale


def normalize_back(grad, gain, hat, scale):
    grad_hat = grad * gain
    return scale * (grad_hat - mean_rows(grad_hat) - hat * mean_rows(grad_hat * hat))


def lanes_of(step):
    return pl.ds(pl.multiple_of(step * WIDE, WIDE), WIDE)


def scatter_tiles(scratch, step, value):
    for part in range(PER):
        scratch[pl.ds(step * PER + part, C, stride=TILES), :] = value[:, part * 128 : part * 128 + 128]


def gather_tiles(scratch, step):
    return jnp.concatenate(
        [scratch[pl.ds(step * PER + part, C, stride=TILES), :] for part in range(PER)], axis=1
    )


def pack_tiles(scratch, send, offset):
    send[:, offset : offset + TILES, :] = scratch[...].astype(BF).reshape(C, TILES, 128)


def unpack_tiles(recv, offset, scratch):
    scratch[...] = recv[:, offset : offset + TILES, :].reshape(PAIRS, 128).astype(F32)


def swap_halves(first, second):
    low = jnp.concatenate([first[:, :64], second[:, :64]], axis=1)
    high = jnp.concatenate([first[:, 64:], second[:, 64:]], axis=1)
    return low, high


def assemble(recv, offset, whole):
    for row in range(16):
        base = row * 32
        for pair in range(4):
            low, high = swap_halves(
                recv[row * 8 + 2 * pair, offset : offset + TILES, :],
                recv[row * 8 + 2 * pair + 1, offset : offset + TILES, :],
            )
            whole[base : base + 16, pair * 128 : pair * 128 + 128] = low
            whole[base + 16 : base + 32, pair * 128 : pair * 128 + 128] = high


def disassemble(whole, send, offset):
    for row in range(16):
        base = row * 32
        for pair in range(4):
            first, second = swap_halves(
                whole[base : base + 16, pair * 128 : pair * 128 + 128],
                whole[base + 16 : base + 32, pair * 128 : pair * 128 + 128],
            )
            send[row * 8 + 2 * pair, offset : offset + TILES, :] = first
            send[row * 8 + 2 * pair + 1, offset : offset + TILES, :] = second


def load_pairs(pair_ref, step):
    parts = []
    for part in range(PER):
        tile = step * PER + part
        parts.append(jnp.concatenate([pair_ref[tile], pair_ref[tile + TILES]], axis=0).astype(F32).T)
    return jnp.concatenate(parts, axis=1)


def store_pairs(value, step, out_ref):
    for part in range(PER):
        rows = value[:, part * 128 : part * 128 + 128].T
        out_ref[step * PER + part] = rows[:64].astype(out_ref.dtype)
        out_ref[step * PER + part + TILES] = rows[64:].astype(out_ref.dtype)


def project_step(x, mask, five, norms, scratch_a, scratch_b, gate_ref, step):
    hat, _ = normalize(x)
    normed = (hat * norms[0] + norms[1]).astype(BF)
    projected = dot(five[...], normed)
    left = mask * sigmoid(projected[:C]) * projected[C : 2 * C]
    right = mask * sigmoid(projected[2 * C : 3 * C]) * projected[3 * C : 4 * C]
    scatter_tiles(scratch_a, step, left)
    scatter_tiles(scratch_b, step, right)
    gate_ref[:, lanes_of(step)] = sigmoid(projected[4 * C :]).astype(BF)


def update_step(x, gate, z, out_t, expand_t, norms):
    z_hat, z_scale = normalize(z)
    updated = (z_hat * norms[2] + norms[3]).astype(BF)
    branch = dot(out_t[...], updated)
    middle = x + gate * branch
    mid_hat, mid_scale = normalize(middle)
    normed = (mid_hat * norms[4] + norms[5]).astype(BF)
    gate_up = dot(expand_t[...], normed)
    return (z_hat, z_scale, updated, branch, middle, mid_hat, mid_scale, normed, gate_up)


def swiglu(gate_up):
    gate_half = gate_up[:HID]
    sig = sigmoid(gate_half)
    silu = gate_half * sig
    return (sig, silu, (silu * gate_up[HID:]).astype(BF))


def back_step(upstream, parts, hidden_parts, gate, weights, norms, kept, lanes, g_norm):
    z_hat, z_scale, updated, branch, middle, mid_hat, mid_scale, normed, gate_up = parts
    sig, silu, hidden = hidden_parts
    shrink, expand, out_n = weights
    upstream_low = upstream.astype(BF)
    grad_hidden = dot(shrink[...], upstream_low)
    grad_gate = (grad_hidden * gate_up[HID:] * (sig + silu * (1.0 - sig))).astype(BF)
    grad_up = (grad_hidden * silu).astype(BF)
    grad_gate_up = jnp.concatenate([grad_gate, grad_up], axis=0)
    grad_normed = dot(expand[...], grad_gate_up)
    add_norm(g_norm, 4, grad_normed * mid_hat, grad_normed)
    grad_middle = upstream + normalize_back(grad_normed, norms[4], mid_hat, mid_scale)
    scaled = grad_middle * gate
    grad_branch = scaled.astype(BF)
    grad_out_gate = (scaled * branch * (1.0 - gate)).astype(BF)
    grad_updated = dot(out_n[...], grad_branch)
    add_norm(g_norm, 2, grad_updated * z_hat, grad_updated)
    grad_z = normalize_back(grad_updated, norms[2], z_hat, z_scale)
    for name, value in zip(KEPT, (hidden, grad_gate_up, normed, upstream_low, updated, grad_branch)):
        kept[name][:, lanes] = value
    return (grad_middle, grad_out_gate, grad_z)


def weight_grads(layer, kept, grad_rows):
    def steps(step):
        hidden, grad_gate_up, normed, upstream, updated, grad_branch = (kept[name][:, lanes_of(step)] for name in KEPT)
        grad_rows[shrink_rows(layer), :] += dot_nt(hidden, upstream)
        term = dot_nt(normed, grad_gate_up)
        for block in range(8):
            grad_rows[expand_rows(layer, block // 4, block % 4), :] += term[:, block * C : block * C + C]
        grad_rows[triangle_rows(layer, 5), :] += dot_nt(updated, grad_branch)

    for_steps(steps)


def add_norm(g_norm, index, gain_term, bias_term):
    for place, term in ((index, gain_term), (index + 1, bias_term)):
        total = term[:, :128]
        for part in range(1, PER):
            total = total + term[:, part * 128 : part * 128 + 128]
        g_norm[place] += total


def project_back_step(
    x, mask, grad_left, grad_right, grad_out_gate, grad_middle, five, five_n, norms, grads
):
    layer, grad_rows, g_norm = grads
    hat, scale = normalize(x)
    normed = (hat * norms[0] + norms[1]).astype(BF)
    projected = dot(five[: 4 * C, :], normed)
    pieces = []
    for grad, base in ((grad_left, 0), (grad_right, 2 * C)):
        sig = sigmoid(projected[base : base + C])
        masked = grad * mask * sig
        pieces.append((masked * projected[base + C : base + 2 * C] * (1.0 - sig)).astype(BF))
        pieces.append(masked.astype(BF))
    pieces.append(grad_out_gate)
    grad_projected = jnp.concatenate(pieces, axis=0)
    term = dot_nt(normed, grad_projected)
    for matrix in range(5):
        grad_rows[triangle_rows(layer, matrix), :] += term[:, matrix * C : matrix * C + C]
    grad_normed = dot(five_n[...], grad_projected)
    add_norm(g_norm, 0, grad_normed * hat, grad_normed)
    return grad_middle + normalize_back(grad_normed, norms[0], hat, scale)


class Norms:
    def __init__(self, ref, layer):
        self.ref, self.layer = ref, layer

    def __getitem__(self, index):
        value = self.ref[self.layer, index]
        return jnp.concatenate([value] * PER, axis=1)


def zero(*refs):
    for ref in refs:
        ref[...] = jnp.zeros_like(ref)


def distance(offset):
    return sum(min(step, 4 - step) for step in offset[:3])


OFFSETS = [(i % 4, i // 4 % 4, i // 16 % 4, i // 64) for i in range(1, 128)]
OFFSETS = [o for _, _, o in sorted((-distance(o), (i * 53 + 17) % 127, o) for i, o in enumerate(OFFSETS))]


class Place:
    def __init__(self):
        self.row, self.col = lax.axis_index("row"), lax.axis_index("col")
        self.me = self.row * COLS + self.col
        self.core = lax.rem(self.row, 2)
        x, y, z = lax.rem(self.row // 2, 4), self.row // 8 * 2 + lax.rem(self.col, 2), self.col // 2
        self.chip = self.row // 2 * COLS + self.col
        xs = [lax.rem(x + step, 4) * 2 for step in range(4)]
        ys = [lax.rem(y + step, 4) for step in range(4)]
        zs = [lax.rem(z + step, 4) * 2 for step in range(4)]
        cores = [self.core, 1 - self.core]
        highs, lows = [v // 2 * 8 for v in ys], [lax.rem(v, 2) for v in ys]
        self.rows = {(a, b, d): highs[b] + xs[a] + cores[d] for a in range(4) for b in range(4) for d in range(2)}
        self.cols = {(b, c): zs[c] + lows[b] for b in range(4) for c in range(4)}

    def at(self, offset):
        a, b, c, d = offset
        return self.rows[a, b, d], self.cols[b, c]


def exchange_start(place, send, recv, send_sem, recv_sem):
    for offset in OFFSETS:
        row, col = place.at(offset)
        pltpu.make_async_remote_copy(
            send.at[row * COLS + col], recv.at[place.me], send_sem, recv_sem, device_id=(row, col), device_id_type=MESH
        ).start()
    recv[place.me] = send[place.me]


def exchange_wait(ref, sem):
    others = pl.ds(0, DEVICES - 1)
    pltpu.make_async_copy(ref.at[others], ref.at[others], sem).wait()


def join(recv, left, right, whole, send):
    assemble(recv, 0, left)
    assemble(recv, TILES, right)
    whole[...] = dot_nt(left[...], right[...]).astype(BF)
    disassemble(whole, send, 0)


def join_back(recv, left, right, whole, result, send):
    assemble(recv, 0, whole)
    result[...] = dot(whole[...], right[...]).astype(BF)
    disassemble(result, send, 0)
    result[...] = dot_tn(whole[...], left[...]).astype(BF)
    disassemble(result, send, TILES)


INPUTS = ("lengths", "pair", "triangle", "norms_in", "cotangent_far", "expand_far", "shrink_far")
FAR = 3
STORES = ("pair_out", "pair_grad")
OUTPUTS = ("pair_out_far", "pair_grad_far", "total")
SCRATCH = {
    "pair_out": ((CROPS, 32, 64, C), BF),
    "pair_grad": ((CROPS, 32, 64, C), F32),
    "cotangent": ((CROPS, 32, 64, C), BF),
    "expand_in": ((LAYERS, 2, C, HID), F32),
    "shrink_in": ((LAYERS, HID, C), F32),
    "mask": ((CROPS, 1, PAIRS), F32),
    "norms": ((LAYERS, 6, C, 128), F32),
    "five": ((LAYERS, 5 * C, C), BF),
    "five_n": ((LAYERS, C, 5 * C), BF),
    "out_t": ((LAYERS, C, C), BF),
    "out_n": ((LAYERS, C, C), BF),
    "expand_t": ((LAYERS, 2 * HID, C), BF),
    "expand": ((LAYERS, C, 2 * HID), BF),
    "shrink_t": ((LAYERS, C, HID), BF),
    "shrink": ((LAYERS, HID, C), BF),
    "x": ((LAYERS, CROPS, C, PAIRS), F32),
    "gate": ((LAYERS, CROPS, C, PAIRS), BF),
    "recv_ab": ((CROPS, C, 2 * TILES, 128), BF),
    "recv_z": ((LAYERS, CROPS, C, TILES, 128), BF),
    "recv_dz": ((CROPS, C, TILES, 128), BF),
    "send_wide": ((CROPS, C, 2 * TILES, 128), BF),
    "send_slim": ((CROPS, C, TILES, 128), BF),
    "left": ((LAYERS, CROPS, 512, 512), BF),
    "right": ((LAYERS, CROPS, 512, 512), BF),
    "mid": ((CROPS, C, PAIRS), F32),
    "out_gate": ((CROPS, C, PAIRS), BF),
    "tiles_a": ((PAIRS, 128), F32),
    "tiles_b": ((PAIRS, 128), F32),
    "tiles_z": ((PAIRS, 128), F32),
    "whole": ((512, 512), BF),
    "result": ((512, 512), BF),
    "hidden": ((HID, PAIRS), BF),
    "grad_gate_up": ((2 * HID, PAIRS), BF),
    "normed": ((C, PAIRS), BF),
    "upstream": ((C, PAIRS), BF),
    "updated": ((C, PAIRS), BF),
    "grad_branch": ((C, PAIRS), BF),
    "level": ((C, PAIRS), F32),
    "grad_rows": ((ROWS, 128), F32),
    "g_norm": ((LAYERS, 6, C, 128), F32),
}
for group, (_, pieces, piece) in (("early", EARLY), ("late", LATE)):
    SCRATCH.update({
        group + "_share": ((pieces * piece, 128), BF),
        group + "_sibling": ((pieces * piece, 128), BF),
        group + "_pieces": ((pieces, piece, 128), BF),
        group + "_landed": ((DEVICES // 2, piece, 128), BF),
        group + "_summed": ((pieces, piece, 128), BF),
    })


def prepare_triangle(r, layer):
    for index in range(6):
        row = r["norms_in"][index, layer : layer + 1, :]
        r["norms"][layer, index] = jnp.broadcast_to(row, (C, C)).T
    for matrix in range(5):
        weight = r["triangle"][layer, matrix]
        r["five"][layer, matrix * C : matrix * C + C, :] = weight.T.astype(BF)
        r["five_n"][layer, :, matrix * C : matrix * C + C] = weight.astype(BF)
    r["out_t"][layer] = r["triangle"][layer, 5].T.astype(BF)
    r["out_n"][layer] = r["triangle"][layer, 5].astype(BF)


def prepare_transition(r, layer):
    for matrix in range(2):
        for block in range(4):
            lanes = slice(block * C, block * C + C)
            rows = slice(matrix * HID + block * C, matrix * HID + block * C + C)
            weight = r["expand_in"][layer, matrix, :, lanes]
            r["expand_t"][layer, rows, :] = weight.T.astype(BF)
            r["expand"][layer, :, rows] = weight.astype(BF)
    for block in range(4):
        rows = slice(block * C, block * C + C)
        weight = r["shrink_in"][layer, rows, :]
        r["shrink_t"][layer, :, rows] = weight.T.astype(BF)
        r["shrink"][layer, rows, :] = weight.astype(BF)


def prepare_mask(r, place):
    pair = lax.broadcasted_iota(jnp.int32, (1, PAIRS), 1)
    tile, lane = pair // 128, lax.rem(pair, 128)
    first = place.row * 32 + lane // 64 * TILES + tile
    second = place.col * 64 + lax.rem(lane, 64)
    last = jnp.maximum(first, second)
    for crop in range(CROPS):
        r["mask"][crop] = jnp.clip(r["lengths"][crop] - last, 0, 1).astype(F32)


def for_crops(visit):
    def run(crop, carry):
        visit(crop)
        return carry

    lax.fori_loop(0, CROPS, run, 0)


def between_crops(visit, rest):
    def run(crop):
        visit(crop)
        pl.when(crop == 0)(rest)

    for_crops(run)


def for_steps(visit):
    def run(step, carry):
        visit(step)
        return carry

    lax.fori_loop(0, CHUNKS, run, 0)


def window_kernel(*refs):
    names = INPUTS + OUTPUTS + tuple(SCRATCH)
    r = dict(zip(names, refs))
    send_sem, recv_sem, sum_sem, load_sem, store_sem = refs[len(names) :]
    place = Place()
    loads = [
        pltpu.make_async_copy(r[far], r[near], load_sem.at[index])
        for index, (far, near) in enumerate(
            (("expand_far", "expand_in"), ("shrink_far", "shrink_in"), ("cotangent_far", "cotangent"))
        )
    ]
    for load in loads:
        load.start()

    barrier = pltpu.get_barrier_semaphore()
    for offset in OFFSETS:
        pl.semaphore_signal(barrier, inc=1, device_id=place.at(offset), device_id_type=MESH)

    early, late = Sum("early", EARLY, place, r, sum_sem.at[0]), Sum("late", LATE, place, r, sum_sem.at[1])

    def sent(kind, crop, index):
        exchange_wait(r[kind].at[crop], send_sem.at[index + crop])

    def second_sent(kind, crop, index):
        if not isinstance(crop, int):
            pl.when(crop == 1)(lambda: sent(kind, 1, index))
        elif crop:
            sent(kind, 1, index)

    def begin(kind, crop, recv, index, alone=False):
        if alone and not isinstance(crop, int):
            pl.when(crop == 1)(lambda: sent(kind, 0, index))
        elif alone and crop:
            sent(kind, 0, index)
        exchange_start(place, r[kind].at[crop], recv, send_sem.at[index + crop], recv_sem.at[index + crop])

    def project(layer, crop, step, x):
        project_step(
            x, r["mask"][crop, :, lanes_of(step)], r["five"].at[layer], Norms(r["norms"], layer), r["tiles_a"], r["tiles_b"],
            r["gate"].at[layer, crop], step,
        )

    def send_sides(layer, crop):
        if layer:
            second_sent("send_wide", crop, 0)
        pack_tiles(r["tiles_a"], r["send_wide"].at[crop], 0)
        pack_tiles(r["tiles_b"], r["send_wide"].at[crop], TILES)
        begin("send_wide", crop, r["recv_ab"].at[crop], layer * 8, alone=True)

    def update(layer, crop, step):
        lanes = lanes_of(step)
        gate = r["gate"][layer, crop, :, lanes].astype(F32)
        gains = Norms(r["norms"], layer)
        parts = update_step(
            r["x"][layer, crop, :, lanes], gate, gather_tiles(r["tiles_z"], step), r["out_t"].at[layer], r["expand_t"].at[layer], gains
        )
        return gate, gains, parts

    def back(layer, crop, step, upstream, gate, gains, parts, hidden_parts):
        lanes = lanes_of(step)
        weights = (r["shrink"].at[layer], r["expand"].at[layer], r["out_n"].at[layer])
        middle, out_gate, grad_z = back_step(
            upstream, parts, hidden_parts, gate, weights, gains, r, lanes, r["g_norm"].at[layer]
        )
        r["mid"][crop, :, lanes] = middle
        r["out_gate"][crop, :, lanes] = out_gate
        scatter_tiles(r["tiles_z"], step, grad_z)

    def project_back(layer, crop, step):
        lanes = lanes_of(step)
        return project_back_step(
            r["x"][layer, crop, :, lanes], r["mask"][crop, :, lanes], gather_tiles(r["tiles_a"], step), gather_tiles(r["tiles_b"], step),
            r["out_gate"][crop, :, lanes], r["mid"][crop, :, lanes], r["five"].at[layer], r["five_n"].at[layer],
            Norms(r["norms"], layer), (layer, r["grad_rows"], r["g_norm"].at[layer]),
        )

    def send_grad_z(layer, crop):
        if layer:
            second_sent("send_slim", crop, 10)
        else:
            sent("send_slim", crop, 12)
        pack_tiles(r["tiles_z"], r["send_slim"].at[crop], 0)
        begin("send_slim", crop, r["recv_dz"].at[crop], layer * 8 + 4)

    prepare_mask(r, place)
    prepare_triangle(r, 0)

    def first(crop):
        def steps(step):
            x = load_pairs(r["pair"].at[crop], step)
            r["x"][0, crop, :, lanes_of(step)] = x
            project(0, crop, step, x)

        for_steps(steps)

        @pl.when(crop == 0)
        def _():
            pl.semaphore_wait(barrier, DEVICES - 1)

        send_sides(0, crop)

    for_crops(first)
    for load in loads:
        load.wait()
    prepare_transition(r, 0)
    for layer in range(1, LAYERS):
        prepare_triangle(r, layer)
        prepare_transition(r, layer)
    zero(r["grad_rows"], r["g_norm"])

    def store(name, crop):
        near, far = r[name].at[crop], r[name + "_far"].at[crop]
        pltpu.make_async_copy(near, far, store_sem.at[STORES.index(name) * CROPS + crop]).start()

    def products(layer, crop):
        recv = r["recv_ab"].at[crop]
        exchange_wait(recv, recv_sem.at[layer * 8 + crop])
        if layer:
            second_sent("send_slim", crop, 2)
        join(recv, r["left"].at[layer, crop], r["right"].at[layer, crop], r["whole"], r["send_slim"].at[crop])
        begin("send_slim", crop, r["recv_z"].at[layer, crop], layer * 8 + 2, alone=True)

    def onward(crop):
        recv = r["recv_z"].at[0, crop]
        exchange_wait(recv, recv_sem.at[2 + crop])
        unpack_tiles(recv, 0, r["tiles_z"])

        def forward(step):
            gate, gains, parts = update(0, crop, step)
            x_new = parts[4] + dot(r["shrink_t"][0], swiglu(parts[-1])[2])
            r["x"][1, crop, :, lanes_of(step)] = x_new
            project(1, crop, step, x_new)

        for_steps(forward)
        send_sides(1, crop)

    def turn(crop):
        recv = r["recv_z"].at[1, crop]
        exchange_wait(recv, recv_sem.at[10 + crop])
        unpack_tiles(recv, 0, r["tiles_z"])

        def steps(step):
            gate, gains, parts = update(1, crop, step)
            r["level"][:, lanes_of(step)] = parts[4]
            back(1, crop, step, load_pairs(r["cotangent"].at[crop], step), gate, gains, parts, swiglu(parts[-1]))

        for_steps(steps)
        send_grad_z(1, crop)

    def after_turn(crop):
        weight_grads(1, r, r["grad_rows"])

        def steps(step):
            lanes = lanes_of(step)
            store_pairs(r["level"][:, lanes] + dot(r["shrink_t"][1], r["hidden"][:, lanes]), step, r["pair_out"].at[crop])

        for_steps(steps)
        store("pair_out", crop)

    def products_back(layer, crop):
        recv = r["recv_dz"].at[crop]
        exchange_wait(recv, recv_sem.at[layer * 8 + 4 + crop])
        second_sent("send_wide", crop, 8 if layer else 14)
        join_back(recv, r["left"].at[layer, crop], r["right"].at[layer, crop], r["whole"], r["result"], r["send_wide"].at[crop])
        begin("send_wide", crop, r["recv_ab"].at[crop], layer * 8 + 6, alone=True)

    def receive_sides_grad(layer, crop):
        recv = r["recv_ab"].at[crop]
        exchange_wait(recv, recv_sem.at[layer * 8 + 6 + crop])
        unpack_tiles(recv, 0, r["tiles_a"])
        unpack_tiles(recv, TILES, r["tiles_b"])

    def deep(crop):
        receive_sides_grad(1, crop)
        unpack_tiles(r["recv_z"].at[0, crop], 0, r["tiles_z"])

        def steps(step):
            upstream = project_back(1, crop, step)
            gate, gains, parts = update(0, crop, step)
            back(0, crop, step, upstream, gate, gains, parts, swiglu(parts[-1]))

        for_steps(steps)
        send_grad_z(0, crop)

    def last(crop):
        receive_sides_grad(0, crop)
        pl.when(crop == 1)(early.scatter)
        for_steps(lambda step: store_pairs(project_back(0, crop, step), step, r["pair_grad"].at[crop]))
        store("pair_grad", crop)

    for_crops(lambda crop: products(0, crop))
    for_crops(onward)
    for_crops(lambda crop: products(1, crop))

    def after_deep():
        weight_grads(0, r, r["grad_rows"])

    def after_both():
        after_deep()
        early.share()

    between_crops(turn, lambda: after_turn(0))
    between_crops(lambda crop: products_back(1, crop), lambda: after_turn(1))
    between_crops(deep, after_deep)
    between_crops(lambda crop: products_back(0, crop), after_both)
    for_crops(last)
    for layer in range(LAYERS):
        for index in range(6):
            row = NORM_ROW + index * LAYERS + layer
            r["grad_rows"][row : row + 1, :] = jnp.sum(r["g_norm"][layer, index].T, axis=0, keepdims=True)
    late.share()
    late.scatter()
    early.spread()
    late.spread()
    early.gather()
    late.gather()
    early.finish()
    late.finish()
    for crop in range(CROPS):
        sent("send_slim", crop, 4)
    sent("send_wide", 1, 6)
    for crop in range(CROPS):
        for name in STORES:
            near, far = r[name].at[crop], r[name + "_far"].at[crop]
            pltpu.make_async_copy(near, far, store_sem.at[STORES.index(name) * CROPS + crop]).wait()


class Sum:
    def __init__(self, name, group, place, r, sem):
        self.first, self.count, self.piece = group
        self.half = self.count * self.piece
        self.place, self.r, self.sem = place, r, sem
        self.share_ref, self.sibling, self.pieces, self.landed, self.summed = (
            r[name + suffix] for suffix in ("_share", "_sibling", "_pieces", "_landed", "_summed")
        )
        self.owner = place.chip < self.count
        self.offsets = [offset for offset in OFFSETS if offset[3] == 0]

    def rows(self, core):
        return pl.ds(pl.multiple_of(self.first + core * self.half, 16), self.half)

    def swap(self, source, target, index):
        return pltpu.make_async_remote_copy(
            source, target, self.sem.at[index], self.sem.at[index + 1], device_id=self.place.at((0, 0, 0, 1)), device_id_type=MESH
        )

    def push(self, source, target, index, offset):
        pltpu.make_async_remote_copy(
            source, target, self.sem.at[index], self.sem.at[index + 1], device_id=self.place.at(offset), device_id_type=MESH
        ).start()

    def wait(self, ref, count, index):
        some = ref.at[pl.ds(0, count)]
        pltpu.make_async_copy(some, some, self.sem.at[index]).wait()

    def share(self):
        self.share_ref[...] = self.r["grad_rows"][self.rows(1 - self.place.core), :].astype(BF)
        self.swap(self.share_ref, self.sibling, 0).start()

    def scatter(self):
        self.swap(self.share_ref, self.sibling, 0).wait()
        both = self.r["grad_rows"][self.rows(self.place.core), :] + self.sibling[...].astype(F32)
        self.pieces[...] = both.astype(BF).reshape(self.count, self.piece, 128)
        for offset in self.offsets:
            row, col = self.place.at(offset)
            piece = row // 2 * COLS + col

            @pl.when(piece < self.count)
            def _():
                self.push(self.pieces.at[piece], self.landed.at[self.place.chip], 2, offset)

    def spread(self):
        chip, chips = self.place.chip, DEVICES // 2

        @pl.when(self.owner)
        def _():
            self.landed[chip] = self.pieces[chip]
            self.wait(self.landed, chips - 1, 3)

            self.summed[chip] = jnp.sum(self.landed[...].astype(F32), axis=0).astype(BF)
            for offset in self.offsets:
                self.push(self.summed.at[chip], self.summed.at[chip], 4, offset)

    def gather(self):
        @pl.when(self.owner)
        def _():
            self.wait(self.pieces, self.count - 1, 2)
            self.wait(self.landed, DEVICES // 2 - 1, 4)
            self.wait(self.summed, self.count - 1, 5)

        @pl.when(jnp.logical_not(self.owner))
        def _():
            self.wait(self.pieces, self.count, 2)
            self.wait(self.summed, self.count, 5)

        own = self.r["total"].at[self.rows(self.place.core)]
        own[...] = self.summed[...].reshape(self.half, 128)
        self.swap(own, own, 6).start()

    def finish(self):
        own = self.r["total"].at[self.rows(self.place.core)]
        self.swap(own, own, 6).wait()


def window(outs, lengths, *args):
    return pl.pallas_call(
        window_kernel,
        out_shape=[jax.ShapeDtypeStruct(shape, dtype) for shape, dtype in outs],
        in_specs=[pl.BlockSpec(memory_space=pltpu.SMEM)] + [pl.BlockSpec(memory_space=pltpu.VMEM)] * (len(args) - FAR)
        + [pl.BlockSpec(memory_space=pl.ANY)] * FAR,
        out_specs=[pl.BlockSpec(memory_space=pl.ANY)] * 2 + [pl.BlockSpec(memory_space=pltpu.VMEM)],
        scratch_shapes=[pltpu.VMEM(shape, dtype) for shape, dtype in SCRATCH.values()]
        + [pltpu.SemaphoreType.DMA((8 * LAYERS,))] * 2
        + [pltpu.SemaphoreType.DMA((2, 8)), pltpu.SemaphoreType.DMA((FAR,)), pltpu.SemaphoreType.DMA((2 * CROPS,))],
        compiler_params=pltpu.CompilerParams(collective_id=1, has_side_effects=True, vmem_limit_bytes=VMEM_LIMIT),
        name="window",
    )(lengths, *args)


def adamw(gradient, weight, first, second, clip_factor, step_rate, decay_rate, outs):
    clipped = gradient * clip_factor
    moment = BETA_ONE * first + (1.0 - BETA_ONE) * clipped
    square = BETA_TWO * second + (1.0 - BETA_TWO) * clipped * clipped
    correct_one = 1.0 - BETA_ONE**STEP
    correct_two = 1.0 - BETA_TWO**STEP
    update = moment * (step_rate / correct_one) / (jnp.sqrt(square * (1.0 / correct_two)) + ADAM_EPS)
    renewed = weight * (1.0 - step_rate * decay_rate) - update
    for (ref, place), value in zip(outs, (moment, square, renewed, renewed)):
        ref[place] = value.astype(ref.dtype)


def settle_kernel(*refs):
    total_in, pair_ins, ins = refs[0], refs[1:3], refs[3:15]
    pair_outs, outs, norm_ref = refs[15:17], refs[17:32], refs[32]
    total, pairs, held, made = refs[33], refs[34:36], refs[36:48], refs[48:63]
    total_sem, pair_sem, in_sem, out_sem = refs[63:]

    pair_loads = [pltpu.make_async_copy(*refs_in, pair_sem.at[index]) for index, refs_in in enumerate(zip(pair_ins, pairs))]
    pair_stores = [pltpu.make_async_copy(*refs_out, pair_sem.at[2 + index]) for index, refs_out in enumerate(zip(pairs, pair_outs))]
    first = pltpu.make_async_copy(total_in, total, total_sem)
    first.start()
    for copy in pair_loads:
        copy.start()
    loads = {}
    for part in range(LAYERS):
        for index in range(9):
            loads[part, index] = pltpu.make_async_copy(ins[index].at[part], held[index].at[part], in_sem.at[part * 9 + index])
            loads[part, index].start()
    for index in range(9, 12):
        loads[0, index] = pltpu.make_async_copy(ins[index], held[index], in_sem.at[9 * LAYERS + index - 9])
        loads[0, index].start()
    first.wait()
    for load, copy in zip(pair_loads, pair_stores):
        load.wait()
        copy.start()

    def square(step, carry):
        rows = total[pl.ds(pl.multiple_of(step * 464, 16), 464), :].astype(F32)
        return carry + jnp.sum((rows * rows).reshape(58, 8, 128), axis=0)

    squares = lax.fori_loop(0, ROWS // 464, square, jnp.zeros((8, 128), F32))
    grad_norm = jnp.sqrt(jnp.sum(jnp.sum(squares, axis=1, keepdims=True), axis=0, keepdims=True))
    norm_ref[...] = grad_norm
    factor = jnp.minimum(1.0, CLIP / (grad_norm + 1e-06))
    stores = []

    def store(index, part):
        pieces = (made[index], outs[index]) if part is None else (made[index].at[part], outs[index].at[part])
        copy = pltpu.make_async_copy(*pieces, out_sem.at[len(stores)])
        copy.start()
        stores.append(copy)

    def run(kind, start, size, place):
        values = [ref[place] for ref in held[3 * kind : 3 * kind + 3]]
        gradient = total[start : start + size, :].astype(F32)
        adamw(gradient, *values, factor, RATE, DECAY_RATE, [(ref, place) for ref in made[4 * kind : 4 * kind + 4]])

    for part in range(LAYERS):
        for kind in range(3):
            for index in range(3):
                loads[part, 3 * kind + index].wait()
            for block in range((6, 8, 4)[kind]):
                if kind == 0:
                    run(kind, triangle_start(part, block), C, (part, block))
                elif kind == 1:
                    place = (part, block // 4, slice(None), slice(block % 4 * C, block % 4 * C + C))
                    run(kind, EXPAND_ROW + (part * 8 + block) * C, C, place)
                else:
                    run(kind, SHRINK_ROW + part * HID + block * C, C, (part, slice(block * C, block * C + C)))
            for index in range(4):
                store(4 * kind + index, part)
    for index in range(9, 12):
        loads[0, index].wait()
    rows = total[NORM_ROW : NORM_ROW + 16, :].astype(F32)
    for index in range(6):
        values = [ref[index] for ref in held[9:12]]
        outputs = [(ref, index) for ref in made[12:15]]
        adamw(rows[index * LAYERS : index * LAYERS + LAYERS], *values, factor, NORM_RATE, 0.0, outputs)
    for index in range(12, 15):
        store(index, None)
    for copy in stores + pair_stores:
        copy.wait()


def settle(total, pair_maps, kinds):
    arrays = [array for kind in kinds for array in kind]
    made = [(kind[0].shape, dtype) for kind in kinds[:3] for dtype in (F32, F32, F32, BF)] + [(kinds[3][0].shape, F32)] * 3
    anywhere = pl.BlockSpec(memory_space=pl.ANY)
    shapes = [jax.ShapeDtypeStruct(pair.shape, pair.dtype) for pair in pair_maps]
    shapes += [jax.ShapeDtypeStruct(*shape) for shape in made] + [jax.ShapeDtypeStruct((1, 1), F32)]
    return pl.pallas_call(
        settle_kernel,
        out_shape=shapes,
        in_specs=[anywhere] * (3 + len(arrays)),
        out_specs=[anywhere] * (len(shapes) - 1) + [pl.BlockSpec(memory_space=pltpu.VMEM)],
        scratch_shapes=[pltpu.VMEM(total.shape, total.dtype)]
        + [pltpu.VMEM(pair.shape, pair.dtype) for pair in pair_maps]
        + [pltpu.VMEM(array.shape, array.dtype) for array in arrays]
        + [pltpu.VMEM(*shape) for shape in made]
        + [pltpu.SemaphoreType.DMA, pltpu.SemaphoreType.DMA((4,))]
        + [pltpu.SemaphoreType.DMA((9 * LAYERS + 3,)), pltpu.SemaphoreType.DMA((12 * LAYERS + 3,))],
        compiler_params=pltpu.CompilerParams(vmem_limit_bytes=VMEM_LIMIT),
        name="settle",
    )(total, *pair_maps, *arrays)


def local(
    pair_in, lengths, pair_cotangent, triangle_weights, expand_weights, shrink_weights, norm_params, triangle_first,
    triangle_second, expand_first, expand_second, shrink_first, shrink_second, norm_first, norm_second,
):
    norms = [jnp.swapaxes(array, 0, 1) for array in (norm_params, norm_first, norm_second)]
    outs = [(pair_in.shape, BF), (pair_in.shape, F32), ((ROWS, 128), BF)]
    pair_out, pair_grad, total = window(
        outs, lengths, pair_in, triangle_weights, norms[0], pair_cotangent, expand_weights, shrink_weights
    )
    kinds = (
        (triangle_weights, triangle_first, triangle_second),
        (expand_weights, expand_first, expand_second),
        (shrink_weights, shrink_first, shrink_second),
        norms,
    )
    pair_out, pair_grad, *new = settle(total, (pair_out, pair_grad), kinds)
    moments = [new[4 * kind + place] for kind in range(3) for place in range(3)]
    norms_new = [jnp.swapaxes(array, 0, 1) for array in new[12:15]]
    copies = [new[4 * kind + 3] for kind in range(3)]
    return (pair_out, pair_grad, *moments, *norms_new, *copies, new[15].reshape(()))


def solution(mesh):
    pair = P(None, "row", "col", None)
    return jax.shard_map(
        local,
        mesh=mesh,
        in_specs=(pair, P(), pair) + (P(),) * 12,
        out_specs=(pair, pair) + (P(),) * 16,
        check_vma=False,
    )
```
